128 devices in a mesh: lat: 8 (over z, x_lo), lon: 16 (over x_hi, y, core).
Axes of the slice: x: 4 (x_hi: 2, x_lo: 2; x = x_hi * 2 + x_lo), y: 4, z: 4, core: 2. Of those that a mesh axis runs over, the one named last changes fastest.
Arguments:
- tokens: bfloat16 [2, 96, 192, 1024], P(None, 'lat', 'lon'), may hold values from -37 to 37
- masked: int32 [8, 16, 144], P('lat', 'lon'), may hold values from 0 to 287, all different within a row
- mask_embed: bfloat16 [1024], replicated, may hold values from -6 to 6
- w_qkv: bfloat16 [1024, 3072], replicated
- w_out: bfloat16 [1024, 1024], replicated, may hold values from -0.1875 to 0.1875
- cotangent: bfloat16 [2, 96, 192, 1024], P(None, 'lat', 'lon'), may hold values from -6 to 6
Outputs:
- block_out: bfloat16 [2, 96, 192, 1024], P(None, 'lat', 'lon')
- grad_tokens: bfloat16 [2, 96, 192, 1024], P(None, 'lat', 'lon')
- grad_qkv: float32 [1024, 3072], P(('lat', 'lon'))
- grad_out: float32 [1024, 1024], P(('lat', 'lon'))
- grad_mask: float32 [1024], P(('lat', 'lon'))
The draws below stay inside these ranges and needn't reach their ends.
Inputs may be any that keep to these rules, and one draw needn't show every extreme that they name: `masked`: within each tile the 144 listed positions are all different.
All inputs are finite; a program needn't handle non-finite values.
Results may differ from the reference program's by a relative error of at most 0.012.
The reference program's roundings to bfloat16 on the way count: a program that leaves them out, or rounds other values in their place, can miss the bound.
Values may be sent and summed in bfloat16 or wider, within the bound.
A program may use at most 128 MiB of HBM per device.

```python
import math
import jax
import jax.numpy as jnp
from jax import lax

D = 1024
HEADS = 16
LEV = 2
TILE = 12
MASKED = 144
NLAT = 96
NLON = 192


def draw_tokens(key, part):
    key = jax.random.fold_in(key, 11)
    first = jax.random.fold_in(key, 0)
    base = jnp.clip(jax.random.normal(first, (LEV, NLAT, NLON, D), jnp.float32), -6.0, 6.0)
    return base.astype(jnp.bfloat16)


def draw_w_qkv(key, part):
    key = jax.random.fold_in(key, 23)
    first, second, third = jax.random.split(key, 3)
    norm = 1.0 / math.sqrt(D)
    wq = jnp.clip(jax.random.normal(first, (D, D), jnp.float32), -6.0, 6.0) * norm
    wk = jnp.clip(jax.random.normal(second, (D, D), jnp.float32), -6.0, 6.0) * norm
    wv = jnp.clip(jax.random.normal(third, (D, D), jnp.float32), -6.0, 6.0) * norm
    return jnp.concatenate([wq, wk, wv], axis=1).astype(jnp.bfloat16)


def block_levels(key, extent, cuts, least, largest):
    loudness, own = 1.0, jax.random.fold_in(key, 6)
    for position, parts in cuts:
        steps = jnp.exp(jax.random.uniform(jax.random.fold_in(own, position), (parts,), jnp.float32, least / len(cuts), largest / len(cuts)))
        loudness = loudness * jnp.repeat(steps, extent[position] // parts).reshape([-1 if axis == position else 1 for axis in range(len(extent))])
    return loudness


def picks_of(key, rows, amount, top, lift):
    sequence = jax.random.permutation(jax.random.fold_in(key, 1), amount)
    boost = sequence
    for power in range(3):
        boost = boost * boost // amount
    boost = boost * lift // amount
    tickets = jax.random.randint(jax.random.fold_in(key, 2), (rows, amount), 0, 4096) + boost
    sure = jax.random.permutation(jax.random.fold_in(key, 3), rows)[jnp.arange(amount) % rows]
    tickets = jnp.where(jnp.arange(rows)[:, None] == sure[None, :], 1 << 14, tickets)
    priority = tickets * amount + jnp.arange(amount)
    return lax.top_k(priority.astype(jnp.int32), top)[1].astype(jnp.int32)


def centred(stream_key, dims, scale, limit, shards=(), held_as=jnp.bfloat16):
    values = jax.random.normal(stream_key, dims, jnp.float32) * scale
    if len(shards) > 0:
        values = block_levels(stream_key, dims, shards, -0.22, 0.18) * values
    return jnp.clip(values, min=-limit, max=limit).astype(held_as)


def setup_inputs(seed: int = 0) -> dict:
    arg_keys = jax.random.split(jax.random.key(seed), 7)
    return {
        "tokens": draw_tokens(jax.random.fold_in(arg_keys[6], 71), 0),
        "masked": picks_of(arg_keys[1], (NLAT // TILE) * (NLON // TILE), LEV * TILE * TILE, MASKED, 0).reshape((NLAT // TILE, NLON // TILE, MASKED)),
        "mask_embed": centred(arg_keys[2], (D,), 1.0, 6.0),
        "w_qkv": draw_w_qkv(jax.random.fold_in(arg_keys[6], 71), 0),
        "w_out": centred(arg_keys[4], (D, D), D ** -0.5, 0.1875),
        "cotangent": centred(arg_keys[5], (LEV, NLAT, NLON, D), 1.0, 6.0, ((1, 8), (2, 16))),
    }


def tile_flags(masked, lev):
    rows_t, cols_t, count = masked.shape
    cells = lev * 144
    hit = jnp.any(masked[:, :, None, :] == jnp.arange(cells, dtype=jnp.int32)[:, None], axis=-1)
    return hit.reshape(rows_t, cols_t, lev, 12, 12).transpose(2, 0, 3, 1, 4).reshape(lev, rows_t * 12, cols_t * 12)

def attend_tiles(query, kv_ext, dctx, lat_ok, heads):
    lev, rlat, rlon, width = query.shape
    tiles_lat = rlat // 12
    tiles_lon = rlon // 12
    head_dim = width // heads
    group = 4 if heads % 4 == 0 else heads
    ngroup = heads // group
    scale = 1.0 / math.sqrt(head_dim)
    cells = lev * 144
    keys = lev * 576
    qpos = jnp.arange(cells, dtype=jnp.int32)
    kpos = jnp.arange(keys, dtype=jnp.int32)
    qrow = qpos // 12 % 12
    qcol = qpos % 12
    krow = kpos // 24 % 24
    kcol = kpos % 24
    base = (krow[None, :] >= qrow[:, None]) & (krow[None, :] <= qrow[:, None] + 11)
    base = base & (kcol[None, :] >= qcol[:, None]) & (kcol[None, :] <= qcol[:, None] + 11)
    f32 = jnp.float32

    def head_group(args, allowed):
        qh, kh, vh, dh = args
        scores = jnp.einsum('qgd,kgd->gqk', qh.astype(f32), kh.astype(f32)) * scale
        scores = jnp.where(allowed[None], scores, -1e+30)
        top = lax.optimization_barrier(jnp.max(scores, axis=-1, keepdims=True))
        expo = jnp.exp(scores - top)
        probs = expo / lax.optimization_barrier(jnp.sum(expo, axis=-1, keepdims=True))
        probs_b = probs.astype(jnp.bfloat16)
        ctx = jnp.einsum('gqk,kgd->qgd', probs_b.astype(f32), vh.astype(f32)).astype(jnp.bfloat16)
        dprob = jnp.einsum('qgd,kgd->gqk', dh.astype(f32), vh.astype(f32))
        delta = lax.optimization_barrier(jnp.sum(probs * dprob, axis=-1, keepdims=True))
        dscore = (probs * (dprob - delta)).astype(jnp.bfloat16)
        dquery = (jnp.einsum('gqk,kgd->qgd', dscore.astype(f32), kh.astype(f32)) * scale).astype(jnp.bfloat16)
        dkey = jnp.einsum('gqk,qgd->kgd', dscore.astype(f32), qh.astype(f32)) * scale
        dvalue = jnp.einsum('gqk,qgd->kgd', probs_b.astype(f32), dh.astype(f32))
        return (ctx, dquery, dkey, dvalue)

    def split_heads(arr, rows):
        return arr.reshape(rows, ngroup, group, head_dim).transpose(1, 0, 2, 3)

    def join_heads(arr, rows):
        return arr.transpose(1, 0, 2, 3).reshape(rows, width)

    def step(acc, tile):
        zero = jnp.zeros((), jnp.int32)
        row0 = (tile // tiles_lon * 12).astype(jnp.int32)
        col0 = (tile % tiles_lon * 12).astype(jnp.int32)
        qt = lax.dynamic_slice(query, (zero, row0, col0, zero), (lev, 12, 12, width)).reshape(cells, width)
        dt = lax.dynamic_slice(dctx, (zero, row0, col0, zero), (lev, 12, 12, width)).reshape(cells, width)
        kvt = lax.dynamic_slice(kv_ext, (zero, row0, col0, zero), (lev, 24, 24, 2 * width)).reshape(keys, 2 * width)
        okt = lax.dynamic_slice(lat_ok, (row0,), (24,))
        ok_keys = jnp.broadcast_to(okt[None, :, None], (lev, 24, 24)).reshape(keys)
        allowed = base & ok_keys[None, :]
        outs = lax.map(lambda a: head_group(a, allowed), (split_heads(qt, cells), split_heads(kvt[:, :width], keys), split_heads(kvt[:, width:], keys), split_heads(dt, cells)))
        ctx_t = join_heads(outs[0], cells)
        dq_t = join_heads(outs[1], cells)
        dkv_t = jnp.concatenate([join_heads(outs[2], keys), join_heads(outs[3], keys)], axis=1)
        dkv_t = dkv_t.reshape(lev, 24, 24, 2 * width).astype(acc.dtype)
        start = (zero, row0, col0, zero)
        acc = lax.dynamic_update_slice(acc, lax.dynamic_slice(acc, start, dkv_t.shape) + dkv_t, start)
        return (acc, (ctx_t, dq_t))
    acc0 = jnp.zeros(kv_ext.shape, jnp.float32)
    acc, (ctx_all, dq_all) = lax.scan(step, acc0, jnp.arange(tiles_lat * tiles_lon, dtype=jnp.int32))

    def arrange(arr):
        return arr.reshape(tiles_lat, tiles_lon, lev, 12, 12, width).transpose(2, 0, 3, 1, 4, 5).reshape(lev, rlat, rlon, width)
    return (arrange(ctx_all), arrange(dq_all), acc)

def reference(tokens, masked, mask_embed, w_qkv, w_out, cotangent):
    lev, nlat, nlon, width = tokens.shape
    cells = lev * nlat * nlon
    flags = tile_flags(masked, lev)
    xm = jnp.where(flags[..., None], mask_embed, tokens)
    flat = xm.reshape(cells, width)
    g_flat = cotangent.reshape(cells, width)
    qkv = jnp.dot(flat, w_qkv, preferred_element_type=jnp.float32).astype(jnp.bfloat16)
    query = qkv[:, :width].reshape(lev, nlat, nlon, width)
    kv = qkv[:, width:].reshape(lev, nlat, nlon, 2 * width)
    kv_ext = jnp.concatenate([kv[:, :, nlon - 6:], kv, kv[:, :, :6]], axis=2)
    kv_ext = jnp.pad(kv_ext, ((0, 0), (6, 6), (0, 0), (0, 0)))
    rows = jnp.arange(nlat + 12, dtype=jnp.int32) - 6
    lat_ok = (rows >= 0) & (rows < nlat)
    dctx = lax.dot_general(g_flat, w_out, (((1,), (1,)), ((), ())), preferred_element_type=jnp.float32).astype(jnp.bfloat16)
    ctx, dq, acc = attend_tiles(query, kv_ext, dctx.reshape(lev, nlat, nlon, width), lat_ok, HEADS)
    ctx_flat = ctx.reshape(cells, width)
    block_out = (flat.astype(jnp.float32) + jnp.dot(ctx_flat, w_out, preferred_element_type=jnp.float32)).astype(jnp.bfloat16)
    band = acc[:, 6:6 + nlat]
    own = band[:, :, 6:6 + nlon]
    own = own.at[:, :, nlon - 6:].add(band[:, :, :6])
    own = own.at[:, :, :6].add(band[:, :, nlon + 6:])
    dkv = own.astype(jnp.bfloat16).reshape(cells, 2 * width)
    dqkv = jnp.concatenate([dq.reshape(cells, width), dkv], axis=1)
    total = g_flat.astype(jnp.float32) + lax.dot_general(dqkv, w_qkv, (((1,), (1,)), ((), ())), preferred_element_type=jnp.float32)
    hit = flags.reshape(cells, 1)
    grad_tokens = jnp.where(hit, 0.0, total).astype(jnp.bfloat16).reshape(tokens.shape)
    scale = 1.0 / math.sqrt(cells)
    grad_mask = lax.optimization_barrier(jnp.sum(jnp.where(hit, total, 0.0), axis=0)) * scale
    grad_qkv = lax.dot_general(flat, dqkv, (((0,), (0,)), ((), ())), preferred_element_type=jnp.float32) * scale
    grad_out = lax.dot_general(ctx_flat, g_flat, (((0,), (0,)), ((), ())), preferred_element_type=jnp.float32) * scale
    return (block_out.reshape(tokens.shape), grad_tokens, grad_qkv, grad_out, grad_mask)
```

```python
import functools
import math

import jax
import jax.numpy as jnp
from jax import lax
from jax.experimental import pallas as pl
from jax.experimental.pallas import tpu as pltpu
from jax.sharding import PartitionSpec as P

HEADS = 16


def passed_along(array, axis, by):
    devices = lax.axis_size(axis)
    pairs = [(i, i + by) for i in range(devices) if 0 <= i + by < devices]
    return lax.ppermute(array, axis, pairs)


def from_behind(array, axis, by):
    devices = lax.axis_size(axis)
    return lax.ppermute(array, axis, [(i, (i + by) % devices) for i in range(devices)])


def extended_2(block, sides, width, periodic):
    for axis, dim in sides:
        count = lax.axis_size(axis)
        forward = [(i, i + 1) for i in range(count - 1)]
        if periodic:
            forward.append((count - 1, 0))
        backward = [(target, source) for source, target in forward]
        low = lax.ppermute(
            lax.slice_in_dim(block, block.shape[dim] - width, None, axis=dim), axis, forward
        )
        high = lax.ppermute(lax.slice_in_dim(block, 0, width, axis=dim), axis, backward)
        block = jnp.concatenate([low, block, high], axis=dim)
    return block


def tile_flags(masked, lev):
    rows_t, cols_t, count = masked.shape
    cells = lev * 144
    hit = jnp.any(masked[:, :, None, :] == jnp.arange(cells, dtype=jnp.int32)[:, None], axis=-1)
    return (
        hit.reshape(rows_t, cols_t, lev, 12, 12)
        .transpose(2, 0, 3, 1, 4)
        .reshape(lev, rows_t * 12, cols_t * 12)
    )


def attend_tiles(query, kv_ext, dctx, lat_ok, heads):
    lev, rlat, rlon, width = query.shape
    tiles_lat = rlat // 12
    tiles_lon = rlon // 12
    head_dim = width // heads
    group = 4
    ngroup = heads // group
    scale = 1.0 / math.sqrt(head_dim)
    cells = lev * 144
    keys = lev * 576
    qpos = jnp.arange(cells, dtype=jnp.int32)
    kpos = jnp.arange(keys, dtype=jnp.int32)
    qrow = qpos // 12 % 12
    qcol = qpos % 12
    krow = kpos // 24 % 24
    kcol = kpos % 24
    base = (krow[None, :] >= qrow[:, None]) & (krow[None, :] <= qrow[:, None] + 11)
    base = base & (kcol[None, :] >= qcol[:, None]) & (kcol[None, :] <= qcol[:, None] + 11)
    f32 = jnp.float32

    def head_group(args, allowed):
        qh, kh, vh, dh = args
        scores = jnp.einsum("qgd,kgd->gqk", qh, kh, preferred_element_type=f32) * scale
        scores = jnp.where(allowed[None], scores, -1e30)
        top = jnp.max(scores, axis=-1, keepdims=True)
        expo = jnp.exp(scores - top)
        probs = expo / jnp.sum(expo, axis=-1, keepdims=True)
        probs_b = probs.astype(jnp.bfloat16)
        ctx = jnp.einsum("gqk,kgd->qgd", probs_b, vh, preferred_element_type=f32).astype(
            jnp.bfloat16
        )
        dprob = jnp.einsum("qgd,kgd->gqk", dh, vh, preferred_element_type=f32)
        delta = jnp.sum(probs * dprob, axis=-1, keepdims=True)
        dscore = (probs * (dprob - delta)).astype(jnp.bfloat16)
        dquery = (
            jnp.einsum("gqk,kgd->qgd", dscore, kh, preferred_element_type=f32) * scale
        ).astype(jnp.bfloat16)
        dkey = jnp.einsum("gqk,qgd->kgd", dscore, qh, preferred_element_type=f32) * scale
        dvalue = jnp.einsum("gqk,qgd->kgd", probs_b, dh, preferred_element_type=f32)
        return (ctx, dquery, dkey, dvalue)

    def split_heads(arr, rows):
        return arr.reshape(rows, ngroup, group, head_dim).transpose(1, 0, 2, 3)

    def join_heads(arr, rows):
        return arr.transpose(1, 0, 2, 3).reshape(rows, width)

    def step(acc, tile):
        qt = query.reshape(cells, width)
        dt = dctx.reshape(cells, width)
        kvt = kv_ext.reshape(keys, 2 * width)
        ok_keys = jnp.broadcast_to(lat_ok[None, :, None], (lev, 24, 24)).reshape(keys)
        allowed = base & ok_keys[None, :]
        outs = lax.map(
            lambda a: head_group(a, allowed),
            (
                split_heads(qt, cells),
                split_heads(kvt[:, :width], keys),
                split_heads(kvt[:, width:], keys),
                split_heads(dt, cells),
            ),
        )
        ctx_t = join_heads(outs[0], cells)
        dq_t = join_heads(outs[1], cells)
        dkv_t = jnp.concatenate([join_heads(outs[2], keys), join_heads(outs[3], keys)], axis=1)
        dkv_t = dkv_t.reshape(lev, 24, 24, 2 * width)
        acc = acc + dkv_t
        return (acc, (ctx_t, dq_t))

    acc0 = jnp.zeros(kv_ext.shape, jnp.float32)
    acc, (ctx_all, dq_all) = lax.scan(
        step, acc0, jnp.arange(tiles_lat * tiles_lon, dtype=jnp.int32)
    )

    def arrange(arr):
        return (
            arr.reshape(tiles_lat, tiles_lon, lev, 12, 12, width)
            .transpose(2, 0, 3, 1, 4, 5)
            .reshape(lev, rlat, rlon, width)
        )

    return (arrange(ctx_all), arrange(dq_all), acc)


def return_strips(extended):
    rows = extended.shape[1] - 12
    cols = extended.shape[2] - 12
    for offset in (1, -1):
        if offset == 1:
            piece = extended[:, rows + 6 :]
            target = 6
        else:
            piece = extended[:, :6]
            target = rows
        arrived = passed_along(piece.astype(jnp.bfloat16), "lat", offset).astype(piece.dtype)
        extended = extended.at[:, target : target + 6].add(arrived)
    band = extended[:, 6 : rows + 6]
    for offset in (1, -1):
        if offset == 1:
            piece = band[:, :, cols + 6 :]
            target = 6
        else:
            piece = band[:, :, :6]
            target = cols
        arrived = from_behind(piece.astype(jnp.bfloat16), "lon", offset).astype(piece.dtype)
        band = band.at[:, :, target : target + 6].add(arrived)
    return band[:, :, 6 : cols + 6]


MESH = pl.DeviceIdType.MESH
BF16 = jnp.bfloat16
F32 = jnp.float32

HALF = 2048
WIDE = HALF + 128
PARTS = ((0, 768), (768, 640), (1408, 768))
ORDERS = (("z", "y", "x"), ("x", "z", "y"), ("y", "x", "z"))
REMAINS = (
    ((2, 2, 4), (2, 2), ()),
    ((4, 4), (4,), ()),
    ((4, 2, 2), (4,), ()),
)


def piece_of(part, stage, at):
    every = slice(None)
    hi, lo = lax.div(at, 2), lax.rem(at, 2)
    table = (
        ((at,), (every, every, at), (lo, hi)),
        ((every, lo, hi), (at,), (at,)),
        ((every, every, every, at), (every, lo, hi), (at,)),
    )
    return table[part][stage]


def reduce_kernel(
    lt, rhs, mask_col, gq, go, gm,
    own, got, r10, r11, r12, b0, b1, b2, r20, r21, r22, c0, c1, c2, r30, r31, r32,
    final, crossed, send0, recv0, send, recv, send4, recv4,
):
    r1, r2, r3 = (r10, r11, r12), (r20, r21, r22), (r30, r31, r32)
    sums = (b0, b1, b2), (c0, c1, c2)
    lat, lon = lax.axis_index("lat"), lax.axis_index("lon")
    z, xl = lax.div(lat, 2), lax.rem(lat, 2)
    xh, y, core = lax.div(lon, 8), lax.rem(lax.div(lon, 2), 4), lax.rem(lon, 2)
    x = xh * 2 + xl
    mine = {"x": x, "y": y, "z": z}

    def device(axis, by):
        zz, yy, xx = z, y, x
        if axis == "z":
            zz = lax.rem(z + by, 4)
        elif axis == "y":
            yy = lax.rem(y + by, 4)
        else:
            xx = lax.rem(x + by, 4)
        return (zz * 2 + lax.rem(xx, 2), lax.div(xx, 2) * 8 + yy * 2 + core)

    partner = (lat, lon + 1 - 2 * core)

    barrier = pltpu.get_barrier_semaphore()
    pl.semaphore_signal(barrier, inc=1, device_id=partner, device_id_type=MESH)
    for axis in "xyz":
        for by in (1, 2, 3):
            pl.semaphore_signal(barrier, inc=1, device_id=device(axis, by), device_id_type=MESH)
    pl.semaphore_wait(barrier, 10)

    def make_half(half):
        own[half, :, :, :, :, :, HALF:] = mask_col[...].reshape(4, 2, 2, 4, 16, 128)
        for j in range(2):
            which = half * 2 + j
            left = lax.div(which, 3)

            @pl.loop(0, 4)
            def _(tile):
                rows = pl.ds(pl.multiple_of(tile * 256, 256), 256)
                made = jnp.dot(lt[left, rows, :], rhs[which], preferred_element_type=F32)
                own[half, tile, :, :, :, :, j * 1024 : (j + 1) * 1024] = made.astype(BF16).reshape(
                    2, 2, 4, 16, 1024
                )

    def columns(part):
        return pl.ds(PARTS[part][0], PARTS[part][1])

    make_half(1 - core)
    cross = []
    for part in range(3):
        copy = pltpu.make_async_remote_copy(
            src_ref=own.at[1 - core, :, :, :, :, :, columns(part)],
            dst_ref=got.at[:, :, :, :, :, columns(part)],
            send_sem=send0.at[part],
            recv_sem=recv0.at[part],
            device_id=partner,
            device_id_type=MESH,
        )
        copy.start()
        cross.append(copy)
    make_half(core)

    def start_stage(part, stage, source, slots):
        axis = ORDERS[part][stage]
        copies = []
        for by in (2, 1, 3):
            there = piece_of(part, stage, lax.rem(mine[axis] + by, 4))
            copy = pltpu.make_async_remote_copy(
                src_ref=source(there),
                dst_ref=slots.at[by - 1],
                send_sem=send.at[part * 9 + stage * 3 + by - 1],
                recv_sem=recv.at[part * 9 + stage * 3 + by - 1],
                device_id=device(axis, by),
                device_id_type=MESH,
            )
            copy.start()
            copies.append(copy)
        return copies

    started = []
    for part in range(3):
        cross[part].wait()
        cols = columns(part)

        @pl.loop(0, 4)
        def _(a):
            for b in range(2):
                for c in range(2):
                    total = own[core, a, b, c, :, :, cols].astype(F32) + got[
                        a, b, c, :, :, cols
                    ].astype(F32)
                    own[core, a, b, c, :, :, cols] = total.astype(BF16)

        started.append(
            start_stage(
                part, 0, lambda there, cols=cols: own.at[(core, *there, *open_dims(there, 4), slice(None), cols)], r1[part]
            )
        )
    for part in range(3):
        for copy in started[part]:
            copy.wait()
        cols = columns(part)
        here = piece_of(part, 0, mine[ORDERS[part][0]])
        piece = own[(core, *here, *open_dims(here, 4), slice(None), cols)].astype(F32)
        for slot in range(3):
            piece = piece + r1[part][slot].astype(F32)
        b = sums[0][part]
        b[...] = piece.astype(BF16)
        dims = len(REMAINS[part][0])
        started[part] = start_stage(
            part, 1, lambda there, b=b, dims=dims: b.at[(*there, *open_dims(there, dims))], r2[part]
        )
    for part in range(3):
        for copy in started[part]:
            copy.wait()
        b, c = sums[0][part], sums[1][part]
        dims = len(REMAINS[part][0])
        here = piece_of(part, 1, mine[ORDERS[part][1]])
        piece = b[(*here, *open_dims(here, dims))].astype(F32)
        for slot in range(3):
            piece = piece + r2[part][slot].astype(F32)
        c[...] = piece.astype(BF16)
        started[part] = start_stage(part, 2, lambda there, c=c: c.at[there], r3[part])
    scale = 1.0 / 192.0
    for part in range(3):
        for copy in started[part]:
            copy.wait()
        c = sums[1][part]
        here = piece_of(part, 2, mine[ORDERS[part][2]])
        piece = c[here].astype(F32)
        for slot in range(3):
            piece = piece + r3[part][slot].astype(F32)
        final[:, columns(part)] = piece * scale
    swap = pltpu.make_async_remote_copy(
        src_ref=final.at[pl.ds(pl.multiple_of((1 - core) * 8, 8), 8), pl.ds(0, HALF)],
        dst_ref=crossed,
        send_sem=send4,
        recv_sem=recv4,
        device_id=partner,
        device_id_type=MESH,
    )
    swap.start()
    swap.wait()
    rows = pl.ds(pl.multiple_of(core * 8, 8), 8)
    gm[...] = final[rows, HALF:]

    @pl.when(core == 0)
    def _():
        gq[:, :HALF] = final[rows, :HALF]
        gq[:, HALF:] = crossed[:, :1024]
        go[...] = crossed[:, 1024:]

    @pl.when(core == 1)
    def _():
        gq[:, :HALF] = crossed[...]
        gq[:, HALF:] = final[rows, :1024]
        go[...] = final[rows, 1024:HALF]


def open_dims(there, dims):
    return (slice(None),) * (dims - len(there))


def reduced_gradients(lt, rhs, mask_col):
    stages = [[], [], [], [], []]
    for part, (_, wide) in enumerate(PARTS):
        first, second, _ = REMAINS[part]
        stages[0].append(pltpu.VMEM((3, *first, 16, wide), BF16))
        stages[1].append(pltpu.VMEM((*first, 16, wide), BF16))
        stages[2].append(pltpu.VMEM((3, *second, 16, wide), BF16))
        stages[3].append(pltpu.VMEM((*second, 16, wide), BF16))
        stages[4].append(pltpu.VMEM((3, 16, wide), BF16))
    vmem = pl.BlockSpec(memory_space=pltpu.VMEM)
    return pl.pallas_call(
        reduce_kernel,
        out_shape=(
            jax.ShapeDtypeStruct((8, 3072), F32),
            jax.ShapeDtypeStruct((8, 1024), F32),
            jax.ShapeDtypeStruct((8, 128), F32),
        ),
        in_specs=[vmem] * 3,
        out_specs=(vmem,) * 3,
        scratch_shapes=[
            pltpu.VMEM((2, 4, 2, 2, 4, 16, WIDE), BF16),
            pltpu.VMEM((4, 2, 2, 4, 16, WIDE), BF16),
            *[one for group in stages for one in group],
            pltpu.VMEM((16, WIDE), F32),
            pltpu.VMEM((8, HALF), F32),
            pltpu.SemaphoreType.DMA((3,)),
            pltpu.SemaphoreType.DMA((3,)),
            pltpu.SemaphoreType.DMA((27,)),
            pltpu.SemaphoreType.DMA((27,)),
            pltpu.SemaphoreType.DMA,
            pltpu.SemaphoreType.DMA,
        ],
        compiler_params=pltpu.CompilerParams(
            collective_id=1, has_side_effects=True, vmem_limit_bytes=56 * 1024 * 1024
        ),
        name="reduce_gradients",
    )(lt, rhs, mask_col)


def local(tokens, masked, mask_embed, w_qkv, w_out, cotangent):
    lev, rlat, rlon, width = tokens.shape
    cells = lev * rlat * rlon
    flags = tile_flags(masked, lev)
    xm = jnp.where(flags[..., None], mask_embed, tokens)
    flat = xm.reshape(cells, width)
    g_flat = cotangent.reshape(cells, width)
    dctx = lax.dot_general(
        g_flat, w_out, (((1,), (1,)), ((), ())), preferred_element_type=jnp.float32
    ).astype(jnp.bfloat16)
    query = jnp.dot(flat, w_qkv[:, :width], preferred_element_type=jnp.float32).astype(jnp.bfloat16)
    taller = extended_2(xm, (("lat", 1),), 6, False)
    extended = extended_2(taller, (("lon", 2),), 6, True)
    ext_flat = extended.reshape((rlat + 12) * (rlon + 12) * lev, width)
    extended = jnp.dot(ext_flat, w_qkv[:, width:], preferred_element_type=jnp.float32).astype(
        jnp.bfloat16
    )
    extended = extended.reshape(lev, rlat + 12, rlon + 12, 2 * width)
    rows_all = rlat * lax.axis_size("lat")
    global_rows = lax.axis_index("lat") * rlat + jnp.arange(rlat + 12, dtype=jnp.int32) - 6
    lat_ok = (global_rows >= 0) & (global_rows < rows_all)
    ctx, dq, accum = attend_tiles(
        query.reshape(lev, rlat, rlon, width),
        extended,
        dctx.reshape(lev, rlat, rlon, width),
        lat_ok,
        HEADS,
    )
    ctx_flat = ctx.reshape(cells, width)
    block_out = (
        flat.astype(jnp.float32) + jnp.dot(ctx_flat, w_out, preferred_element_type=jnp.float32)
    ).astype(jnp.bfloat16)
    owned = return_strips(accum).astype(jnp.bfloat16).reshape(cells, 2 * width)
    dqkv = jnp.concatenate([dq.reshape(cells, width), owned], axis=1)
    total = g_flat.astype(jnp.float32) + lax.dot_general(
        dqkv, w_qkv, (((1,), (1,)), ((), ())), preferred_element_type=jnp.float32
    )
    hit = flags.reshape(cells, 1)
    grad_tokens = jnp.where(hit, 0.0, total).astype(jnp.bfloat16).reshape(tokens.shape)
    mask_term = jnp.sum(jnp.where(hit, total, 0.0), axis=0)
    lt = jnp.stack([flat.T, ctx_flat.T])
    rhs = jnp.stack([dqkv[:, :width], dqkv[:, width : 2 * width], dqkv[:, 2 * width :], g_flat])
    mask_col = jnp.broadcast_to(mask_term[:, None], (width, 128)).astype(BF16)
    grad_qkv, grad_out, grad_mask = reduced_gradients(lt, rhs, mask_col)
    grad_mask = grad_mask[:, 0]
    return (block_out.reshape(tokens.shape), grad_tokens, grad_qkv, grad_out, grad_mask)


def solution(mesh):
    placed = (
        P(None, "lat", "lon", None),
        P("lat", "lon", None),
        P(),
        P(),
        P(),
        P(None, "lat", "lon", None),
    )
    return jax.shard_map(
        local,
        mesh=mesh,
        in_specs=placed,
        out_specs=(
            P(None, "lat", "lon", None),
            P(None, "lat", "lon", None),
            P(("lat", "lon"), None),
            P(("lat", "lon"), None),
            P(("lat", "lon")),
        ),
        check_vma=False,
    )
```

```python
import math

import jax
import jax.numpy as jnp
import numpy as np
from jax import lax
from jax.experimental import pallas as pl
from jax.experimental.pallas import tpu as pltpu
from jax.sharding import PartitionSpec as P

HEADS = 16
MESH = pl.DeviceIdType.MESH
BF16 = jnp.bfloat16
F32 = jnp.float32


def piece_order():
    column, row, lev = np.meshgrid(np.arange(12), np.arange(6), np.arange(2), indexing="ij")
    top = (column * 24 + row * 2 + lev).reshape(-1)
    return np.concatenate([top, top + 12])


def middle_order():
    column, row, lev = np.meshgrid(np.arange(12), np.arange(24), np.arange(2), indexing="ij")
    north = column * 12 + row * 2 + lev
    inside = 144 + column * 24 + (row - 6) * 2 + lev
    south = 432 + column * 12 + (row - 18) * 2 + lev
    return np.where(row < 6, north, np.where(row < 18, inside, south)).reshape(-1)


def one_hot(order):
    return (order[:, None] == np.arange(order.size)[None, :]).astype(np.float32)


def near():
    query = np.arange(96)
    key = np.arange(768)
    row, column = query % 24 // 2, query // 24
    krow, kcolumn = key % 48 // 2, key // 48
    allowed = (krow[None] >= row[:, None]) & (krow[None] <= row[:, None] + 11)
    return allowed & (kcolumn[None] >= column[:, None]) & (kcolumn[None] <= column[:, None] + 11)


def dot(a, b):
    return jnp.dot(a, b, preferred_element_type=F32)


def dot_nt(a, b):
    return lax.dot_general(a, b, (((1,), (1,)), ((), ())), preferred_element_type=F32)


def dot_tn(a, b):
    return lax.dot_general(a, b, (((0,), (0,)), ((), ())), preferred_element_type=F32)


def attention_kernel(
    xm, g, w_qkv, w_out, bias, to_piece, from_piece, to_middle, from_middle,
    ctx, dqkv,
    pieces, stacked, ext, q, d, kv, acc, side_out, side_in, piece_out, piece_in, own,
    send, recv,
):
    lat, lon = lax.axis_index("lat"), lax.axis_index("lon")
    north, south = (lax.rem(lat + 7, 8), lon), (lax.rem(lat + 1, 8), lon)
    west, east = (lat, lax.rem(lon + 15, 16)), (lat, lax.rem(lon + 1, 16))
    barrier = pltpu.get_barrier_semaphore()
    for neighbour in (north, south, west, east):
        pl.semaphore_signal(barrier, inc=1, device_id=neighbour, device_id_type=MESH)

    pieces[...] = dot(to_piece[...], xm[...]).astype(BF16)
    stacked[144:432, :] = xm[...]
    pl.semaphore_wait(barrier, 4)

    def copy_to(source, target, sem, device):
        return pltpu.make_async_remote_copy(
            src_ref=source,
            dst_ref=target,
            send_sem=send.at[sem],
            recv_sem=recv.at[sem],
            device_id=device,
            device_id_type=MESH,
        )

    def part(start, rows):
        return pl.ds(start, rows)

    first = (
        copy_to(pieces.at[part(0, 144)], stacked.at[part(432, 144)], 0, north),
        copy_to(pieces.at[part(144, 144)], stacked.at[part(0, 144)], 1, south),
    )
    for copy in first:
        copy.start()

    @pl.loop(0, 4)
    def _(t):
        cols = pl.ds(pl.multiple_of(t * 256, 256), 256)
        q[:, cols] = dot(xm[...], w_qkv[:, cols]).astype(BF16)
        d[:, cols] = dot_nt(g[...], w_out[cols, :]).astype(BF16)

    for copy in first:
        copy.wait()
    ext[288:864, :] = dot(to_middle[...], stacked[...]).astype(BF16)
    second = (
        copy_to(ext.at[part(288, 288)], ext.at[part(864, 288)], 2, west),
        copy_to(ext.at[part(576, 288)], ext.at[part(0, 288)], 3, east),
    )
    for copy in second:
        copy.start()

    def project(start, rows):
        @pl.loop(0, 8)
        def _(t):
            cols = pl.ds(pl.multiple_of(t * 256, 256), 256)
            from_cols = pl.ds(pl.multiple_of(t * 256 + 1024, 256), 256)
            kv[start : start + rows, cols] = dot(
                ext[start : start + rows, :], w_qkv[:, from_cols]
            ).astype(BF16)

    project(288, 576)
    for copy in second:
        copy.wait()
    project(0, 288)
    project(864, 288)

    lane_head = lax.broadcasted_iota(jnp.int32, (96, 256), 1) // 64
    picks = [lane_head == h for h in range(4)]
    nothing = jnp.zeros((96, 256), BF16)
    factor = math.log2(math.e) / 8.0

    def side_copies(t):
        return (
            copy_to(side_out.at[t, 0], side_in.at[t, 1], 4 + 4 * t, west),
            copy_to(side_out.at[t, 1], side_in.at[t, 0], 5 + 4 * t, east),
        )

    def piece_copies(t):
        return (
            copy_to(piece_out.at[t, part(0, 144)], piece_in.at[t, part(144, 144)], 6 + 4 * t, north),
            copy_to(piece_out.at[t, part(144, 144)], piece_in.at[t, part(0, 144)], 7 + 4 * t, south),
        )

    def joined(out):
        total = jnp.where(picks[0], out[0:96], 0.0)
        for h in range(1, 4):
            total = jnp.where(picks[h], out[h * 96 : h * 96 + 96], total)
        return total

    def quad(t):
        cols = pl.ds(pl.multiple_of(t * 256, 256), 256)
        vcols = pl.ds(pl.multiple_of(t * 256 + 1024, 256), 256)
        acc[t] = jnp.zeros((1152, 512), F32)

        @pl.loop(0, 3)
        def _(j):
            rows = pl.ds(pl.multiple_of(j * 96, 96), 96)
            keys = pl.ds(pl.multiple_of(j * 192, 192), 768)
            qj, dj = q[rows, cols], d[rows, cols]
            qm = jnp.concatenate([jnp.where(pick, qj, nothing) for pick in picks], axis=0)
            dm = jnp.concatenate([jnp.where(pick, dj, nothing) for pick in picks], axis=0)
            kw, vw = kv[keys, cols], kv[keys, vcols]
            s = dot_nt(qm, kw).reshape(4, 96, 768) + bias[...][None]
            top = jnp.max(s, axis=-1, keepdims=True)
            e = jnp.exp2((s - top) * factor)
            p = e * (1.0 / jnp.sum(e, axis=-1, keepdims=True))
            p = p.reshape(384, 768)
            pb = p.astype(BF16)
            out = dot(pb, vw)
            delta = jnp.sum(out * dm.astype(F32), axis=-1, keepdims=True)
            ctx[rows, cols] = joined(out).astype(BF16)
            ds = (p * (dot_nt(dm, vw) - delta)).astype(BF16)
            dqkv[rows, cols] = (joined(dot(ds, kw)) * 0.125).astype(BF16)
            acc[t, keys, 0:256] += dot_tn(ds, qm)
            acc[t, keys, 256:512] += dot_tn(pb, dm)

        side_out[t, 0] = acc[t, 0:288, :].astype(BF16)
        side_out[t, 1] = acc[t, 864:1152, :].astype(BF16)
        for copy in side_copies(t):
            copy.start()

    def sides_back(t):
        for copy in side_copies(t):
            copy.wait()
        mid = acc[t, 288:864, :] + side_in[t].astype(F32).reshape(576, 512)
        high = mid.astype(BF16)
        low = (mid - high.astype(F32)).astype(BF16)
        parts = dot(from_middle[...], high)
        piece_out[t, 0:144, :] = parts[0:144].astype(BF16)
        piece_out[t, 144:288, :] = parts[432:576].astype(BF16)
        for copy in piece_copies(t):
            copy.start()
        own[t] = parts[144:432] + dot(from_middle[144:432, :], low)

    def pieces_back(t):
        for copy in piece_copies(t):
            copy.wait()
        total = own[t] + dot(from_piece[...], piece_in[t])
        kcols = pl.ds(pl.multiple_of(t * 256 + 1024, 256), 256)
        vcols = pl.ds(pl.multiple_of(t * 256 + 2048, 256), 256)
        dqkv[:, kcols] = (total[:, 0:256] * 0.125).astype(BF16)
        dqkv[:, vcols] = total[:, 256:512].astype(BF16)

    @pl.loop(0, 6)
    def _(t):
        @pl.when(t < 4)
        def _():
            quad(t)

        @pl.when((t >= 1) & (t < 5))
        def _():
            sides_back(t - 1)

        @pl.when(t >= 2)
        def _():
            pieces_back(t - 2)


def attention(xm, g, w_qkv, w_out, bias):
    order, middle = one_hot(piece_order()), one_hot(middle_order())
    vmem = pl.BlockSpec(memory_space=pltpu.VMEM)
    consts = [jnp.asarray(m, BF16) for m in (order, order.T, middle, middle.T)]
    return pl.pallas_call(
        attention_kernel,
        out_shape=(
            jax.ShapeDtypeStruct((288, 1024), BF16),
            jax.ShapeDtypeStruct((288, 3072), BF16),
        ),
        in_specs=[vmem] * 9,
        out_specs=(vmem,) * 2,
        scratch_shapes=[
            pltpu.VMEM((288, 1024), BF16),
            pltpu.VMEM((576, 1024), BF16),
            pltpu.VMEM((1152, 1024), BF16),
            pltpu.VMEM((288, 1024), BF16),
            pltpu.VMEM((288, 1024), BF16),
            pltpu.VMEM((1152, 2048), BF16),
            pltpu.VMEM((4, 1152, 512), F32),
            pltpu.VMEM((4, 2, 288, 512), BF16),
            pltpu.VMEM((4, 2, 288, 512), BF16),
            pltpu.VMEM((4, 288, 512), BF16),
            pltpu.VMEM((4, 288, 512), BF16),
            pltpu.VMEM((4, 288, 512), F32),
            pltpu.SemaphoreType.DMA((20,)),
            pltpu.SemaphoreType.DMA((20,)),
        ],
        compiler_params=pltpu.CompilerParams(
            collective_id=2, has_side_effects=True, vmem_limit_bytes=60 * 1024 * 1024
        ),
        name="attention",
    )(xm, g, w_qkv, w_out, bias, *consts)


HALF = 2048
WIDE = HALF + 128
PARTS = ((0, 768), (768, 640), (1408, 768))
ORDERS = (("z", "y", "x"), ("x", "z", "y"), ("y", "x", "z"))
REMAINS = (
    ((2, 2, 4), (2, 2), ()),
    ((4, 4), (4,), ()),
    ((4, 2, 2), (4,), ()),
)


def piece_of(part, stage, at):
    every = slice(None)
    hi, lo = lax.div(at, 2), lax.rem(at, 2)
    table = (
        ((at,), (every, every, at), (lo, hi)),
        ((every, lo, hi), (at,), (at,)),
        ((every, every, every, at), (every, lo, hi), (at,)),
    )
    return table[part][stage]


def reduce_kernel(
    lt, rhs, mask_col, gq, go, gm,
    own, got, r10, r11, r12, b0, b1, b2, r20, r21, r22, c0, c1, c2, r30, r31, r32,
    final, crossed, send0, recv0, send, recv, send4, recv4,
):
    r1, r2, r3 = (r10, r11, r12), (r20, r21, r22), (r30, r31, r32)
    sums = (b0, b1, b2), (c0, c1, c2)
    lat, lon = lax.axis_index("lat"), lax.axis_index("lon")
    z, xl = lax.div(lat, 2), lax.rem(lat, 2)
    xh, y, core = lax.div(lon, 8), lax.rem(lax.div(lon, 2), 4), lax.rem(lon, 2)
    x = xh * 2 + xl
    mine = {"x": x, "y": y, "z": z}

    def device(axis, by):
        zz, yy, xx = z, y, x
        if axis == "z":
            zz = lax.rem(z + by, 4)
        elif axis == "y":
            yy = lax.rem(y + by, 4)
        else:
            xx = lax.rem(x + by, 4)
        return (zz * 2 + lax.rem(xx, 2), lax.div(xx, 2) * 8 + yy * 2 + core)

    partner = (lat, lon + 1 - 2 * core)

    barrier = pltpu.get_barrier_semaphore()
    pl.semaphore_signal(barrier, inc=1, device_id=partner, device_id_type=MESH)
    for axis in "xyz":
        for by in (1, 2, 3):
            pl.semaphore_signal(barrier, inc=1, device_id=device(axis, by), device_id_type=MESH)
    pl.semaphore_wait(barrier, 10)

    def make_half(half):
        own[half, :, :, :, :, :, HALF:] = mask_col[...].reshape(4, 2, 2, 4, 16, 128)
        for j in range(2):
            which = half * 2 + j
            left = lax.div(which, 3)

            @pl.loop(0, 4)
            def _(tile):
                rows = pl.ds(pl.multiple_of(tile * 256, 256), 256)
                made = jnp.dot(lt[left, rows, :], rhs[which], preferred_element_type=F32)
                own[half, tile, :, :, :, :, j * 1024 : (j + 1) * 1024] = made.astype(BF16).reshape(
                    2, 2, 4, 16, 1024
                )

    def columns(part):
        return pl.ds(PARTS[part][0], PARTS[part][1])

    make_half(1 - core)
    cross = []
    for part in range(3):
        copy = pltpu.make_async_remote_copy(
            src_ref=own.at[1 - core, :, :, :, :, :, columns(part)],
            dst_ref=got.at[:, :, :, :, :, columns(part)],
            send_sem=send0.at[part],
            recv_sem=recv0.at[part],
            device_id=partner,
            device_id_type=MESH,
        )
        copy.start()
        cross.append(copy)
    make_half(core)

    def start_stage(part, stage, source, slots):
        axis = ORDERS[part][stage]
        copies = []
        for by in (2, 1, 3):
            there = piece_of(part, stage, lax.rem(mine[axis] + by, 4))
            copy = pltpu.make_async_remote_copy(
                src_ref=source(there),
                dst_ref=slots.at[by - 1],
                send_sem=send.at[part * 9 + stage * 3 + by - 1],
                recv_sem=recv.at[part * 9 + stage * 3 + by - 1],
                device_id=device(axis, by),
                device_id_type=MESH,
            )
            copy.start()
            copies.append(copy)
        return copies

    started = []
    for part in range(3):
        cross[part].wait()
        cols = columns(part)

        @pl.loop(0, 4)
        def _(a):
            for b in range(2):
                for c in range(2):
                    total = own[core, a, b, c, :, :, cols].astype(F32) + got[
                        a, b, c, :, :, cols
                    ].astype(F32)
                    own[core, a, b, c, :, :, cols] = total.astype(BF16)

        started.append(
            start_stage(
                part, 0, lambda there, cols=cols: own.at[(core, *there, *open_dims(there, 4), slice(None), cols)], r1[part]
            )
        )
    for part in range(3):
        for copy in started[part]:
            copy.wait()
        cols = columns(part)
        here = piece_of(part, 0, mine[ORDERS[part][0]])
        piece = own[(core, *here, *open_dims(here, 4), slice(None), cols)].astype(F32)
        for slot in range(3):
            piece = piece + r1[part][slot].astype(F32)
        b = sums[0][part]
        b[...] = piece.astype(BF16)
        dims = len(REMAINS[part][0])
        started[part] = start_stage(
            part, 1, lambda there, b=b, dims=dims: b.at[(*there, *open_dims(there, dims))], r2[part]
        )
    for part in range(3):
        for copy in started[part]:
            copy.wait()
        b, c = sums[0][part], sums[1][part]
        dims = len(REMAINS[part][0])
        here = piece_of(part, 1, mine[ORDERS[part][1]])
        piece = b[(*here, *open_dims(here, dims))].astype(F32)
        for slot in range(3):
            piece = piece + r2[part][slot].astype(F32)
        c[...] = piece.astype(BF16)
        started[part] = start_stage(part, 2, lambda there, c=c: c.at[there], r3[part])
    scale = 1.0 / 192.0
    for part in range(3):
        for copy in started[part]:
            copy.wait()
        c = sums[1][part]
        here = piece_of(part, 2, mine[ORDERS[part][2]])
        piece = c[here].astype(F32)
        for slot in range(3):
            piece = piece + r3[part][slot].astype(F32)
        final[:, columns(part)] = piece * scale
    swap = pltpu.make_async_remote_copy(
        src_ref=final.at[pl.ds(pl.multiple_of((1 - core) * 8, 8), 8), pl.ds(0, HALF)],
        dst_ref=crossed,
        send_sem=send4,
        recv_sem=recv4,
        device_id=partner,
        device_id_type=MESH,
    )
    swap.start()
    swap.wait()
    rows = pl.ds(pl.multiple_of(core * 8, 8), 8)
    gm[...] = final[rows, HALF:]

    @pl.when(core == 0)
    def _():
        gq[:, :HALF] = final[rows, :HALF]
        gq[:, HALF:] = crossed[:, :1024]
        go[...] = crossed[:, 1024:]

    @pl.when(core == 1)
    def _():
        gq[:, :HALF] = crossed[...]
        gq[:, HALF:] = final[rows, :1024]
        go[...] = final[rows, 1024:HALF]


def open_dims(there, dims):
    return (slice(None),) * (dims - len(there))


def reduced_gradients(lt, rhs, mask_col):
    stages = [[], [], [], [], []]
    for part, (_, wide) in enumerate(PARTS):
        first, second, _ = REMAINS[part]
        stages[0].append(pltpu.VMEM((3, *first, 16, wide), BF16))
        stages[1].append(pltpu.VMEM((*first, 16, wide), BF16))
        stages[2].append(pltpu.VMEM((3, *second, 16, wide), BF16))
        stages[3].append(pltpu.VMEM((*second, 16, wide), BF16))
        stages[4].append(pltpu.VMEM((3, 16, wide), BF16))
    vmem = pl.BlockSpec(memory_space=pltpu.VMEM)
    return pl.pallas_call(
        reduce_kernel,
        out_shape=(
            jax.ShapeDtypeStruct((8, 3072), F32),
            jax.ShapeDtypeStruct((8, 1024), F32),
            jax.ShapeDtypeStruct((8, 128), F32),
        ),
        in_specs=[vmem] * 3,
        out_specs=(vmem,) * 3,
        scratch_shapes=[
            pltpu.VMEM((2, 4, 2, 2, 4, 16, WIDE), BF16),
            pltpu.VMEM((4, 2, 2, 4, 16, WIDE), BF16),
            *[one for group in stages for one in group],
            pltpu.VMEM((16, WIDE), F32),
            pltpu.VMEM((8, HALF), F32),
            pltpu.SemaphoreType.DMA((3,)),
            pltpu.SemaphoreType.DMA((3,)),
            pltpu.SemaphoreType.DMA((27,)),
            pltpu.SemaphoreType.DMA((27,)),
            pltpu.SemaphoreType.DMA,
            pltpu.SemaphoreType.DMA,
        ],
        compiler_params=pltpu.CompilerParams(
            collective_id=1, has_side_effects=True, vmem_limit_bytes=56 * 1024 * 1024
        ),
        name="reduce_gradients",
    )(lt, rhs, mask_col)


def local(tokens, masked, mask_embed, w_qkv, w_out, cotangent):
    width = tokens.shape[-1]
    hit = jnp.any(masked[0, 0, None, :] == jnp.arange(288, dtype=jnp.int32)[:, None], axis=-1)
    hit = hit.reshape(2, 12, 12).transpose(2, 1, 0).reshape(288, 1)

    def to_own(array):
        return array.transpose(2, 1, 0, 3).reshape(288, width)

    def from_own(array):
        return array.reshape(12, 12, 2, width).transpose(2, 1, 0, 3)

    xm = jnp.where(hit, mask_embed[None, :], to_own(tokens))
    g = to_own(cotangent)
    rows = lax.axis_index("lat") * 12 + jnp.arange(768, dtype=jnp.int32) % 48 // 2 - 6
    on_grid = (rows >= 0) & (rows < 96)
    bias = jnp.where(jnp.asarray(near()) & on_grid[None], 0.0, -jnp.inf).astype(F32)
    ctx, dqkv = attention(xm, g, w_qkv, w_out, bias)
    block_out = (xm.astype(F32) + dot(ctx, w_out)).astype(BF16)
    total = g.astype(F32) + dot_nt(dqkv, w_qkv)
    grad_tokens = jnp.where(hit, 0.0, total).astype(BF16)
    mask_term = jnp.sum(jnp.where(hit, total, 0.0), axis=0)
    lt = jnp.stack([xm.T, ctx.T])
    rhs = jnp.stack([dqkv[:, :width], dqkv[:, width : 2 * width], dqkv[:, 2 * width :], g])
    mask_col = jnp.broadcast_to(mask_term[:, None], (width, 128)).astype(BF16)
    grad_qkv, grad_out, grad_mask = reduced_gradients(lt, rhs, mask_col)
    return (from_own(block_out), from_own(grad_tokens), grad_qkv, grad_out, grad_mask[:, 0])


def solution(mesh):
    placed = (
        P(None, "lat", "lon", None),
        P("lat", "lon", None),
        P(),
        P(),
        P(),
        P(None, "lat", "lon", None),
    )
    return jax.shard_map(
        local,
        mesh=mesh,
        in_specs=placed,
        out_specs=(
            P(None, "lat", "lon", None),
            P(None, "lat", "lon", None),
            P(("lat", "lon"), None),
            P(("lat", "lon"), None),
            P(("lat", "lon")),
        ),
        check_vma=False,
    )
```

```python
import math

import jax
import jax.numpy as jnp
import numpy as np
from jax import lax
from jax.experimental import pallas as pl
from jax.experimental.pallas import tpu as pltpu
from jax.sharding import PartitionSpec as P

HEADS = 16
MESH = pl.DeviceIdType.MESH
BF16 = jnp.bfloat16
F32 = jnp.float32
EVERY = slice(None)


JOBS = (
    (0, 0, 512, "zyx"),
    (0, 512, 512, "yzx"),
    (1, 0, 384, "xzy"),
    (1, 384, 384, "zyx"),
    (1, 768, 384, "yxz"),
)
WIDE = (1024, 1152)


def piece_order():
    column, row, lev = np.meshgrid(np.arange(12), np.arange(6), np.arange(2), indexing="ij")
    top = (column * 24 + row * 2 + lev).reshape(-1)
    return np.concatenate([top, top + 12])


def middle_order():
    column, row, lev = np.meshgrid(np.arange(12), np.arange(24), np.arange(2), indexing="ij")
    north = column * 12 + row * 2 + lev
    inside = 144 + column * 24 + (row - 6) * 2 + lev
    south = 432 + column * 12 + (row - 18) * 2 + lev
    return np.where(row < 6, north, np.where(row < 18, inside, south)).reshape(-1)


def padded_order():
    column, row, lev = np.meshgrid(np.arange(12), np.arange(12), np.arange(2), indexing="ij")
    return (lev * 192 + row * 16 + column).reshape(-1)


def one_hot(order, size):
    return (order[:, None] == np.arange(size)[None, :]).astype(np.float32)


def near():
    query = np.arange(96)
    key = np.arange(768)
    row, column = query % 24 // 2, query // 24
    krow, kcolumn = key % 48 // 2, key // 48
    allowed = (krow[None] >= row[:, None]) & (krow[None] <= row[:, None] + 11)
    return allowed & (kcolumn[None] >= column[:, None]) & (kcolumn[None] <= column[:, None] + 11)


def dot(a, b):
    return jnp.dot(a, b, preferred_element_type=F32)


def dot_nt(a, b):
    return lax.dot_general(a, b, (((1,), (1,)), ((), ())), preferred_element_type=F32)


def dot_tn(a, b):
    return lax.dot_general(a, b, (((0,), (0,)), ((), ())), preferred_element_type=F32)


def without(axes, count):
    return [axis for axis in "zxy" if axis not in axes[:count]]


def extent(axes):
    return tuple(size for axis in axes for size in ((2, 2) if axis == "x" else (4,)))


def index_of(axes, chosen, at):
    out = []
    for axis in axes:
        if axis == "x":
            out += [lax.rem(at, 2), lax.div(at, 2)] if chosen == "x" else [EVERY, EVERY]
        else:
            out += [at] if axis == chosen else [EVERY]
    return tuple(out)


def block_kernel(
    tokens, masked, embed, w_qkv_hbm, w_out_hbm, cotangent, near_bias,
    from_padded, to_padded, to_piece, from_piece, to_middle, from_middle,
    block_out, grad_tokens, gq, go, gm,
    w_qkv, w_out, padded, xm, g, bias, hits, ctx, dqkv,
    pieces, stacked, ext, q, d, kv, acc, side_out, side_in, piece_out, piece_in, own_kv,
    made, got_a, got_b, *rest,
):
    scratch = [rest[5 * i : 5 * i + 5] for i in range(5)]
    final_a, final_b, cross_a, cross_b, load, send, recv = rest[25:]
    lat, lon = lax.axis_index("lat"), lax.axis_index("lon")
    z, xl = lax.div(lat, 2), lax.rem(lat, 2)
    xh, y, core = lax.div(lon, 8), lax.rem(lax.div(lon, 2), 4), lax.rem(lon, 2)
    x = xh * 2 + xl
    mine = {"x": x, "y": y, "z": z}

    def device(axis, by):
        zz, yy, xx = z, y, x
        if axis == "z":
            zz = lax.rem(z + by, 4)
        elif axis == "y":
            yy = lax.rem(y + by, 4)
        else:
            xx = lax.rem(x + by, 4)
        return (zz * 2 + lax.rem(xx, 2), lax.div(xx, 2) * 8 + yy * 2 + core)

    partner = (lat, lon + 1 - 2 * core)
    north, south = (lax.rem(lat + 7, 8), lon), (lax.rem(lat + 1, 8), lon)
    west, east = (lat, lax.rem(lon + 15, 16)), (lat, lax.rem(lon + 1, 16))

    barrier = pltpu.get_barrier_semaphore()
    greeted = [north, south, west, east, partner]
    greeted += [device(axis, by) for axis in "xyz" for by in (1, 2, 3)]
    for other in greeted:
        pl.semaphore_signal(barrier, inc=1, device_id=other, device_id_type=MESH)

    loads = (
        pltpu.make_async_copy(w_qkv_hbm, w_qkv, load.at[0]),
        pltpu.make_async_copy(w_out_hbm, w_out, load.at[1]),
    )
    for copy in loads:
        copy.start()

    place = lax.broadcasted_iota(jnp.int32, (288, 144), 0)
    place = lax.rem(place, 2) * 144 + lax.div(lax.rem(place, 24), 2) * 12 + lax.div(place, 24)
    found = jnp.where(masked[0] == place, 1.0, 0.0)
    hit = jnp.max(found, axis=-1, keepdims=True) > 0.5
    hits[...] = jnp.where(hit, 1.0, 0.0) + jnp.zeros((288, 128), F32)
    padded[...] = jnp.zeros((24, 16, 1024), BF16)
    padded[:, 0:12, :] = tokens[...].reshape(24, 12, 1024)
    own_tokens = dot(from_padded[...], padded[...].reshape(384, 1024))
    xm[...] = jnp.where(hit, embed[...].astype(F32), own_tokens).astype(BF16)

    pieces[...] = dot(to_piece[...], xm[...]).astype(BF16)
    stacked[144:432, :] = xm[...]
    pl.semaphore_wait(barrier, len(greeted))

    def copy_to(source, target, sem, other):
        return pltpu.make_async_remote_copy(
            src_ref=source,
            dst_ref=target,
            send_sem=send.at[sem],
            recv_sem=recv.at[sem],
            device_id=other,
            device_id_type=MESH,
        )

    def part(start, rows):
        return pl.ds(start, rows)

    def tile(t, start=0):
        return pl.ds(pl.multiple_of(t * 256 + start, 256), 256)

    first = (
        copy_to(pieces.at[part(0, 144)], stacked.at[part(432, 144)], 0, north),
        copy_to(pieces.at[part(144, 144)], stacked.at[part(0, 144)], 1, south),
    )
    for copy in first:
        copy.start()

    padded[:, 0:12, :] = cotangent[...].reshape(24, 12, 1024)
    g[...] = dot(from_padded[...], padded[...].reshape(384, 1024)).astype(BF16)
    key_row = lax.broadcasted_iota(jnp.int32, (1, 768), 1)
    key_row = lax.div(lax.rem(key_row, 48), 2) + lat * 12 - 6
    bias[...] = jnp.where((key_row >= 0) & (key_row < 96), near_bias[...], -jnp.inf)
    for copy in loads:
        copy.wait()

    @pl.loop(0, 4)
    def _(t):
        cols = tile(t)
        q[:, cols] = dot(xm[...], w_qkv[:, cols]).astype(BF16)
        d[:, cols] = dot_nt(g[...], w_out[cols, :]).astype(BF16)

    for copy in first:
        copy.wait()
    ext[288:864, :] = dot(to_middle[...], stacked[...]).astype(BF16)
    second = (
        copy_to(ext.at[part(288, 288)], ext.at[part(864, 288)], 2, west),
        copy_to(ext.at[part(576, 288)], ext.at[part(0, 288)], 3, east),
    )
    for copy in second:
        copy.start()

    def project(start, rows):
        @pl.loop(0, 8)
        def _(t):
            kv[start : start + rows, tile(t)] = dot(
                ext[start : start + rows, :], w_qkv[:, tile(t, 1024)]
            ).astype(BF16)

    project(288, 576)
    for copy in second:
        copy.wait()
    project(0, 288)
    project(864, 288)

    lane_head = lax.div(lax.broadcasted_iota(jnp.int32, (96, 256), 1), 64)
    picks = [lane_head == h for h in range(4)]
    nothing = jnp.zeros((96, 256), BF16)
    factor = math.log2(math.e) / 8.0

    def side_copies(t):
        return (
            copy_to(side_out.at[t, 0], side_in.at[t, 1], 4 + 4 * t, west),
            copy_to(side_out.at[t, 1], side_in.at[t, 0], 5 + 4 * t, east),
        )

    def piece_copies(t):
        return (
            copy_to(piece_out.at[t, part(0, 144)], piece_in.at[t, part(144, 144)], 6 + 4 * t, north),
            copy_to(piece_out.at[t, part(144, 144)], piece_in.at[t, part(0, 144)], 7 + 4 * t, south),
        )

    def joined(out):
        total = jnp.where(picks[0], out[0:96], 0.0)
        for h in range(1, 4):
            total = jnp.where(picks[h], out[h * 96 : h * 96 + 96], total)
        return total

    def quad(t):
        cols, vcols = tile(t), tile(t, 1024)
        slot = lax.rem(t, 2)
        acc[slot] = jnp.zeros((1152, 512), F32)

        @pl.loop(0, 3)
        def _(j):
            rows = pl.ds(pl.multiple_of(j * 96, 96), 96)
            keys = pl.ds(pl.multiple_of(j * 192, 192), 768)
            qj, dj = q[rows, cols], d[rows, cols]
            qm = jnp.concatenate([jnp.where(pick, qj, nothing) for pick in picks], axis=0)
            dm = jnp.concatenate([jnp.where(pick, dj, nothing) for pick in picks], axis=0)
            kw, vw = kv[keys, cols], kv[keys, vcols]
            s = dot_nt(qm, kw).reshape(4, 96, 768) + bias[...][None]
            top = jnp.max(s, axis=-1, keepdims=True)
            e = jnp.exp2((s - top) * factor)
            p = e * (1.0 / jnp.sum(e, axis=-1, keepdims=True))
            p = p.reshape(384, 768)
            pb = p.astype(BF16)
            out = dot(pb, vw)
            delta = jnp.sum(out * dm.astype(F32), axis=-1, keepdims=True)
            ctx[rows, cols] = joined(out).astype(BF16)
            ds = (p * (dot_nt(dm, vw) - delta)).astype(BF16)
            dqkv[rows, cols] = (joined(dot(ds, kw)) * 0.125).astype(BF16)
            acc[slot, keys, 0:256] += dot_tn(ds, qm)
            acc[slot, keys, 256:512] += dot_tn(pb, dm)

        side_out[t, 0] = acc[slot, 0:288, :].astype(BF16)
        side_out[t, 1] = acc[slot, 864:1152, :].astype(BF16)
        for copy in side_copies(t):
            copy.start()

    def sides_back(t):
        for copy in side_copies(t):
            copy.wait()
        slot = lax.rem(t, 2)
        mid = acc[slot, 288:864, :] + side_in[t].astype(F32).reshape(576, 512)
        high = mid.astype(BF16)
        low = (mid - high.astype(F32)).astype(BF16)
        parts = dot(from_middle[...], high)
        piece_out[t, 0:144, :] = parts[0:144].astype(BF16)
        piece_out[t, 144:288, :] = parts[432:576].astype(BF16)
        for copy in piece_copies(t):
            copy.start()
        own_kv[slot] = parts[144:432] + dot(from_middle[144:432, :], low)

    def pieces_back(t):
        for copy in piece_copies(t):
            copy.wait()
        total = own_kv[lax.rem(t, 2)] + dot(from_piece[...], piece_in[t])
        dqkv[:, tile(t, 1024)] = (total[:, 0:256] * 0.125).astype(BF16)
        dqkv[:, tile(t, 2048)] = total[:, 256:512].astype(BF16)

    @pl.loop(0, 4)
    def _(t):
        quad(t)

        @pl.when(t >= 1)
        def _():
            sides_back(t - 1)

        @pl.when(t >= 2)
        def _():
            pieces_back(t - 2)

    gots = (got_a, got_b)

    def columns(job):
        return pl.ds(JOBS[job][1], JOBS[job][2])

    def store_made(half, t, value):
        made[half, t, :, :, :, :, 0:1024] = value.astype(BF16).reshape(2, 2, 4, 16, 1024)

    def make_a(half):
        @pl.when(half == 0)
        def _():
            @pl.loop(0, 4)
            def _(t):
                store_made(half, t, dot_tn(xm[:, tile(t)], dqkv[:, 0:1024]))

        @pl.when(half == 1)
        def _():
            @pl.loop(0, 4)
            def _(t):
                store_made(half, t, dot_tn(ctx[:, tile(t)], g[...]))

    def make_b(half):
        cols = pl.ds(pl.multiple_of(half * 1024 + 1024, 1024), 1024)

        @pl.loop(0, 4)
        def _(t):
            store_made(half, t, dot_tn(xm[:, tile(t)], dqkv[:, cols]))

    def exchange(job):
        where = (EVERY,) * 5 + (columns(job),)
        return copy_to(made.at[(1 - core, *where)], gots[JOBS[job][0]].at[where], 20 + job, partner)

    def exchanged(job):
        exchange(job).wait()
        cols, got = columns(job), gots[JOBS[job][0]]

        @pl.loop(0, 4)
        def _(a):
            for b in range(2):
                for c in range(2):
                    total = made[core, a, b, c, :, :, cols].astype(F32)
                    total = total + got[a, b, c, :, :, cols].astype(F32)
                    made[core, a, b, c, :, :, cols] = total.astype(BF16)

    def held(job, stage, at):
        order = JOBS[job][3]
        here = index_of(without(order, stage), order[stage], at)
        if stage == 0:
            return made, (core, *here, EVERY, columns(job))
        return scratch[job][2 * stage - 1], (*here, EVERY, EVERY)

    def stage_copies(job, stage):
        axis = JOBS[job][3][stage]
        copies = []
        for by in (2, 1, 3):
            ref, where = held(job, stage, lax.rem(mine[axis] + by, 4))
            target = scratch[job][2 * stage].at[by - 1]
            sem = 25 + job * 9 + stage * 3 + by - 1
            copies.append(copy_to(ref.at[where], target, sem, device(axis, by)))
        return copies

    def start(job, stage):
        for copy in stage_copies(job, stage):
            copy.start()

    def reduced(job, stage):
        for copy in stage_copies(job, stage):
            copy.wait()
        ref, where = held(job, stage, mine[JOBS[job][3][stage]])
        piece = ref[where].astype(F32)
        for slot in range(3):
            piece = piece + scratch[job][2 * stage][slot].astype(F32)
        if stage < 2:
            scratch[job][2 * stage + 1][...] = piece.astype(BF16)
        else:
            final = (final_a, final_b)[JOBS[job][0]]
            final[:, columns(job)] = piece * (1.0 / 192.0)

    def swap(phase):
        rows = pl.ds(pl.multiple_of((1 - core) * 8, 8), 8)
        source = (final_a, final_b)[phase].at[rows, pl.ds(0, 1024)]
        return copy_to(source, (cross_a, cross_b)[phase], 70 + phase, partner)

    make_a(1 - core)
    for job in (0, 1):
        exchange(job).start()
    sides_back(3)
    make_a(core)
    for job in (0, 1):
        exchanged(job)
        start(job, 0)
    pieces_back(2)

    @pl.loop(0, 4)
    def _(t):
        cols = tile(t)
        value = xm[:, cols].astype(F32) + dot(ctx[...], w_out[:, cols])
        value = dot(to_padded[...], value.astype(BF16)).astype(BF16)
        block_out[:, :, :, cols] = value.reshape(2, 12, 16, 256)[:, :, 0:12, :]

    for job in (0, 1):
        reduced(job, 0)
        start(job, 1)
    pieces_back(3)

    make_b(1 - core)
    for job in (2, 3):
        exchange(job).start()

    @pl.loop(0, 4)
    def _(t):
        cols = tile(t)
        hit = hits[...]
        total = g[:, cols].astype(F32) + dot_nt(dqkv[...], w_qkv[cols, :])
        kept = jnp.where(jnp.concatenate([hit, hit], axis=1) > 0.5, 0.0, total).astype(BF16)
        kept = dot(to_padded[...], kept).astype(BF16)
        grad_tokens[:, :, :, cols] = kept.reshape(2, 12, 16, 256)[:, :, 0:12, :]
        high = total.astype(BF16)
        low = (total - high.astype(F32)).astype(BF16)
        column = dot_tn(high, hit.astype(BF16)) + dot_tn(low, hit.astype(BF16))
        column = column.astype(BF16).reshape(2, 2, 4, 16, 128)
        made[0, t, :, :, :, :, 1024:1152] = column
        made[1, t, :, :, :, :, 1024:1152] = column

    exchange(4).start()
    make_b(core)
    for job in (0, 1):
        reduced(job, 1)
        start(job, 2)
    for job in (2, 3, 4):
        exchanged(job)
        start(job, 0)
    for job in (0, 1):
        reduced(job, 2)
    swap(0).start()
    for stage in (0, 1):
        for job in (2, 3, 4):
            reduced(job, stage)
            start(job, stage + 1)
    for job in (2, 3, 4):
        reduced(job, 2)
    swap(1).start()
    swap(0).wait()
    swap(1).wait()
    rows = pl.ds(pl.multiple_of(core * 8, 8), 8)
    gm[...] = final_b[rows, 1024:]

    @pl.when(core == 0)
    def _():
        gq[:, 0:1024] = final_a[rows, :]
        gq[:, 1024:2048] = final_b[rows, 0:1024]
        gq[:, 2048:] = cross_b[...]
        go[...] = cross_a[...]

    @pl.when(core == 1)
    def _():
        gq[:, 0:1024] = cross_a[...]
        gq[:, 1024:2048] = cross_b[...]
        gq[:, 2048:] = final_b[rows, 0:1024]
        go[...] = final_a[rows, :]


def local(tokens, masked, mask_embed, w_qkv, w_out, cotangent):
    natural = one_hot(padded_order(), 384)
    piece, middle = one_hot(piece_order(), 288), one_hot(middle_order(), 576)
    orders = [natural, natural.T, piece, piece.T, middle, middle.T]
    near_bias = np.where(near(), 0.0, -np.inf).astype(np.float32)
    vmem, hbm = pl.BlockSpec(memory_space=pltpu.VMEM), pl.BlockSpec(memory_space=pl.ANY)
    jobs = []
    for _, _, wide, order in JOBS:
        for stage in (1, 2):
            left = extent(without(order, stage))
            jobs.append(pltpu.VMEM((3, *left, 16, wide), BF16))
            jobs.append(pltpu.VMEM((*left, 16, wide), BF16))
        jobs.append(pltpu.VMEM((3, 16, wide), BF16))
    block_out, grad_tokens, gq, go, gm = pl.pallas_call(
        block_kernel,
        out_shape=(
            jax.ShapeDtypeStruct(tokens.shape, BF16),
            jax.ShapeDtypeStruct(tokens.shape, BF16),
            jax.ShapeDtypeStruct((8, 3072), F32),
            jax.ShapeDtypeStruct((8, 1024), F32),
            jax.ShapeDtypeStruct((8, 128), F32),
        ),
        in_specs=[vmem, vmem, vmem, hbm, hbm, vmem, vmem] + [vmem] * 6,
        out_specs=(vmem,) * 5,
        scratch_shapes=[
            pltpu.VMEM((1024, 3072), BF16),
            pltpu.VMEM((1024, 1024), BF16),
            pltpu.VMEM((24, 16, 1024), BF16),
            pltpu.VMEM((288, 1024), BF16),
            pltpu.VMEM((288, 1024), BF16),
            pltpu.VMEM((96, 768), F32),
            pltpu.VMEM((288, 128), F32),
            pltpu.VMEM((288, 1024), BF16),
            pltpu.VMEM((288, 3072), BF16),
            pltpu.VMEM((288, 1024), BF16),
            pltpu.VMEM((576, 1024), BF16),
            pltpu.VMEM((1152, 1024), BF16),
            pltpu.VMEM((288, 1024), BF16),
            pltpu.VMEM((288, 1024), BF16),
            pltpu.VMEM((1152, 2048), BF16),
            pltpu.VMEM((2, 1152, 512), F32),
            pltpu.VMEM((4, 2, 288, 512), BF16),
            pltpu.VMEM((4, 2, 288, 512), BF16),
            pltpu.VMEM((4, 288, 512), BF16),
            pltpu.VMEM((4, 288, 512), BF16),
            pltpu.VMEM((2, 288, 512), F32),
            pltpu.VMEM((2, 4, 2, 2, 4, 16, 1152), BF16),
            pltpu.VMEM((4, 2, 2, 4, 16, 1024), BF16),
            pltpu.VMEM((4, 2, 2, 4, 16, 1152), BF16),
            *jobs,
            pltpu.VMEM((16, 1024), F32),
            pltpu.VMEM((16, 1152), F32),
            pltpu.VMEM((8, 1024), F32),
            pltpu.VMEM((8, 1024), F32),
            pltpu.SemaphoreType.DMA((2,)),
            pltpu.SemaphoreType.DMA((72,)),
            pltpu.SemaphoreType.DMA((72,)),
        ],
        compiler_params=pltpu.CompilerParams(
            collective_id=1, has_side_effects=True, vmem_limit_bytes=62 * 1024 * 1024
        ),
        name="attention_block",
    )(
        tokens, masked, mask_embed[None], w_qkv, w_out, cotangent, jnp.asarray(near_bias),
        *[jnp.asarray(order, BF16) for order in orders],
    )
    return (block_out, grad_tokens, gq, go, gm[:, 0])


def solution(mesh):
    placed = (
        P(None, "lat", "lon", None),
        P("lat", "lon", None),
        P(),
        P(),
        P(),
        P(None, "lat", "lon", None),
    )
    return jax.shard_map(
        local,
        mesh=mesh,
        in_specs=placed,
        out_specs=(
            P(None, "lat", "lon", None),
            P(None, "lat", "lon", None),
            P(("lat", "lon"), None),
            P(("lat", "lon"), None),
            P(("lat", "lon")),
        ),
        check_vma=False,
    )
```

```python
import math

import jax
import jax.numpy as jnp
import numpy as np
from jax import lax
from jax.experimental import pallas as pl
from jax.experimental.pallas import tpu as pltpu
from jax.sharding import PartitionSpec as P

HEADS = 16
MESH = pl.DeviceIdType.MESH
BF16 = jnp.bfloat16
F32 = jnp.float32
EVERY = slice(None)


JOBS = (
    (0, 0, 512, "zyx"),
    (0, 512, 512, "yzx"),
    (1, 0, 256, "zyx"),
    (1, 256, 256, "yzx"),
    (1, 512, 128, "zyx"),
    (1, 640, 128, "yzx"),
    (1, 768, 128, "xzy"),
    (1, 896, 128, "yxz"),
    (1, 1024, 128, "zyx"),
)
OF_QUAD = ((2,), (3,), (4, 5), (6, 7))


def piece_order():
    column, row, lev = np.meshgrid(np.arange(12), np.arange(6), np.arange(2), indexing="ij")
    top = (column * 24 + row * 2 + lev).reshape(-1)
    return np.concatenate([top, top + 12])


def middle_order():
    column, row, lev = np.meshgrid(np.arange(12), np.arange(24), np.arange(2), indexing="ij")
    north = column * 12 + row * 2 + lev
    inside = 144 + column * 24 + (row - 6) * 2 + lev
    south = 432 + column * 12 + (row - 18) * 2 + lev
    return np.where(row < 6, north, np.where(row < 18, inside, south)).reshape(-1)


def given_order():
    column, row, lev = np.meshgrid(np.arange(12), np.arange(12), np.arange(2), indexing="ij")
    return (row * 24 + column * 2 + lev).reshape(-1)


def one_hot(order, size):
    return (order[:, None] == np.arange(size)[None, :]).astype(np.float32)


def near():
    query = np.arange(96)
    key = np.arange(768)
    row, column = query % 24 // 2, query // 24
    krow, kcolumn = key % 48 // 2, key // 48
    allowed = (krow[None] >= row[:, None]) & (krow[None] <= row[:, None] + 11)
    return allowed & (kcolumn[None] >= column[:, None]) & (kcolumn[None] <= column[:, None] + 11)


def dot(a, b):
    return jnp.dot(a, b, preferred_element_type=F32)


def dot_nt(a, b):
    return lax.dot_general(a, b, (((1,), (1,)), ((), ())), preferred_element_type=F32)


def dot_tn(a, b):
    return lax.dot_general(a, b, (((0,), (0,)), ((), ())), preferred_element_type=F32)


def without(axes, count):
    return [axis for axis in "zxy" if axis not in axes[:count]]


def extent(axes):
    return tuple(size for axis in axes for size in ((2, 2) if axis == "x" else (4,)))


def index_of(axes, chosen, at):
    out = []
    for axis in axes:
        if axis == "x":
            out += [lax.rem(at, 2), lax.div(at, 2)] if chosen == "x" else [EVERY, EVERY]
        else:
            out += [at] if axis == chosen else [EVERY]
    return tuple(out)


def block_kernel(
    tokens, masked, place, embed, w_qkv_hbm, w_out_hbm, cotangent, near_bias,
    from_given, to_given, to_piece, from_piece, to_middle, from_middle,
    block_out, grad_tokens, gq, go, gm,
    w_qkv, w_out, xm, g, bias, hits, ctx, dqkv,
    pieces, stacked, ext, q, d, kv, acc, side_out, side_in, piece_out, piece_in, own_kv,
    total, made_a, made_b, got_a, got_b, *rest,
):
    scratch = [rest[5 * i : 5 * i + 5] for i in range(len(JOBS))]
    final_a, final_b, cross_a, cross_b, load, send, recv = rest[5 * len(JOBS) :]
    lat, lon = lax.axis_index("lat"), lax.axis_index("lon")
    z, xl = lax.div(lat, 2), lax.rem(lat, 2)
    xh, y, core = lax.div(lon, 8), lax.rem(lax.div(lon, 2), 4), lax.rem(lon, 2)
    x = xh * 2 + xl
    mine = {"x": x, "y": y, "z": z}

    def device(axis, by):
        zz, yy, xx = z, y, x
        if axis == "z":
            zz = lax.rem(z + by, 4)
        elif axis == "y":
            yy = lax.rem(y + by, 4)
        else:
            xx = lax.rem(x + by, 4)
        return (zz * 2 + lax.rem(xx, 2), lax.div(xx, 2) * 8 + yy * 2 + core)

    partner = (lat, lon + 1 - 2 * core)
    north, south = (lax.rem(lat + 7, 8), lon), (lax.rem(lat + 1, 8), lon)
    west, east = (lat, lax.rem(lon + 15, 16)), (lat, lax.rem(lon + 1, 16))

    barrier = pltpu.get_barrier_semaphore()
    greeted = [north, south, west, east, partner]
    greeted += [device(axis, by) for axis in "xyz" for by in (1, 2, 3)]
    for other in greeted:
        pl.semaphore_signal(barrier, inc=1, device_id=other, device_id_type=MESH)

    loads = (
        pltpu.make_async_copy(w_qkv_hbm, w_qkv, load.at[0]),
        pltpu.make_async_copy(w_out_hbm, w_out, load.at[1]),
    )
    for copy in loads:
        copy.start()

    found = jnp.where(masked[0] == place[...], 1.0, 0.0)
    hit = jnp.max(found, axis=-1, keepdims=True) > 0.5
    hits[...] = jnp.where(hit, 1.0, 0.0) + jnp.zeros((288, 128), F32)
    own_tokens = dot(from_given[...], tokens[...].reshape(288, 1024))
    mask_row = jnp.concatenate([embed[i : i + 1, :] for i in range(8)], axis=1).astype(F32)
    xm[...] = jnp.where(hit, mask_row, own_tokens).astype(BF16)

    pieces[...] = dot(to_piece[...], xm[...]).astype(BF16)
    stacked[144:432, :] = xm[...]
    pl.semaphore_wait(barrier, len(greeted))

    def copy_to(source, target, sem, other):
        return pltpu.make_async_remote_copy(
            src_ref=source,
            dst_ref=target,
            send_sem=send.at[sem],
            recv_sem=recv.at[sem],
            device_id=other,
            device_id_type=MESH,
        )

    def part(start, rows):
        return pl.ds(start, rows)

    def tile(t, start=0):
        return pl.ds(pl.multiple_of(t * 256 + start, 256), 256)

    first = (
        copy_to(pieces.at[part(0, 144)], stacked.at[part(432, 144)], 0, north),
        copy_to(pieces.at[part(144, 144)], stacked.at[part(0, 144)], 1, south),
    )
    for copy in first:
        copy.start()

    g[...] = dot(from_given[...], cotangent[...].reshape(288, 1024)).astype(BF16)
    key_row = lax.broadcasted_iota(jnp.int32, (1, 768), 1)
    key_row = lax.div(lax.rem(key_row, 48), 2) + lat * 12 - 6
    bias[...] = jnp.where((key_row >= 0) & (key_row < 96), near_bias[...], -jnp.inf)
    for copy in loads:
        copy.wait()

    @pl.loop(0, 4)
    def _(t):
        cols = tile(t)
        q[:, cols] = dot(xm[...], w_qkv[:, cols]).astype(BF16)
        d[:, cols] = dot_nt(g[...], w_out[cols, :]).astype(BF16)

    for copy in first:
        copy.wait()
    ext[288:864, :] = dot(to_middle[...], stacked[...]).astype(BF16)
    second = (
        copy_to(ext.at[part(288, 288)], ext.at[part(864, 288)], 2, west),
        copy_to(ext.at[part(576, 288)], ext.at[part(0, 288)], 3, east),
    )
    for copy in second:
        copy.start()

    def project(start, rows):
        @pl.loop(0, 8)
        def _(t):
            kv[start : start + rows, tile(t)] = dot(
                ext[start : start + rows, :], w_qkv[:, tile(t, 1024)]
            ).astype(BF16)

    project(288, 576)
    for copy in second:
        copy.wait()
    project(0, 288)
    project(864, 288)

    lane_head = lax.div(lax.broadcasted_iota(jnp.int32, (96, 256), 1), 64)
    picks = [lane_head == h for h in range(4)]
    nothing = jnp.zeros((96, 256), BF16)
    factor = math.log2(math.e) / 8.0

    def side_copies(t):
        return (
            copy_to(side_out.at[lax.rem(t, 2), 0], side_in.at[t, 1], 4 + 4 * t, west),
            copy_to(side_out.at[lax.rem(t, 2), 1], side_in.at[t, 0], 5 + 4 * t, east),
        )

    def piece_copies(t):
        out = piece_out.at[lax.rem(t, 2)]
        return (
            copy_to(out.at[part(0, 144)], piece_in.at[t, part(144, 144)], 6 + 4 * t, north),
            copy_to(out.at[part(144, 144)], piece_in.at[t, part(0, 144)], 7 + 4 * t, south),
        )

    def joined(out):
        total = jnp.where(picks[0], out[0:96], 0.0)
        for h in range(1, 4):
            total = jnp.where(picks[h], out[h * 96 : h * 96 + 96], total)
        return total

    def quad(t):
        cols, vcols = tile(t), tile(t, 1024)
        slot = lax.rem(t, 2)
        acc[slot] = jnp.zeros((1152, 512), F32)

        @pl.loop(0, 3)
        def _(j):
            rows = pl.ds(pl.multiple_of(j * 96, 96), 96)
            keys = pl.ds(pl.multiple_of(j * 192, 192), 768)
            qj, dj = q[rows, cols], d[rows, cols]
            qm = jnp.concatenate([jnp.where(pick, qj, nothing) for pick in picks], axis=0)
            dm = jnp.concatenate([jnp.where(pick, dj, nothing) for pick in picks], axis=0)
            kw, vw = kv[keys, cols], kv[keys, vcols]
            s = dot_nt(qm, kw).reshape(4, 96, 768) + bias[...][None]
            top = jnp.max(s, axis=-1, keepdims=True)
            e = jnp.exp2((s - top) * factor)
            p = e * (1.0 / jnp.sum(e, axis=-1, keepdims=True))
            p = p.reshape(384, 768)
            pb = p.astype(BF16)
            out = dot(pb, vw)
            delta = jnp.sum(out * dm.astype(F32), axis=-1, keepdims=True)
            ctx[rows, cols] = joined(out).astype(BF16)
            ds = (p * (dot_nt(dm, vw) - delta)).astype(BF16)
            dqkv[rows, cols] = (joined(dot(ds, kw)) * 0.125).astype(BF16)
            acc[slot, keys, 0:256] += dot_tn(ds, qm)
            acc[slot, keys, 256:512] += dot_tn(pb, dm)

        side_out[slot, 0] = acc[slot, 0:288, :].astype(BF16)
        side_out[slot, 1] = acc[slot, 864:1152, :].astype(BF16)
        for copy in side_copies(t):
            copy.start()

    def sides_back(t):
        for copy in side_copies(t):
            copy.wait()
        slot = lax.rem(t, 2)
        mid = acc[slot, 288:864, :] + side_in[t].astype(F32).reshape(576, 512)
        high = mid.astype(BF16)
        low = (mid - high.astype(F32)).astype(BF16)
        parts = dot(from_middle[...], high)
        piece_out[slot, 0:144, :] = parts[0:144].astype(BF16)
        piece_out[slot, 144:288, :] = parts[432:576].astype(BF16)
        for copy in piece_copies(t):
            copy.start()
        own_kv[slot] = parts[144:432] + dot(from_middle[144:432, :], low)

    def pieces_back(t):
        for copy in piece_copies(t):
            copy.wait()
        both = own_kv[lax.rem(t, 2)] + dot(from_piece[...], piece_in[t])
        dk, dv = (both[:, 0:256] * 0.125).astype(BF16), both[:, 256:512].astype(BF16)
        dqkv[:, tile(t, 1024)] = dk
        dqkv[:, tile(t, 2048)] = dv
        for c in range(4):
            rows = slice(256 * c, 256 * c + 256)
            more = dot_nt(dk, w_qkv[rows, tile(t, 1024)]) + dot_nt(dv, w_qkv[rows, tile(t, 2048)])
            total[:, rows] += more

    total[...] = g[...].astype(F32)

    @pl.loop(0, 4)
    def _(t):
        quad(t)

        @pl.when(t >= 1)
        def _():
            sides_back(t - 1)

        @pl.when(t >= 2)
        def _():
            pieces_back(t - 2)

    mades, gots = (made_a, made_b), (got_a, got_b)

    def columns(job):
        return pl.ds(JOBS[job][1], JOBS[job][2])

    def make_a(half):
        def store(t, value):
            made_a[half, t] = value.astype(BF16).reshape(2, 2, 4, 16, 1024)

        @pl.when(half == 0)
        def _():
            @pl.loop(0, 4)
            def _(t):
                store(t, dot_tn(xm[:, tile(t)], dqkv[:, 0:1024]))

        @pl.when(half == 1)
        def _():
            @pl.loop(0, 4)
            def _(t):
                store(t, dot_tn(ctx[:, tile(t)], g[...]))

    def make_b(n, half):
        cols = pl.ds(pl.multiple_of(half * 1024 + 1024 + 256 * n, 256), 256)

        @pl.loop(0, 4)
        def _(t):
            value = dot_tn(xm[:, tile(t)], dqkv[:, cols]).astype(BF16)
            made_b[half, t, :, :, :, :, 256 * n : 256 * n + 256] = value.reshape(2, 2, 4, 16, 256)

    def exchange(job):
        where = (EVERY,) * 5 + (columns(job),)
        phase = JOBS[job][0]
        return copy_to(mades[phase].at[(1 - core, *where)], gots[phase].at[where], 20 + job, partner)

    def exchanged(job):
        exchange(job).wait()
        cols, made, got = columns(job), mades[JOBS[job][0]], gots[JOBS[job][0]]

        @pl.loop(0, 4)
        def _(a):
            for b in range(2):
                for c in range(2):
                    both = made[core, a, b, c, :, :, cols].astype(F32)
                    both = both + got[a, b, c, :, :, cols].astype(F32)
                    made[core, a, b, c, :, :, cols] = both.astype(BF16)

        start(job, 0)

    def held(job, stage, at):
        order = JOBS[job][3]
        here = index_of(without(order, stage), order[stage], at)
        if stage == 0:
            return mades[JOBS[job][0]], (core, *here, EVERY, columns(job))
        return scratch[job][2 * stage - 1], (*here, EVERY, EVERY)

    def stage_copies(job, stage):
        axis = JOBS[job][3][stage]
        copies = []
        for by in (2, 1, 3):
            ref, where = held(job, stage, lax.rem(mine[axis] + by, 4))
            target = scratch[job][2 * stage].at[by - 1]
            sem = 20 + len(JOBS) + job * 9 + stage * 3 + by - 1
            copies.append(copy_to(ref.at[where], target, sem, device(axis, by)))
        return copies

    def start(job, stage):
        for copy in stage_copies(job, stage):
            copy.start()

    def reduced(job, stage):
        for copy in stage_copies(job, stage):
            copy.wait()
        ref, where = held(job, stage, mine[JOBS[job][3][stage]])
        piece = ref[where].astype(F32)
        for slot in range(3):
            piece = piece + scratch[job][2 * stage][slot].astype(F32)
        if stage < 2:
            scratch[job][2 * stage + 1][...] = piece.astype(BF16)
            start(job, stage + 1)
        else:
            final = (final_a, final_b)[JOBS[job][0]]
            final[:, columns(job)] = piece * (1.0 / 192.0)

    def swap(phase):
        rows = pl.ds(pl.multiple_of((1 - core) * 8, 8), 8)
        source = (final_a, final_b)[phase].at[rows, pl.ds(0, 1024)]
        return copy_to(source, (cross_a, cross_b)[phase], 20 + 10 * len(JOBS) + phase, partner)

    def group(n):
        make_b(n, 1 - core)
        for job in OF_QUAD[n]:
            exchange(job).start()
        make_b(n, core)

    sides_back(3)
    make_a(1 - core)
    for job in (0, 1):
        exchange(job).start()
    group(0)
    make_a(core)
    for job in (0, 1):
        exchanged(job)
    exchanged(2)
    group(1)
    exchanged(3)

    @pl.loop(0, 4)
    def _(t):
        cols = tile(t)
        value = xm[:, cols].astype(F32) + dot(ctx[...], w_out[:, cols])
        value = dot(to_given[...], value.astype(BF16)).astype(BF16)
        block_out[:, :, :, cols] = value.reshape(12, 12, 2, 256)
        total[:, cols] += dot_nt(dqkv[:, 0:1024], w_qkv[cols, 0:1024])

    pieces_back(2)
    group(2)
    for job in (0, 1, 2):
        reduced(job, 0)
    for job in (4, 5):
        exchanged(job)
    reduced(3, 0)
    pieces_back(3)
    group(3)
    for job in (6, 7):
        exchanged(job)

    @pl.loop(0, 4)
    def _(t):
        cols = tile(t)
        hit = hits[...]
        value = total[:, cols]
        high = value.astype(BF16)
        low = (value - high.astype(F32)).astype(BF16)
        column = dot_tn(high, hit.astype(BF16)) + dot_tn(low, hit.astype(BF16))
        column = column.astype(BF16).reshape(2, 2, 4, 16, 128)
        made_b[0, t, :, :, :, :, 1024:1152] = column
        made_b[1, t, :, :, :, :, 1024:1152] = column

    exchange(8).start()
    for job in (0, 1, 2, 3):
        reduced(job, 1)
    exchanged(8)
    for job in (4, 5):
        reduced(job, 0)

    @pl.loop(0, 4)
    def _(t):
        cols = tile(t)
        hit = hits[...]
        value = total[:, cols]
        kept = jnp.where(jnp.concatenate([hit, hit], axis=1) > 0.5, 0.0, value).astype(BF16)
        kept = dot(to_given[...], kept).astype(BF16)
        grad_tokens[:, :, :, cols] = kept.reshape(12, 12, 2, 256)

    for job in (6, 7, 8):
        reduced(job, 0)
    for job in (0, 1):
        reduced(job, 2)
    swap(0).start()
    for job in (4, 5, 6, 7, 8):
        reduced(job, 1)
    for job in (2, 3, 4, 5, 6, 7, 8):
        reduced(job, 2)
    swap(1).start()
    swap(0).wait()
    swap(1).wait()
    rows = pl.ds(pl.multiple_of(core * 8, 8), 8)
    gm[...] = final_b[rows, 1024:]

    @pl.when(core == 0)
    def _():
        gq[:, 0:1024] = final_a[rows, :]
        gq[:, 1024:2048] = final_b[rows, 0:1024]
        gq[:, 2048:] = cross_b[...]
        go[...] = cross_a[...]

    @pl.when(core == 1)
    def _():
        gq[:, 0:1024] = cross_a[...]
        gq[:, 1024:2048] = cross_b[...]
        gq[:, 2048:] = final_b[rows, 0:1024]
        go[...] = final_a[rows, :]


def hand_out_kernel(block_out, grad_tokens, gq, go, gm, *targets):
    for source, target in zip((block_out, grad_tokens, gq, go), targets):
        target[...] = source[...]
    row = lax.broadcasted_iota(jnp.int32, (8, 128), 0)
    lane = lax.broadcasted_iota(jnp.int32, (8, 128), 1)
    targets[4][...] = jnp.sum(jnp.where(row == lane, gm[...], 0.0), axis=0)[0:8]


def local(tokens, masked, mask_embed, w_qkv, w_out, cotangent):
    given = one_hot(given_order(), 288)
    piece, middle = one_hot(piece_order(), 288), one_hot(middle_order(), 576)
    orders = [given, given.T, piece, piece.T, middle, middle.T]
    row, lev = np.arange(288) % 24 // 2, np.arange(288) % 2
    place = lev * 144 + row * 12 + np.arange(288) // 24
    place = np.broadcast_to(place[:, None], (288, 144)).astype(np.int32)
    near_bias = np.where(near(), 0.0, -np.inf).astype(np.float32)
    vmem, hbm = pl.BlockSpec(memory_space=pltpu.VMEM), pl.BlockSpec(memory_space=pl.ANY)
    jobs = []
    for _, _, wide, order in JOBS:
        for stage in (1, 2):
            left = extent(without(order, stage))
            jobs.append(pltpu.VMEM((3, *left, 16, wide), BF16))
            jobs.append(pltpu.VMEM((*left, 16, wide), BF16))
        jobs.append(pltpu.VMEM((3, 16, wide), BF16))
    block_out, grad_tokens, gq, go, gm = pl.pallas_call(
        block_kernel,
        out_shape=(
            jax.ShapeDtypeStruct((12, 12, 2, 1024), BF16),
            jax.ShapeDtypeStruct((12, 12, 2, 1024), BF16),
            jax.ShapeDtypeStruct((8, 3072), F32),
            jax.ShapeDtypeStruct((8, 1024), F32),
            jax.ShapeDtypeStruct((8, 128), F32),
        ),
        in_specs=[vmem, vmem, vmem, vmem, hbm, hbm, vmem, vmem] + [vmem] * 6,
        out_specs=(vmem,) * 5,
        scratch_shapes=[
            pltpu.VMEM((1024, 3072), BF16),
            pltpu.VMEM((1024, 1024), BF16),
            pltpu.VMEM((288, 1024), BF16),
            pltpu.VMEM((288, 1024), BF16),
            pltpu.VMEM((96, 768), F32),
            pltpu.VMEM((288, 128), F32),
            pltpu.VMEM((288, 1024), BF16),
            pltpu.VMEM((288, 3072), BF16),
            pltpu.VMEM((288, 1024), BF16),
            pltpu.VMEM((576, 1024), BF16),
            pltpu.VMEM((1152, 1024), BF16),
            pltpu.VMEM((288, 1024), BF16),
            pltpu.VMEM((288, 1024), BF16),
            pltpu.VMEM((1152, 2048), BF16),
            pltpu.VMEM((2, 1152, 512), F32),
            pltpu.VMEM((2, 2, 288, 512), BF16),
            pltpu.VMEM((4, 2, 288, 512), BF16),
            pltpu.VMEM((2, 288, 512), BF16),
            pltpu.VMEM((4, 288, 512), BF16),
            pltpu.VMEM((2, 288, 512), F32),
            pltpu.VMEM((288, 1024), F32),
            pltpu.VMEM((2, 4, 2, 2, 4, 16, 1024), BF16),
            pltpu.VMEM((2, 4, 2, 2, 4, 16, 1152), BF16),
            pltpu.VMEM((4, 2, 2, 4, 16, 1024), BF16),
            pltpu.VMEM((4, 2, 2, 4, 16, 1152), BF16),
            *jobs,
            pltpu.VMEM((16, 1024), F32),
            pltpu.VMEM((16, 1152), F32),
            pltpu.VMEM((8, 1024), F32),
            pltpu.VMEM((8, 1024), F32),
            pltpu.SemaphoreType.DMA((2,)),
            pltpu.SemaphoreType.DMA((22 + 10 * len(JOBS),)),
            pltpu.SemaphoreType.DMA((22 + 10 * len(JOBS),)),
        ],
        compiler_params=pltpu.CompilerParams(
            collective_id=1, has_side_effects=True, vmem_limit_bytes=62 * 1024 * 1024
        ),
        name="attention_block",
    )(
        tokens.transpose(1, 2, 0, 3), masked, jnp.asarray(place), mask_embed.reshape(8, 128), w_qkv, w_out,
        cotangent.transpose(1, 2, 0, 3), jnp.asarray(near_bias),
        *[jnp.asarray(order, BF16) for order in orders],
    )
    block_out, grad_tokens, gq, go, gm = pl.pallas_call(
        hand_out_kernel,
        out_shape=(
            jax.ShapeDtypeStruct((12, 12, 2, 1024), BF16),
            jax.ShapeDtypeStruct((12, 12, 2, 1024), BF16),
            jax.ShapeDtypeStruct((8, 3072), F32),
            jax.ShapeDtypeStruct((8, 1024), F32),
            jax.ShapeDtypeStruct((8,), F32),
        ),
        in_specs=[vmem] * 5,
        out_specs=(vmem,) * 5,
        name="hand_out",
    )(block_out, grad_tokens, gq, go, gm)
    block_out, grad_tokens = block_out.transpose(2, 0, 1, 3), grad_tokens.transpose(2, 0, 1, 3)
    return (block_out, grad_tokens, gq, go, gm)


def solution(mesh):
    placed = (
        P(None, "lat", "lon", None),
        P("lat", "lon", None),
        P(),
        P(),
        P(),
        P(None, "lat", "lon", None),
    )
    return jax.shard_map(
        local,
        mesh=mesh,
        in_specs=placed,
        out_specs=(
            P(None, "lat", "lon", None),
            P(None, "lat", "lon", None),
            P(("lat", "lon"), None),
            P(("lat", "lon"), None),
            P(("lat", "lon")),
        ),
        check_vma=False,
    )
```

```python
import math

import jax
import jax.numpy as jnp
import numpy as np
from jax import lax
from jax.experimental import pallas as pl
from jax.experimental.pallas import tpu as pltpu
from jax.sharding import PartitionSpec as P

HEADS = 16
MESH = pl.DeviceIdType.MESH
BF16 = jnp.bfloat16
F32 = jnp.float32
EVERY = slice(None)


JOBS = (
    (0, 0, 384, "zyx"),
    (0, 384, 384, "yxz"),
    (0, 768, 256, "xzy"),
    (1, 0, 256, "xzy"),
    (1, 256, 256, "zyx"),
    (1, 512, 256, "yxz"),
    (1, 768, 128, "xzy"),
    (1, 896, 128, "yxz"),
    (1, 1024, 128, "zyx"),
)
OF_QUAD = ((3,), (4,), (5,), (6, 7))


def piece_order():
    column, row, lev = np.meshgrid(np.arange(12), np.arange(6), np.arange(2), indexing="ij")
    top = (column * 24 + row * 2 + lev).reshape(-1)
    return np.concatenate([top, top + 12])


def middle_order():
    column, row, lev = np.meshgrid(np.arange(12), np.arange(24), np.arange(2), indexing="ij")
    north = column * 12 + row * 2 + lev
    inside = 144 + column * 24 + (row - 6) * 2 + lev
    south = 432 + column * 12 + (row - 18) * 2 + lev
    return np.where(row < 6, north, np.where(row < 18, inside, south)).reshape(-1)


def given_order():
    column, row, lev = np.meshgrid(np.arange(12), np.arange(12), np.arange(2), indexing="ij")
    return (row * 24 + column * 2 + lev).reshape(-1)


def one_hot(order, size):
    return (order[:, None] == np.arange(size)[None, :]).astype(np.float32)


def near(shift):
    inner, outer = np.arange(96), np.arange(768)
    row = outer[None] % 48 // 2 - inner[:, None] % 24 // 2 - shift
    column = outer[None] // 48 - inner[:, None] // 24 - shift
    allowed = (row >= 0) & (row <= 11) & (column >= 0) & (column <= 11)
    return np.where(allowed, 0.0, -np.inf).astype(np.float32)


def dot(a, b):
    return jnp.dot(a, b, preferred_element_type=F32)


def dot_nt(a, b):
    return lax.dot_general(a, b, (((1,), (1,)), ((), ())), preferred_element_type=F32)


def dot_tn(a, b):
    return lax.dot_general(a, b, (((0,), (0,)), ((), ())), preferred_element_type=F32)


def without(axes, count):
    return [axis for axis in "zxy" if axis not in axes[:count]]


def extent(axes):
    return tuple(size for axis in axes for size in ((2, 2) if axis == "x" else (4,)))


def index_of(axes, chosen, at):
    out = []
    for axis in axes:
        if axis == "x":
            out += [lax.rem(at, 2), lax.div(at, 2)] if chosen == "x" else [EVERY, EVERY]
        else:
            out += [at] if axis == chosen else [EVERY]
    return tuple(out)


def block_kernel(
    tokens, masked, place, embed, w_qkv_hbm, w_out_hbm, cotangent_hbm, near_keys_hbm, near_queries_hbm,
    from_given, to_given, to_piece, to_middle_hbm,
    block_out, grad_tokens, gq, go, gm,
    w_qkv, w_out, cotangent, near_keys, near_queries, to_middle, xm, g, key_bias, query_bias, hits, ctx, dqkv,
    pieces, stacked, ext, g_pieces, g_stacked, g_ext,
    stats, stat_pieces, stat_stacked, stat_ext, stat_rows, q, d, kv, own_kv, ext_q, ext_d,
    total, made_a, made_b, got_a, got_b, *rest,
):
    scratch = [rest[5 * i : 5 * i + 5] for i in range(len(JOBS))]
    final_a, final_b, cross_a, cross_b, load, send, recv = rest[5 * len(JOBS) :]
    lat, lon = lax.axis_index("lat"), lax.axis_index("lon")
    z, xl = lax.div(lat, 2), lax.rem(lat, 2)
    xh, y, core = lax.div(lon, 8), lax.rem(lax.div(lon, 2), 4), lax.rem(lon, 2)
    x = xh * 2 + xl
    mine = {"x": x, "y": y, "z": z}

    def device(axis, by):
        zz, yy, xx = z, y, x
        if axis == "z":
            zz = lax.rem(z + by, 4)
        elif axis == "y":
            yy = lax.rem(y + by, 4)
        else:
            xx = lax.rem(x + by, 4)
        return (zz * 2 + lax.rem(xx, 2), lax.div(xx, 2) * 8 + yy * 2 + core)

    partner = (lat, lon + 1 - 2 * core)
    north, south = (lax.rem(lat + 7, 8), lon), (lax.rem(lat + 1, 8), lon)
    west, east = (lat, lax.rem(lon + 15, 16)), (lat, lax.rem(lon + 1, 16))

    barrier = pltpu.get_barrier_semaphore()
    greeted = [north, south, west, east, partner]
    greeted += [device(axis, by) for axis in "xyz" for by in (1, 2, 3)]
    for other in greeted:
        pl.semaphore_signal(barrier, inc=1, device_id=other, device_id_type=MESH)

    loaded = (
        (cotangent_hbm, cotangent),
        (near_keys_hbm, near_keys),
        (near_queries_hbm, near_queries),
        (to_middle_hbm, to_middle),
        (w_qkv_hbm, w_qkv),
        (w_out_hbm, w_out),
    )
    loads = [pltpu.make_async_copy(*pair, load.at[i]) for i, pair in enumerate(loaded)]
    for copy in loads:
        copy.start()

    found = jnp.where(masked[0] == place[...], 1.0, 0.0)
    hit = jnp.max(found, axis=-1, keepdims=True) > 0.5
    hits[...] = jnp.where(hit, 1.0, 0.0) + jnp.zeros((288, 128), F32)
    own_tokens = dot(from_given[...], tokens[...].reshape(288, 1024))
    mask_row = jnp.concatenate([embed[i : i + 1, :] for i in range(8)], axis=1).astype(F32)
    xm[...] = jnp.where(hit, mask_row, own_tokens).astype(BF16)

    pieces[...] = dot(to_piece[...], xm[...]).astype(BF16)
    stacked[144:432, :] = xm[...]
    pl.semaphore_wait(barrier, len(greeted))

    def copy_to(source, target, sem, other):
        return pltpu.make_async_remote_copy(
            src_ref=source,
            dst_ref=target,
            send_sem=send.at[sem],
            recv_sem=recv.at[sem],
            device_id=other,
            device_id_type=MESH,
        )

    def part(start, rows):
        return pl.ds(start, rows)

    def tile(t, start=0):
        return pl.ds(pl.multiple_of(t * 256 + start, 256), 256)

    def to_neighbours(source, target, sem):
        return (
            copy_to(source.at[part(0, 144)], target.at[part(432, 144)], sem, north),
            copy_to(source.at[part(144, 144)], target.at[part(0, 144)], sem + 1, south),
        )

    def to_sides(whole, sem):
        return (
            copy_to(whole.at[part(288, 288)], whole.at[part(864, 288)], sem, west),
            copy_to(whole.at[part(576, 288)], whole.at[part(0, 288)], sem + 1, east),
        )

    def begin(copies):
        for copy in copies:
            copy.start()

    def finish(copies):
        for copy in copies:
            copy.wait()

    def reordered(matrix, value):
        high = value.astype(BF16)
        rest_of = value - high.astype(F32)
        middle = rest_of.astype(BF16)
        low = (rest_of - middle.astype(F32)).astype(BF16)
        return (dot(matrix, high) + dot(matrix, middle)) + dot(matrix, low)

    rows_moved = to_neighbours(pieces, stacked, 0)
    sides_moved = to_sides(ext, 2)
    g_rows_moved = to_neighbours(g_pieces, g_stacked, 4)
    g_sides_moved = to_sides(g_ext, 6)
    stat_rows_moved = to_neighbours(stat_pieces, stat_stacked, 8)
    stat_sides_moved = to_sides(stat_ext, 10)
    begin(rows_moved)

    finish(loads[:4])
    g[...] = dot(from_given[...], cotangent[...].reshape(288, 1024)).astype(BF16)
    g_pieces[...] = dot(to_piece[...], g[...]).astype(BF16)
    g_stacked[144:432, :] = g[...]
    total[...] = g[...].astype(F32)
    stats[...] = jnp.zeros((288, 128), F32)
    ext_row = lax.broadcasted_iota(jnp.int32, (1, 768), 1)
    ext_row = lax.div(lax.rem(ext_row, 48), 2) + lat * 12 - 6
    on_grid = (ext_row >= 0) & (ext_row < 96)
    key_bias[...] = jnp.where(on_grid, near_keys[...], -jnp.inf)
    query_bias[...] = jnp.where(on_grid, near_queries[...], -jnp.inf)
    finish(loads[4:])

    @pl.loop(0, 4)
    def _(t):
        cols = tile(t)
        q[:, cols] = dot(xm[...], w_qkv[:, cols]).astype(BF16)
        d[:, cols] = dot_nt(g[...], w_out[cols, :]).astype(BF16)
        own_kv[:, cols] = dot(xm[...], w_qkv[:, tile(t, 1024)]).astype(BF16)
        own_kv[:, tile(t, 1024)] = dot(xm[...], w_qkv[:, tile(t, 2048)]).astype(BF16)

    finish(rows_moved)
    ext[288:864, :] = dot(to_middle[...], stacked[...]).astype(BF16)
    begin(sides_moved)

    def project(start, rows):
        @pl.loop(0, 8)
        def _(t):
            kv[start : start + rows, tile(t)] = dot(
                ext[start : start + rows, :], w_qkv[:, tile(t, 1024)]
            ).astype(BF16)

    def project_queries(start, rows):
        @pl.loop(0, 4)
        def _(t):
            ext_q[start : start + rows, tile(t)] = dot(
                ext[start : start + rows, :], w_qkv[:, tile(t)]
            ).astype(BF16)

    project(288, 576)
    project_queries(288, 576)
    finish(sides_moved)
    begin(g_rows_moved)
    project(0, 288)
    project(864, 288)

    lane_head = lax.div(lax.broadcasted_iota(jnp.int32, (96, 256), 1), 64)
    picks = [lane_head == h for h in range(4)]
    nothing = jnp.zeros((96, 256), BF16)
    stat_lane = lax.broadcasted_iota(jnp.int32, (96, 128), 1)
    factor = math.log2(math.e) / 8.0

    def apart(block):
        return jnp.concatenate([jnp.where(pick, block, nothing) for pick in picks], axis=0)

    def joined(out):
        whole = jnp.where(picks[0], out[0:96], 0.0)
        for h in range(1, 4):
            whole = jnp.where(picks[h], out[h * 96 : h * 96 + 96], whole)
        return whole

    def queries(t):
        cols, vcols = tile(t), tile(t, 1024)

        @pl.loop(0, 3)
        def _(j):
            rows = pl.ds(pl.multiple_of(j * 96, 96), 96)
            keys = pl.ds(pl.multiple_of(j * 192, 192), 768)
            qm, dm = apart(q[rows, cols]), apart(d[rows, cols])
            kw, vw = kv[keys, cols], kv[keys, vcols]
            s = dot_nt(qm, kw).reshape(4, 96, 768) + key_bias[...][None]
            top = jnp.max(s, axis=-1, keepdims=True)
            e = jnp.exp2((s - top) * factor)
            share = 1.0 / jnp.sum(e, axis=-1, keepdims=True)
            p = (e * share).reshape(384, 768)
            out = dot(p.astype(BF16), vw)
            delta = jnp.sum(out * dm.astype(F32), axis=-1, keepdims=True)
            ctx[rows, cols] = joined(out).astype(BF16)
            ds = (p * (dot_nt(dm, vw) - delta)).astype(BF16)
            dqkv[rows, cols] = (joined(dot(ds, kw)) * 0.125).astype(BF16)
            kept = stats[rows, :]
            for h in range(4):
                values = (top[h], share[h], delta[h * 96 : h * 96 + 96])
                for kind, value in enumerate(values):
                    kept = jnp.where(stat_lane == t * 16 + kind * 4 + h, value, kept)
            stats[rows, :] = kept

    def keys_of(t):
        cols, vcols = tile(t), tile(t, 1024)

        @pl.loop(0, 3)
        def _(j):
            rows = pl.ds(pl.multiple_of(j * 96, 96), 96)
            seen = pl.ds(pl.multiple_of(j * 192, 192), 768)
            km, vm = apart(own_kv[rows, cols]), apart(own_kv[rows, vcols])
            qw, dw = ext_q[seen, cols], ext_d[seen, cols]
            known = stat_rows[j, 16 * t : 16 * t + 16, :]
            top, share, delta = (known[4 * i : 4 * i + 4].reshape(4, 1, 768) for i in range(3))
            s = dot_nt(km, qw).reshape(4, 96, 768) + query_bias[...][None]
            p = jnp.exp2((s - top) * factor) * share
            ds = p * (dot_nt(vm, dw).reshape(4, 96, 768) - delta)
            dk = joined(dot(ds.reshape(384, 768).astype(BF16), qw)) * 0.125
            dv = joined(dot(p.reshape(384, 768).astype(BF16), dw))
            dqkv[rows, tile(t, 1024)] = dk.astype(BF16)
            dqkv[rows, tile(t, 2048)] = dv.astype(BF16)

    def add_to_total(t):
        dk, dv = dqkv[:, tile(t, 1024)], dqkv[:, tile(t, 2048)]
        for c in range(4):
            rows = slice(256 * c, 256 * c + 256)
            more = dot_nt(dk, w_qkv[rows, tile(t, 1024)]) + dot_nt(dv, w_qkv[rows, tile(t, 2048)])
            total[:, rows] += more

    @pl.loop(0, 4)
    def _(t):
        queries(t)

        @pl.when(t == 2)
        def _():
            finish(g_rows_moved)
            g_ext[288:864, :] = dot(to_middle[...], g_stacked[...]).astype(BF16)
            begin(g_sides_moved)

    stat_pieces[...] = reordered(to_piece[...], stats[...])
    stat_stacked[144:432, :] = stats[...]
    begin(stat_rows_moved)

    mades, gots = (made_a, made_b), (got_a, got_b)

    def columns(job):
        return pl.ds(JOBS[job][1], JOBS[job][2])

    def make_a(half):
        def store(t, value):
            made_a[half, t] = value.astype(BF16).reshape(2, 2, 4, 16, 1024)

        @pl.when(half == 0)
        def _():
            @pl.loop(0, 4)
            def _(t):
                store(t, dot_tn(xm[:, tile(t)], dqkv[:, 0:1024]))

        @pl.when(half == 1)
        def _():
            @pl.loop(0, 4)
            def _(t):
                store(t, dot_tn(ctx[:, tile(t)], g[...]))

    def make_b(n, half):
        cols = pl.ds(pl.multiple_of(half * 1024 + 1024 + 256 * n, 256), 256)

        @pl.loop(0, 4)
        def _(t):
            value = dot_tn(xm[:, tile(t)], dqkv[:, cols]).astype(BF16)
            made_b[half, t, :, :, :, :, 256 * n : 256 * n + 256] = value.reshape(2, 2, 4, 16, 256)

    def exchange(job):
        where = (EVERY,) * 5 + (columns(job),)
        phase = JOBS[job][0]
        return copy_to(mades[phase].at[(1 - core, *where)], gots[phase].at[where], 12 + job, partner)

    def exchanged(job):
        exchange(job).wait()
        cols, made, got = columns(job), mades[JOBS[job][0]], gots[JOBS[job][0]]

        @pl.loop(0, 4)
        def _(a):
            for b in range(2):
                for c in range(2):
                    both = made[core, a, b, c, :, :, cols].astype(F32)
                    both = both + got[a, b, c, :, :, cols].astype(F32)
                    made[core, a, b, c, :, :, cols] = both.astype(BF16)

        start(job, 0)

    def held(job, stage, at):
        order = JOBS[job][3]
        here = index_of(without(order, stage), order[stage], at)
        if stage == 0:
            return mades[JOBS[job][0]], (core, *here, EVERY, columns(job))
        return scratch[job][2 * stage - 1], (*here, EVERY, EVERY)

    def stage_copies(job, stage):
        axis = JOBS[job][3][stage]
        copies = []
        for by in (2, 1, 3):
            ref, where = held(job, stage, lax.rem(mine[axis] + by, 4))
            target = scratch[job][2 * stage].at[by - 1]
            sem = 12 + len(JOBS) + job * 9 + stage * 3 + by - 1
            copies.append(copy_to(ref.at[where], target, sem, device(axis, by)))
        return copies

    def start(job, stage):
        for copy in stage_copies(job, stage):
            copy.start()

    def reduced(job, stage):
        for copy in stage_copies(job, stage):
            copy.wait()
        ref, where = held(job, stage, mine[JOBS[job][3][stage]])
        piece = ref[where].astype(F32)
        for slot in range(3):
            piece = piece + scratch[job][2 * stage][slot].astype(F32)
        if stage < 2:
            scratch[job][2 * stage + 1][...] = piece.astype(BF16)
            start(job, stage + 1)
        else:
            final = (final_a, final_b)[JOBS[job][0]]
            final[:, columns(job)] = piece * (1.0 / 192.0)

    def swap(phase):
        rows = pl.ds(pl.multiple_of((1 - core) * 8, 8), 8)
        source = (final_a, final_b)[phase].at[rows, pl.ds(0, 1024)]
        return copy_to(source, (cross_a, cross_b)[phase], 12 + 10 * len(JOBS) + phase, partner)

    def group(n):
        make_b(n, 1 - core)
        for job in OF_QUAD[n]:
            exchange(job).start()
        make_b(n, core)

    make_a(1 - core)
    for job in (0, 1, 2):
        exchange(job).start()

    project_queries(0, 288)
    project_queries(864, 288)
    finish(stat_rows_moved)
    stat_ext[288:864, :] = reordered(to_middle[...], stat_stacked[...])
    finish(g_sides_moved)
    begin(stat_sides_moved)
    make_a(core)
    for job in (0, 1, 2):
        exchanged(job)

    @pl.loop(0, 4)
    def _(t):
        ext_d[:, tile(t)] = dot_nt(g_ext[...], w_out[tile(t), :]).astype(BF16)

    finish(stat_sides_moved)
    for j in range(3):
        stat_rows[j] = stat_ext[192 * j : 192 * j + 768, :].T

    def advance(*steps):
        for job, stage in steps:
            reduced(job, stage)

    keys_of(0)
    group(0)
    add_to_total(0)
    exchanged(3)
    keys_of(1)
    advance((0, 0), (1, 0), (2, 0))
    group(1)
    add_to_total(1)
    exchanged(4)
    keys_of(2)
    advance((0, 1), (1, 1), (2, 1), (3, 0))
    group(2)

    @pl.loop(0, 4)
    def _(t):
        cols = tile(t)
        value = xm[:, cols].astype(F32) + dot(ctx[...], w_out[:, cols])
        value = dot(to_given[...], value.astype(BF16)).astype(BF16)
        block_out[:, :, :, cols] = value.reshape(12, 12, 2, 256)
        total[:, cols] += dot_nt(dqkv[:, 0:1024], w_qkv[cols, 0:1024])

    add_to_total(2)
    exchanged(5)
    keys_of(3)
    group(3)
    advance((3, 1), (4, 0))
    add_to_total(3)
    exchanged(6)
    exchanged(7)

    @pl.loop(0, 4)
    def _(t):
        cols = tile(t)
        hit = hits[...]
        value = total[:, cols]
        high = value.astype(BF16)
        low = (value - high.astype(F32)).astype(BF16)
        column = dot_tn(high, hit.astype(BF16)) + dot_tn(low, hit.astype(BF16))
        column = column.astype(BF16).reshape(2, 2, 4, 16, 128)
        made_b[0, t, :, :, :, :, 1024:1152] = column
        made_b[1, t, :, :, :, :, 1024:1152] = column

    exchange(8).start()
    advance((0, 2), (1, 2), (2, 2))
    swap(0).start()
    advance((4, 1), (5, 0))
    exchanged(8)

    @pl.loop(0, 4)
    def _(t):
        cols = tile(t)
        hit = hits[...]
        value = total[:, cols]
        kept = jnp.where(jnp.concatenate([hit, hit], axis=1) > 0.5, 0.0, value).astype(BF16)
        kept = dot(to_given[...], kept).astype(BF16)
        grad_tokens[:, :, :, cols] = kept.reshape(12, 12, 2, 256)

    advance((3, 2), (6, 0), (7, 0), (5, 1), (8, 0), (4, 2), (6, 1), (7, 1), (8, 1))
    advance((5, 2), (6, 2), (7, 2), (8, 2))
    swap(1).start()
    swap(0).wait()
    swap(1).wait()
    rows = pl.ds(pl.multiple_of(core * 8, 8), 8)
    gm[...] = final_b[rows, 1024:]

    @pl.when(core == 0)
    def _():
        gq[:, 0:1024] = final_a[rows, :]
        gq[:, 1024:2048] = final_b[rows, 0:1024]
        gq[:, 2048:] = cross_b[...]
        go[...] = cross_a[...]

    @pl.when(core == 1)
    def _():
        gq[:, 0:1024] = cross_a[...]
        gq[:, 1024:2048] = cross_b[...]
        gq[:, 2048:] = final_b[rows, 0:1024]
        go[...] = final_a[rows, :]


def hand_out_kernel(block_out, grad_tokens, gq, go, gm, *targets):
    for source, target in zip((block_out, grad_tokens, gq, go), targets):
        target[...] = source[...]
    row = lax.broadcasted_iota(jnp.int32, (8, 128), 0)
    lane = lax.broadcasted_iota(jnp.int32, (8, 128), 1)
    targets[4][...] = jnp.sum(jnp.where(row == lane, gm[...], 0.0), axis=0)[0:8]


def local(tokens, masked, mask_embed, w_qkv, w_out, cotangent):
    given = one_hot(given_order(), 288)
    piece, middle = one_hot(piece_order(), 288), one_hot(middle_order(), 576)
    orders = [given, given.T, piece, middle]
    row, lev = np.arange(288) % 24 // 2, np.arange(288) % 2
    place = lev * 144 + row * 12 + np.arange(288) // 24
    place = np.broadcast_to(place[:, None], (288, 144)).astype(np.int32)
    vmem, hbm = pl.BlockSpec(memory_space=pltpu.VMEM), pl.BlockSpec(memory_space=pl.ANY)
    jobs = []
    for _, _, wide, order in JOBS:
        for stage in (1, 2):
            left = extent(without(order, stage))
            jobs.append(pltpu.VMEM((3, *left, 16, wide), BF16))
            jobs.append(pltpu.VMEM((*left, 16, wide), BF16))
        jobs.append(pltpu.VMEM((3, 16, wide), BF16))
    block_out, grad_tokens, gq, go, gm = pl.pallas_call(
        block_kernel,
        out_shape=(
            jax.ShapeDtypeStruct((12, 12, 2, 1024), BF16),
            jax.ShapeDtypeStruct((12, 12, 2, 1024), BF16),
            jax.ShapeDtypeStruct((8, 3072), F32),
            jax.ShapeDtypeStruct((8, 1024), F32),
            jax.ShapeDtypeStruct((8, 128), F32),
        ),
        in_specs=[vmem] * 4 + [hbm] * 5 + [vmem] * 3 + [hbm],
        out_specs=(vmem,) * 5,
        scratch_shapes=[
            pltpu.VMEM((1024, 3072), BF16),
            pltpu.VMEM((1024, 1024), BF16),
            pltpu.VMEM((12, 12, 2, 1024), BF16),
            pltpu.VMEM((96, 768), F32),
            pltpu.VMEM((96, 768), F32),
            pltpu.VMEM((576, 576), BF16),
            pltpu.VMEM((288, 1024), BF16),
            pltpu.VMEM((288, 1024), BF16),
            pltpu.VMEM((96, 768), F32),
            pltpu.VMEM((96, 768), F32),
            pltpu.VMEM((288, 128), F32),
            pltpu.VMEM((288, 1024), BF16),
            pltpu.VMEM((288, 3072), BF16),
            pltpu.VMEM((288, 1024), BF16),
            pltpu.VMEM((576, 1024), BF16),
            pltpu.VMEM((1152, 1024), BF16),
            pltpu.VMEM((288, 1024), BF16),
            pltpu.VMEM((576, 1024), BF16),
            pltpu.VMEM((1152, 1024), BF16),
            pltpu.VMEM((288, 128), F32),
            pltpu.VMEM((288, 128), F32),
            pltpu.VMEM((576, 128), F32),
            pltpu.VMEM((1152, 128), F32),
            pltpu.VMEM((3, 128, 768), F32),
            pltpu.VMEM((288, 1024), BF16),
            pltpu.VMEM((288, 1024), BF16),
            pltpu.VMEM((1152, 2048), BF16),
            pltpu.VMEM((288, 2048), BF16),
            pltpu.VMEM((1152, 1024), BF16),
            pltpu.VMEM((1152, 1024), BF16),
            pltpu.VMEM((288, 1024), F32),
            pltpu.VMEM((2, 4, 2, 2, 4, 16, 1024), BF16),
            pltpu.VMEM((2, 4, 2, 2, 4, 16, 1152), BF16),
            pltpu.VMEM((4, 2, 2, 4, 16, 1024), BF16),
            pltpu.VMEM((4, 2, 2, 4, 16, 1152), BF16),
            *jobs,
            pltpu.VMEM((16, 1024), F32),
            pltpu.VMEM((16, 1152), F32),
            pltpu.VMEM((8, 1024), F32),
            pltpu.VMEM((8, 1024), F32),
            pltpu.SemaphoreType.DMA((6,)),
            pltpu.SemaphoreType.DMA((14 + 10 * len(JOBS),)),
            pltpu.SemaphoreType.DMA((14 + 10 * len(JOBS),)),
        ],
        compiler_params=pltpu.CompilerParams(
            collective_id=1, has_side_effects=True, vmem_limit_bytes=62 * 1024 * 1024
        ),
        name="attention_block",
    )(
        tokens.transpose(1, 2, 0, 3), masked, jnp.asarray(place), mask_embed.reshape(8, 128), w_qkv, w_out,
        cotangent.transpose(1, 2, 0, 3), jnp.asarray(near(0)), jnp.asarray(near(1)),
        *[jnp.asarray(order, BF16) for order in orders],
    )
    block_out, grad_tokens, gq, go, gm = pl.pallas_call(
        hand_out_kernel,
        out_shape=(
            jax.ShapeDtypeStruct((12, 12, 2, 1024), BF16),
            jax.ShapeDtypeStruct((12, 12, 2, 1024), BF16),
            jax.ShapeDtypeStruct((8, 3072), F32),
            jax.ShapeDtypeStruct((8, 1024), F32),
            jax.ShapeDtypeStruct((8,), F32),
        ),
        in_specs=[vmem] * 5,
        out_specs=(vmem,) * 5,
        name="hand_out",
    )(block_out, grad_tokens, gq, go, gm)
    block_out, grad_tokens = block_out.transpose(2, 0, 1, 3), grad_tokens.transpose(2, 0, 1, 3)
    return (block_out, grad_tokens, gq, go, gm)


def solution(mesh):
    placed = (
        P(None, "lat", "lon", None),
        P("lat", "lon", None),
        P(),
        P(),
        P(),
        P(None, "lat", "lon", None),
    )
    return jax.shard_map(
        local,
        mesh=mesh,
        in_specs=placed,
        out_specs=(
            P(None, "lat", "lon", None),
            P(None, "lat", "lon", None),
            P(("lat", "lon"), None),
            P(("lat", "lon"), None),
            P(("lat", "lon")),
        ),
        check_vma=False,
    )
```

```python
import math

import jax
import jax.numpy as jnp
import numpy as np
from jax import lax
from jax.experimental import pallas as pl
from jax.experimental.pallas import tpu as pltpu
from jax.sharding import PartitionSpec as P

HEADS = 16
MESH = pl.DeviceIdType.MESH
BF16 = jnp.bfloat16
F32 = jnp.float32
EVERY = slice(None)


JOBS = (
    (0, 0, 384, "zyx"),
    (0, 384, 384, "yxz"),
    (0, 768, 256, "xzy"),
    (1, 0, 256, "xzy"),
    (1, 256, 256, "zyx"),
    (1, 512, 256, "yxz"),
    (1, 768, 128, "xzy"),
    (1, 896, 128, "yxz"),
    (1, 1024, 128, "zyx"),
)
OF_QUAD = ((3,), (4,), (5,), (6, 7))


def piece_order():
    column, row, lev = np.meshgrid(np.arange(12), np.arange(6), np.arange(2), indexing="ij")
    top = (column * 24 + row * 2 + lev).reshape(-1)
    return np.concatenate([top, top + 12])


def middle_order():
    column, row, lev = np.meshgrid(np.arange(12), np.arange(24), np.arange(2), indexing="ij")
    north = column * 12 + row * 2 + lev
    inside = 144 + column * 24 + (row - 6) * 2 + lev
    south = 432 + column * 12 + (row - 18) * 2 + lev
    return np.where(row < 6, north, np.where(row < 18, inside, south)).reshape(-1)


def given_order():
    column, row, lev = np.meshgrid(np.arange(12), np.arange(12), np.arange(2), indexing="ij")
    return (row * 24 + column * 2 + lev).reshape(-1)


def one_hot(order, size):
    return (order[:, None] == np.arange(size)[None, :]).astype(np.float32)


def near(shift):
    inner, outer = np.arange(96), np.arange(768)
    row = outer[None] % 48 // 2 - inner[:, None] % 24 // 2 - shift
    column = outer[None] // 48 - inner[:, None] // 24 - shift
    allowed = (row >= 0) & (row <= 11) & (column >= 0) & (column <= 11)
    return np.where(allowed, 0.0, -np.inf).astype(np.float32)


def dot(a, b):
    return jnp.dot(a, b, preferred_element_type=F32)


def dot_nt(a, b):
    return lax.dot_general(a, b, (((1,), (1,)), ((), ())), preferred_element_type=F32)


def dot_tn(a, b):
    return lax.dot_general(a, b, (((0,), (0,)), ((), ())), preferred_element_type=F32)


def without(axes, count):
    return [axis for axis in "zxy" if axis not in axes[:count]]


def extent(axes):
    return tuple(size for axis in axes for size in ((2, 2) if axis == "x" else (4,)))


def index_of(axes, chosen, at):
    out = []
    for axis in axes:
        if axis == "x":
            out += [lax.rem(at, 2), lax.div(at, 2)] if chosen == "x" else [EVERY, EVERY]
        else:
            out += [at] if axis == chosen else [EVERY]
    return tuple(out)


def block_kernel(
    tokens, masked, embed, w_qkv_hbm, w_out_hbm, cotangent_hbm, near_keys_hbm, near_queries_hbm,
    from_given, to_given, to_piece, to_middle_hbm,
    block_out, grad_tokens, gq, go, gm,
    w_qkv, w_out, cotangent, key_bias, query_bias, to_middle, xm, g, hits, ctx, dqkv,
    pieces, stacked, ext, g_stacked, g_ext,
    stats, stat_pieces, stat_stacked, stat_ext, stat_rows, q, d, kv, own_kv, ext_q,
    total, xm_t, made_a, made_b, got_a, got_b, *rest,
):
    scratch = [rest[5 * i : 5 * i + 5] for i in range(len(JOBS))]
    final_a, final_b, cross_a, cross_b, load, send, recv = rest[5 * len(JOBS) :]
    lat, lon = lax.axis_index("lat"), lax.axis_index("lon")
    z, xl = lax.div(lat, 2), lax.rem(lat, 2)
    xh, y, core = lax.div(lon, 8), lax.rem(lax.div(lon, 2), 4), lax.rem(lon, 2)
    x = xh * 2 + xl
    mine = {"x": x, "y": y, "z": z}

    def device(axis, by):
        zz, yy, xx = z, y, x
        if axis == "z":
            zz = lax.rem(z + by, 4)
        elif axis == "y":
            yy = lax.rem(y + by, 4)
        else:
            xx = lax.rem(x + by, 4)
        return (zz * 2 + lax.rem(xx, 2), lax.div(xx, 2) * 8 + yy * 2 + core)

    partner = (lat, lon + 1 - 2 * core)
    north, south = (lax.rem(lat + 7, 8), lon), (lax.rem(lat + 1, 8), lon)
    west, east = (lat, lax.rem(lon + 15, 16)), (lat, lax.rem(lon + 1, 16))

    barrier = pltpu.get_barrier_semaphore()
    greeted = [north, south, west, east, partner]
    greeted += [device(axis, by) for axis in "xyz" for by in (1, 2, 3)]
    for other in greeted:
        pl.semaphore_signal(barrier, inc=1, device_id=other, device_id_type=MESH)

    loaded = (
        (cotangent_hbm, cotangent),
        (near_keys_hbm, key_bias),
        (near_queries_hbm, query_bias),
        (to_middle_hbm, to_middle),
        (w_qkv_hbm, w_qkv),
        (w_out_hbm, w_out),
    )
    loads = [pltpu.make_async_copy(*pair, load.at[i]) for i, pair in enumerate(loaded)]
    for copy in loads:
        copy.start()

    place = lax.broadcasted_iota(jnp.int32, (288, 1), 0)
    place = lax.rem(place, 2) * 144 + lax.div(lax.rem(place, 24), 2) * 12 + lax.div(place, 24)
    found = jnp.where(masked[0] == place, 1.0, 0.0)
    hit = jnp.max(found, axis=-1, keepdims=True) > 0.5
    hits[...] = jnp.where(hit, 1.0, 0.0) + jnp.zeros((288, 128), F32)
    own_tokens = dot(from_given[...], tokens[...].reshape(288, 1024))
    mask_row = jnp.concatenate([embed[i : i + 1, :] for i in range(8)], axis=1).astype(F32)
    xm[...] = jnp.where(hit, mask_row, own_tokens).astype(BF16)

    pieces[...] = dot(to_piece[...], xm[...]).astype(BF16)
    stacked[144:432, :] = xm[...]
    pl.semaphore_wait(barrier, len(greeted))

    def copy_to(source, target, sem, other):
        return pltpu.make_async_remote_copy(
            src_ref=source,
            dst_ref=target,
            send_sem=send.at[sem],
            recv_sem=recv.at[sem],
            device_id=other,
            device_id_type=MESH,
        )

    def part(start, rows):
        return pl.ds(start, rows)

    def tile(t, start=0):
        return pl.ds(pl.multiple_of(t * 256 + start, 256), 256)

    def to_neighbours(source, target, sem):
        return (
            copy_to(source.at[part(0, 144)], target.at[part(432, 144)], sem, north),
            copy_to(source.at[part(144, 144)], target.at[part(0, 144)], sem + 1, south),
        )

    def to_sides(whole, sem):
        return (
            copy_to(whole.at[part(288, 288)], whole.at[part(864, 288)], sem, west),
            copy_to(whole.at[part(576, 288)], whole.at[part(0, 288)], sem + 1, east),
        )

    def begin(copies):
        for copy in copies:
            copy.start()

    def finish(copies):
        for copy in copies:
            copy.wait()

    def reordered(matrix, value):
        high = value.astype(BF16)
        rest_of = value - high.astype(F32)
        middle = rest_of.astype(BF16)
        low = (rest_of - middle.astype(F32)).astype(BF16)
        return (dot(matrix, high) + dot(matrix, middle)) + dot(matrix, low)

    rows_moved = to_neighbours(pieces, stacked, 0)
    sides_moved = to_sides(ext, 2)
    g_rows_moved = to_neighbours(pieces, g_stacked, 4)
    g_sides_moved = to_sides(g_ext, 6)
    stat_rows_moved = to_neighbours(stat_pieces, stat_stacked, 8)
    stat_sides_moved = to_sides(stat_ext, 10)
    begin(rows_moved)

    finish(loads[:4])
    g[...] = dot(from_given[...], cotangent[...].reshape(288, 1024)).astype(BF16)
    g_stacked[144:432, :] = g[...]
    total[...] = g[...].astype(F32)
    xm_t[...] = xm[...].T
    stats[...] = jnp.zeros((288, 128), F32)
    ext_row = lax.broadcasted_iota(jnp.int32, (1, 768), 1)
    ext_row = lax.div(lax.rem(ext_row, 48), 2) + lat * 12 - 6
    on_grid = (ext_row >= 0) & (ext_row < 96)
    key_bias[...] = jnp.where(on_grid, key_bias[...], -jnp.inf)
    query_bias[...] = jnp.where(on_grid, query_bias[...], -jnp.inf)
    finish(loads[4:])

    @pl.loop(0, 4)
    def _(t):
        cols = tile(t)
        q[:, cols] = dot(xm[...], w_qkv[:, cols]).astype(BF16)
        d[:, cols] = dot_nt(g[...], w_out[cols, :]).astype(BF16)
        own_kv[:, cols] = dot(xm[...], w_qkv[:, tile(t, 1024)]).astype(BF16)
        own_kv[:, tile(t, 1024)] = dot(xm[...], w_qkv[:, tile(t, 2048)]).astype(BF16)

    finish(rows_moved)
    ext[288:864, :] = dot(to_middle[...], stacked[...]).astype(BF16)
    begin(sides_moved)
    pieces[...] = dot(to_piece[...], g[...]).astype(BF16)

    def project(tiles, target, first_tile, middle):
        @pl.loop(0, tiles)
        def _(t):
            weights = w_qkv[:, tile(t, first_tile * 256)]
            if middle:
                target[288:864, tile(t)] = dot(ext[288:864, :], weights).astype(BF16)
            else:
                sides = jnp.concatenate([ext[0:288, :], ext[864:1152, :]], axis=0)
                sides = dot(sides, weights).astype(BF16)
                target[0:288, tile(t)] = sides[0:288]
                target[864:1152, tile(t)] = sides[288:576]

    project(8, kv, 4, True)
    project(4, ext_q, 0, True)
    finish(sides_moved)
    begin(g_rows_moved)
    project(8, kv, 4, False)

    lane_head = lax.div(lax.broadcasted_iota(jnp.int32, (96, 256), 1), 64)
    picks = [lane_head == h for h in range(4)]
    nothing = jnp.zeros((96, 256), BF16)
    stat_lane = lax.broadcasted_iota(jnp.int32, (96, 128), 1)
    factor = math.log2(math.e) / 8.0

    def apart(block):
        return jnp.concatenate([jnp.where(pick, block, nothing) for pick in picks], axis=0)

    def joined(out):
        whole = jnp.where(picks[0], out[0:96], 0.0)
        for h in range(1, 4):
            whole = jnp.where(picks[h], out[h * 96 : h * 96 + 96], whole)
        return whole

    def queries(t):
        cols, vcols = tile(t), tile(t, 1024)

        for j in range(3):
            rows = pl.ds(j * 96, 96)
            keys = pl.ds(j * 192, 768)
            qm, dm = apart(q[rows, cols]), apart(d[rows, cols])
            kw, vw = kv[keys, cols], kv[keys, vcols]
            s = dot_nt(qm, kw).reshape(4, 96, 768) + key_bias[...][None]
            top = jnp.max(s, axis=-1, keepdims=True)
            e = jnp.exp2((s - top) * factor)
            share = 1.0 / jnp.sum(e, axis=-1, keepdims=True)
            p = (e * share).reshape(384, 768)
            out = dot(p.astype(BF16), vw)
            delta = jnp.sum(out * dm.astype(F32), axis=-1, keepdims=True)
            ctx[rows, cols] = joined(out).astype(BF16)
            ds = (p * (dot_nt(dm, vw) - delta)).astype(BF16)
            dqkv[rows, cols] = (joined(dot(ds, kw)) * 0.125).astype(BF16)
            kept = stats[rows, :]
            for h in range(4):
                values = (top[h], share[h], delta[h * 96 : h * 96 + 96])
                for kind, value in enumerate(values):
                    kept = jnp.where(stat_lane == t * 16 + kind * 4 + h, value, kept)
            stats[rows, :] = kept

    def keys_of(t):
        cols, vcols = tile(t), tile(t, 1024)

        for j in range(3):
            rows = pl.ds(j * 96, 96)
            seen = pl.ds(j * 192, 768)
            km, vm = apart(own_kv[rows, cols]), apart(own_kv[rows, vcols])
            qw, dw = ext_q[seen, cols], kv[seen, cols]
            known = stat_rows[j, 16 * t : 16 * t + 16, :]
            top, share, delta = (known[4 * i : 4 * i + 4].reshape(4, 1, 768) for i in range(3))
            s = dot_nt(km, qw).reshape(4, 96, 768) + query_bias[...][None]
            p = jnp.exp2((s - top) * factor) * share
            ds = p * (dot_nt(vm, dw).reshape(4, 96, 768) - delta)
            dk = joined(dot(ds.reshape(384, 768).astype(BF16), qw)) * 0.125
            dv = joined(dot(p.reshape(384, 768).astype(BF16), dw))
            dqkv[rows, tile(t, 1024)] = dk.astype(BF16)
            dqkv[rows, tile(t, 2048)] = dv.astype(BF16)

    def add_to_total(t):
        dk, dv = dqkv[:, tile(t, 1024)], dqkv[:, tile(t, 2048)]
        for c in range(4):
            rows = slice(256 * c, 256 * c + 256)
            more = dot_nt(dk, w_qkv[rows, tile(t, 1024)]) + dot_nt(dv, w_qkv[rows, tile(t, 2048)])
            total[:, rows] += more

    @pl.loop(0, 4)
    def _(t):
        queries(t)

        @pl.when(t == 2)
        def _():
            finish(g_rows_moved)
            g_ext[288:864, :] = dot(to_middle[...], g_stacked[...]).astype(BF16)
            begin(g_sides_moved)

    stat_pieces[...] = reordered(to_piece[...], stats[...])
    stat_stacked[144:432, :] = stats[...]
    begin(stat_rows_moved)

    mades, gots = (made_a, made_b), (got_a, got_b)

    def columns(job):
        return pl.ds(JOBS[job][1], JOBS[job][2])

    def store_made(made, half, cols, value):
        made[half, :, :, :, :, :, cols] = value.astype(BF16).reshape(4, 2, 2, 4, 16, 256)

    def make_a(half):
        @pl.when(half == 0)
        def _():
            @pl.loop(0, 4)
            def _(t):
                store_made(made_a, half, tile(t), dot(xm_t[...], dqkv[:, tile(t)]))

        @pl.when(half == 1)
        def _():
            @pl.loop(0, 4)
            def _(t):
                store_made(made_a, half, tile(t), dot_tn(ctx[...], g[:, tile(t)]))

    def make_b(n, half):
        cols = pl.ds(pl.multiple_of(half * 1024 + 1024 + 256 * n, 256), 256)
        store_made(made_b, half, pl.ds(256 * n, 256), dot(xm_t[...], dqkv[:, cols]))

    def exchange(job):
        where = (EVERY,) * 5 + (columns(job),)
        phase = JOBS[job][0]
        return copy_to(mades[phase].at[(1 - core, *where)], gots[phase].at[where], 12 + job, partner)

    def exchanged(job):
        exchange(job).wait()
        cols, made, got = columns(job), mades[JOBS[job][0]], gots[JOBS[job][0]]

        @pl.loop(0, 4)
        def _(a):
            for b in range(2):
                for c in range(2):
                    both = made[core, a, b, c, :, :, cols].astype(F32)
                    both = both + got[a, b, c, :, :, cols].astype(F32)
                    made[core, a, b, c, :, :, cols] = both.astype(BF16)

        start(job, 0)

    def held(job, stage, at):
        order = JOBS[job][3]
        here = index_of(without(order, stage), order[stage], at)
        if stage == 0:
            return mades[JOBS[job][0]], (core, *here, EVERY, columns(job))
        return scratch[job][2 * stage - 1], (*here, EVERY, EVERY)

    def stage_copies(job, stage):
        axis = JOBS[job][3][stage]
        copies = []
        for by in (2, 1, 3):
            ref, where = held(job, stage, lax.rem(mine[axis] + by, 4))
            target = scratch[job][2 * stage].at[by - 1]
            sem = 12 + len(JOBS) + job * 9 + stage * 3 + by - 1
            copies.append(copy_to(ref.at[where], target, sem, device(axis, by)))
        return copies

    def start(job, stage):
        for copy in stage_copies(job, stage):
            copy.start()

    def reduced(job, stage):
        for copy in stage_copies(job, stage):
            copy.wait()
        ref, where = held(job, stage, mine[JOBS[job][3][stage]])
        piece = ref[where].astype(F32)
        for slot in range(3):
            piece = piece + scratch[job][2 * stage][slot].astype(F32)
        if stage < 2:
            scratch[job][2 * stage + 1][...] = piece.astype(BF16)
            start(job, stage + 1)
        else:
            final = (final_a, final_b)[JOBS[job][0]]
            final[:, columns(job)] = piece * (1.0 / 192.0)

    def swap(phase):
        rows = pl.ds(pl.multiple_of((1 - core) * 8, 8), 8)
        source = (final_a, final_b)[phase].at[rows, pl.ds(0, 1024)]
        return copy_to(source, (cross_a, cross_b)[phase], 12 + 10 * len(JOBS) + phase, partner)

    def group(n):
        make_b(n, 1 - core)
        for job in OF_QUAD[n]:
            exchange(job).start()
        make_b(n, core)

    make_a(1 - core)
    for job in (0, 1, 2):
        exchange(job).start()

    project(4, ext_q, 0, False)
    finish(stat_rows_moved)
    stat_ext[288:864, :] = reordered(to_middle[...], stat_stacked[...])
    finish(g_sides_moved)
    begin(stat_sides_moved)
    make_a(core)
    for job in (0, 1, 2):
        exchanged(job)

    @pl.loop(0, 4)
    def _(t):
        kv[:, tile(t)] = dot_nt(g_ext[...], w_out[tile(t), :]).astype(BF16)

    finish(stat_sides_moved)
    for j in range(3):
        stat_rows[j] = stat_ext[192 * j : 192 * j + 768, :].T

    def advance(*steps):
        for job, stage in steps:
            reduced(job, stage)

    keys_of(0)
    group(0)
    add_to_total(0)
    exchanged(3)
    keys_of(1)
    advance((0, 0), (1, 0), (2, 0))
    group(1)
    add_to_total(1)
    exchanged(4)
    keys_of(2)
    advance((0, 1), (1, 1), (2, 1), (3, 0))
    group(2)

    @pl.loop(0, 4)
    def _(t):
        cols = tile(t)
        value = xm[:, cols].astype(F32) + dot(ctx[...], w_out[:, cols])
        value = dot(to_given[...], value.astype(BF16)).astype(BF16)
        block_out[:, :, :, cols] = value.reshape(12, 12, 2, 256)
        total[:, cols] += dot_nt(dqkv[:, 0:1024], w_qkv[cols, 0:1024])

    add_to_total(2)
    exchanged(5)
    keys_of(3)
    make_b(3, 1 - core)
    for job in OF_QUAD[3]:
        exchange(job).start()
    add_to_total(3)

    @pl.loop(0, 4)
    def _(t):
        cols = tile(t)
        hit = hits[...]
        value = total[:, cols]
        high = value.astype(BF16)
        low = (value - high.astype(F32)).astype(BF16)
        column = dot_tn(high, hit.astype(BF16)) + dot_tn(low, hit.astype(BF16))
        column = column.astype(BF16).reshape(2, 2, 4, 16, 128)
        made_b[0, t, :, :, :, :, 1024:1152] = column
        made_b[1, t, :, :, :, :, 1024:1152] = column

    exchange(8).start()
    make_b(3, core)
    exchanged(6)
    exchanged(7)
    exchanged(8)
    advance((3, 1), (4, 0), (5, 0), (0, 2), (1, 2), (2, 2))
    swap(0).start()

    @pl.loop(0, 4)
    def _(t):
        cols = tile(t)
        hit = hits[...]
        value = total[:, cols]
        kept = jnp.where(jnp.concatenate([hit, hit], axis=1) > 0.5, 0.0, value).astype(BF16)
        kept = dot(to_given[...], kept).astype(BF16)
        grad_tokens[:, :, :, cols] = kept.reshape(12, 12, 2, 256)

    advance((6, 0), (7, 0), (8, 0), (4, 1), (5, 1), (3, 2), (6, 1), (7, 1), (8, 1))
    advance((4, 2), (5, 2), (6, 2), (7, 2), (8, 2))
    swap(1).start()
    swap(0).wait()
    swap(1).wait()
    rows = pl.ds(pl.multiple_of(core * 8, 8), 8)
    gm[...] = final_b[rows, 1024:]

    @pl.when(core == 0)
    def _():
        gq[:, 0:1024] = final_a[rows, :]
        gq[:, 1024:2048] = final_b[rows, 0:1024]
        gq[:, 2048:] = cross_b[...]
        go[...] = cross_a[...]

    @pl.when(core == 1)
    def _():
        gq[:, 0:1024] = cross_a[...]
        gq[:, 1024:2048] = cross_b[...]
        gq[:, 2048:] = final_b[rows, 0:1024]
        go[...] = final_a[rows, :]


def hand_out_kernel(block_out, grad_tokens, gq, go, gm, *targets):
    for source, target in zip((block_out, grad_tokens, gq, go), targets):
        target[...] = source[...]
    row = lax.broadcasted_iota(jnp.int32, (8, 128), 0)
    lane = lax.broadcasted_iota(jnp.int32, (8, 128), 1)
    targets[4][...] = jnp.sum(jnp.where(row == lane, gm[...], 0.0), axis=0)[0:8]


def local(tokens, masked, mask_embed, w_qkv, w_out, cotangent):
    given = one_hot(given_order(), 288)
    piece, middle = one_hot(piece_order(), 288), one_hot(middle_order(), 576)
    orders = [given, given.T, piece, middle]
    vmem, hbm = pl.BlockSpec(memory_space=pltpu.VMEM), pl.BlockSpec(memory_space=pl.ANY)
    jobs = []
    for _, _, wide, order in JOBS:
        for stage in (1, 2):
            left = extent(without(order, stage))
            jobs.append(pltpu.VMEM((3, *left, 16, wide), BF16))
            jobs.append(pltpu.VMEM((*left, 16, wide), BF16))
        jobs.append(pltpu.VMEM((3, 16, wide), BF16))
    block_out, grad_tokens, gq, go, gm = pl.pallas_call(
        block_kernel,
        out_shape=(
            jax.ShapeDtypeStruct((12, 12, 2, 1024), BF16),
            jax.ShapeDtypeStruct((12, 12, 2, 1024), BF16),
            jax.ShapeDtypeStruct((8, 3072), F32),
            jax.ShapeDtypeStruct((8, 1024), F32),
            jax.ShapeDtypeStruct((8, 128), F32),
        ),
        in_specs=[vmem] * 3 + [hbm] * 5 + [vmem] * 3 + [hbm],
        out_specs=(vmem,) * 5,
        scratch_shapes=[
            pltpu.VMEM((1024, 3072), BF16),
            pltpu.VMEM((1024, 1024), BF16),
            pltpu.VMEM((12, 12, 2, 1024), BF16),
            pltpu.VMEM((96, 768), F32),
            pltpu.VMEM((96, 768), F32),
            pltpu.VMEM((576, 576), BF16),
            pltpu.VMEM((288, 1024), BF16),
            pltpu.VMEM((288, 1024), BF16),
            pltpu.VMEM((288, 128), F32),
            pltpu.VMEM((288, 1024), BF16),
            pltpu.VMEM((288, 3072), BF16),
            pltpu.VMEM((288, 1024), BF16),
            pltpu.VMEM((576, 1024), BF16),
            pltpu.VMEM((1152, 1024), BF16),
            pltpu.VMEM((576, 1024), BF16),
            pltpu.VMEM((1152, 1024), BF16),
            pltpu.VMEM((288, 128), F32),
            pltpu.VMEM((288, 128), F32),
            pltpu.VMEM((576, 128), F32),
            pltpu.VMEM((1152, 128), F32),
            pltpu.VMEM((3, 128, 768), F32),
            pltpu.VMEM((288, 1024), BF16),
            pltpu.VMEM((288, 1024), BF16),
            pltpu.VMEM((1152, 2048), BF16),
            pltpu.VMEM((288, 2048), BF16),
            pltpu.VMEM((1152, 1024), BF16),
            pltpu.VMEM((288, 1024), F32),
            pltpu.VMEM((1024, 288), BF16),
            pltpu.VMEM((2, 4, 2, 2, 4, 16, 1024), BF16),
            pltpu.VMEM((2, 4, 2, 2, 4, 16, 1152), BF16),
            pltpu.VMEM((4, 2, 2, 4, 16, 1024), BF16),
            pltpu.VMEM((4, 2, 2, 4, 16, 1152), BF16),
            *jobs,
            pltpu.VMEM((16, 1024), F32),
            pltpu.VMEM((16, 1152), F32),
            pltpu.VMEM((8, 1024), F32),
            pltpu.VMEM((8, 1024), F32),
            pltpu.SemaphoreType.DMA((6,)),
            pltpu.SemaphoreType.DMA((14 + 10 * len(JOBS),)),
            pltpu.SemaphoreType.DMA((14 + 10 * len(JOBS),)),
        ],
        compiler_params=pltpu.CompilerParams(
            collective_id=1, has_side_effects=True, vmem_limit_bytes=63 * 1024 * 1024
        ),
        name="attention_block",
    )(
        tokens.transpose(1, 2, 0, 3), masked, mask_embed.reshape(8, 128), w_qkv, w_out,
        cotangent.transpose(1, 2, 0, 3), jnp.asarray(near(0)), jnp.asarray(near(1)),
        *[jnp.asarray(order, BF16) for order in orders],
    )
    block_out, grad_tokens, gq, go, gm = pl.pallas_call(
        hand_out_kernel,
        out_shape=(
            jax.ShapeDtypeStruct((12, 12, 2, 1024), BF16),
            jax.ShapeDtypeStruct((12, 12, 2, 1024), BF16),
            jax.ShapeDtypeStruct((8, 3072), F32),
            jax.ShapeDtypeStruct((8, 1024), F32),
            jax.ShapeDtypeStruct((8,), F32),
        ),
        in_specs=[vmem] * 5,
        out_specs=(vmem,) * 5,
        name="hand_out",
    )(block_out, grad_tokens, gq, go, gm)
    block_out, grad_tokens = block_out.transpose(2, 0, 1, 3), grad_tokens.transpose(2, 0, 1, 3)
    return (block_out, grad_tokens, gq, go, gm)


def solution(mesh):
    placed = (
        P(None, "lat", "lon", None),
        P("lat", "lon", None),
        P(),
        P(),
        P(),
        P(None, "lat", "lon", None),
    )
    return jax.shard_map(
        local,
        mesh=mesh,
        in_specs=placed,
        out_specs=(
            P(None, "lat", "lon", None),
            P(None, "lat", "lon", None),
            P(("lat", "lon"), None),
            P(("lat", "lon"), None),
            P(("lat", "lon")),
        ),
        check_vma=False,
    )
```

```python
import math

import jax
import jax.numpy as jnp
import numpy as np
from jax import lax
from jax.experimental import pallas as pl
from jax.experimental.pallas import tpu as pltpu
from jax.sharding import PartitionSpec as P

HEADS = 16
MESH = pl.DeviceIdType.MESH
BF16 = jnp.bfloat16
F32 = jnp.float32
EVERY = slice(None)


JOBS = (
    (0, 0, 384, "zyx"),
    (0, 384, 384, "yxz"),
    (0, 768, 256, "xzy"),
    (1, 0, 256, "xzy"),
    (1, 256, 256, "zyx"),
    (1, 512, 256, "yxz"),
    (1, 768, 128, "xzy"),
    (1, 896, 128, "zyx"),
    (1, 1024, 128, "yxz"),
)
OF_QUAD = ((3,), (4,), (5,), (6, 7))


def piece_order():
    column, row, lev = np.meshgrid(np.arange(12), np.arange(6), np.arange(2), indexing="ij")
    top = (column * 24 + row * 2 + lev).reshape(-1)
    return np.concatenate([top, top + 12])


def middle_order():
    column, row, lev = np.meshgrid(np.arange(12), np.arange(24), np.arange(2), indexing="ij")
    north = column * 12 + row * 2 + lev
    inside = 144 + column * 24 + (row - 6) * 2 + lev
    south = 432 + column * 12 + (row - 18) * 2 + lev
    return np.where(row < 6, north, np.where(row < 18, inside, south)).reshape(-1)


def given_order():
    column, row, lev = np.meshgrid(np.arange(12), np.arange(12), np.arange(2), indexing="ij")
    return (row * 24 + column * 2 + lev).reshape(-1)


def one_hot(order, size):
    return (order[:, None] == np.arange(size)[None, :]).astype(np.float32)


def near(shift):
    inner, outer = np.arange(96), np.arange(768)
    row = outer[None] % 48 // 2 - inner[:, None] % 24 // 2 - shift
    column = outer[None] // 48 - inner[:, None] // 24 - shift
    allowed = (row >= 0) & (row <= 11) & (column >= 0) & (column <= 11)
    return np.where(allowed, 0.0, -np.inf).astype(np.float32)


def dot(a, b):
    return jnp.dot(a, b, preferred_element_type=F32)


def dot_nt(a, b):
    return lax.dot_general(a, b, (((1,), (1,)), ((), ())), preferred_element_type=F32)


def dot_tn(a, b):
    return lax.dot_general(a, b, (((0,), (0,)), ((), ())), preferred_element_type=F32)


def without(axes, count):
    return [axis for axis in "zxy" if axis not in axes[:count]]


def extent(axes):
    return tuple(size for axis in axes for size in ((2, 2) if axis == "x" else (4,)))


def index_of(axes, chosen, at):
    out = []
    for axis in axes:
        if axis == "x":
            out += [lax.rem(at, 2), lax.div(at, 2)] if chosen == "x" else [EVERY, EVERY]
        else:
            out += [at] if axis == chosen else [EVERY]
    return tuple(out)


def block_kernel(
    tokens, masked, embed, w_qkv_hbm, w_out_hbm, cotangent_hbm, near_keys_hbm, near_queries_hbm,
    from_given, to_given, to_piece, to_middle_hbm,
    block_out_hbm, grad_tokens_hbm, gq, go, gm,
    block_out, grad_tokens, w_qkv, w_out, cotangent, key_bias, query_bias, to_middle, xm, g, hits, ctx, dqkv,
    pieces, stacked, ext, g_stacked, g_ext,
    stats, stat_pieces, stat_stacked, stat_ext, stat_rows, q, d, kv, own_kv, ext_q,
    total, xm_t, ctx_t, made_a, made_b, got_a, got_b, *rest,
):
    scratch = [rest[5 * i : 5 * i + 5] for i in range(len(JOBS))]
    final_a, final_b, cross_a, cross_b, load, send, recv = rest[5 * len(JOBS) :]
    lat, lon = lax.axis_index("lat"), lax.axis_index("lon")
    z, xl = lax.div(lat, 2), lax.rem(lat, 2)
    xh, y, core = lax.div(lon, 8), lax.rem(lax.div(lon, 2), 4), lax.rem(lon, 2)
    x = xh * 2 + xl
    mine = {"x": x, "y": y, "z": z}

    def device(axis, by):
        zz, yy, xx = z, y, x
        if axis == "z":
            zz = lax.rem(z + by, 4)
        elif axis == "y":
            yy = lax.rem(y + by, 4)
        else:
            xx = lax.rem(x + by, 4)
        return (zz * 2 + lax.rem(xx, 2), lax.div(xx, 2) * 8 + yy * 2 + core)

    partner = (lat, lon + 1 - 2 * core)
    north, south = (lax.rem(lat + 7, 8), lon), (lax.rem(lat + 1, 8), lon)
    west, east = (lat, lax.rem(lon + 15, 16)), (lat, lax.rem(lon + 1, 16))

    barrier = pltpu.get_barrier_semaphore()
    greeted = [north, south, west, east, partner]
    greeted += [device(axis, by) for axis in "xyz" for by in (1, 2, 3)]
    for other in greeted:
        pl.semaphore_signal(barrier, inc=1, device_id=other, device_id_type=MESH)

    loaded = (
        (cotangent_hbm, cotangent),
        (near_keys_hbm, key_bias),
        (near_queries_hbm, query_bias),
        (to_middle_hbm, to_middle),
        (w_qkv_hbm, w_qkv),
        (w_out_hbm, w_out),
    )
    loads = [pltpu.make_async_copy(*pair, load.at[i]) for i, pair in enumerate(loaded)]
    for copy in loads:
        copy.start()

    place = lax.broadcasted_iota(jnp.int32, (288, 1), 0)
    place = lax.rem(place, 2) * 144 + lax.div(lax.rem(place, 24), 2) * 12 + lax.div(place, 24)
    found = jnp.where(masked[0] == place, 1.0, 0.0)
    hit = jnp.max(found, axis=-1, keepdims=True) > 0.5
    hits[...] = jnp.where(hit, 1.0, 0.0) + jnp.zeros((288, 128), F32)
    own_tokens = dot(from_given[...], tokens[...].reshape(288, 1024))
    mask_row = jnp.concatenate([embed[i : i + 1, :] for i in range(8)], axis=1).astype(F32)
    xm[...] = jnp.where(hit, mask_row, own_tokens).astype(BF16)

    pieces[...] = dot(to_piece[...], xm[...]).astype(BF16)
    stacked[144:432, :] = xm[...]
    pl.semaphore_wait(barrier, len(greeted))

    def copy_to(source, target, sem, other):
        return pltpu.make_async_remote_copy(
            src_ref=source,
            dst_ref=target,
            send_sem=send.at[sem],
            recv_sem=recv.at[sem],
            device_id=other,
            device_id_type=MESH,
        )

    def part(start, rows):
        return pl.ds(start, rows)

    def tile(t, start=0):
        return pl.ds(pl.multiple_of(t * 256 + start, 256), 256)

    def to_neighbours(source, target, sem):
        return (
            copy_to(source.at[part(0, 144)], target.at[part(432, 144)], sem, north),
            copy_to(source.at[part(144, 144)], target.at[part(0, 144)], sem + 1, south),
        )

    def to_sides(whole, sem):
        return (
            copy_to(whole.at[part(288, 288)], whole.at[part(864, 288)], sem, west),
            copy_to(whole.at[part(576, 288)], whole.at[part(0, 288)], sem + 1, east),
        )

    def begin(copies):
        for copy in copies:
            copy.start()

    def finish(copies):
        for copy in copies:
            copy.wait()

    def reordered(matrix, value):
        high = value.astype(BF16)
        rest_of = value - high.astype(F32)
        middle = rest_of.astype(BF16)
        low = (rest_of - middle.astype(F32)).astype(BF16)
        return (dot(matrix, high) + dot(matrix, middle)) + dot(matrix, low)

    rows_moved = to_neighbours(pieces, stacked, 0)
    sides_moved = to_sides(ext, 2)
    g_rows_moved = to_neighbours(pieces, g_stacked, 4)
    g_sides_moved = to_sides(g_ext, 6)
    stat_rows_moved = to_neighbours(stat_pieces, stat_stacked, 8)
    stat_sides_moved = to_sides(stat_ext, 10)
    begin(rows_moved)

    finish(loads[:4])
    g[...] = dot(from_given[...], cotangent[...].reshape(288, 1024)).astype(BF16)
    g_stacked[144:432, :] = g[...]
    total[...] = g[...].astype(F32)
    xm_t[...] = xm[...].T
    stats[...] = jnp.zeros((288, 128), F32)
    ext_row = lax.broadcasted_iota(jnp.int32, (1, 768), 1)
    ext_row = lax.div(lax.rem(ext_row, 48), 2) + lat * 12 - 6
    on_grid = (ext_row >= 0) & (ext_row < 96)
    key_bias[...] = jnp.where(on_grid, key_bias[...], -jnp.inf)
    query_bias[...] = jnp.where(on_grid, query_bias[...], -jnp.inf)
    finish(loads[4:])

    @pl.loop(0, 4)
    def _(t):
        cols = tile(t)
        q[:, cols] = dot(xm[...], w_qkv[:, cols]).astype(BF16)
        d[:, cols] = dot_nt(g[...], w_out[cols, :]).astype(BF16)
        own_kv[:, cols] = dot(xm[...], w_qkv[:, tile(t, 1024)]).astype(BF16)
        own_kv[:, tile(t, 1024)] = dot(xm[...], w_qkv[:, tile(t, 2048)]).astype(BF16)

    finish(rows_moved)
    ext[288:864, :] = dot(to_middle[...], stacked[...]).astype(BF16)
    begin(sides_moved)
    pieces[...] = dot(to_piece[...], g[...]).astype(BF16)

    def project(tiles, target, first_tile, middle):
        @pl.loop(0, tiles)
        def _(t):
            weights = w_qkv[:, tile(t, first_tile * 256)]
            if middle:
                target[288:864, tile(t)] = dot(ext[288:864, :], weights).astype(BF16)
            else:
                sides = jnp.concatenate([ext[0:288, :], ext[864:1152, :]], axis=0)
                sides = dot(sides, weights).astype(BF16)
                target[0:288, tile(t)] = sides[0:288]
                target[864:1152, tile(t)] = sides[288:576]

    project(8, kv, 4, True)
    project(4, ext_q, 0, True)
    finish(sides_moved)
    begin(g_rows_moved)
    project(8, kv, 4, False)

    lane_head = lax.div(lax.broadcasted_iota(jnp.int32, (96, 256), 1), 64)
    picks = [lane_head == h for h in range(4)]
    nothing = jnp.zeros((96, 256), BF16)
    stat_lane = lax.broadcasted_iota(jnp.int32, (96, 128), 1)
    factor = math.log2(math.e) / 8.0

    def apart(block):
        return jnp.concatenate([jnp.where(pick, block, nothing) for pick in picks], axis=0)

    def joined(out):
        whole = jnp.where(picks[0], out[0:96], 0.0)
        for h in range(1, 4):
            whole = jnp.where(picks[h], out[h * 96 : h * 96 + 96], whole)
        return whole

    def queries(t):
        cols, vcols = tile(t), tile(t, 1024)

        for j in range(3):
            rows = pl.ds(j * 96, 96)
            keys = pl.ds(j * 192, 768)
            qm, dm = apart(q[rows, cols]), apart(d[rows, cols])
            kw, vw = kv[keys, cols], kv[keys, vcols]
            s = dot_nt(qm, kw).reshape(4, 96, 768) + key_bias[...][None]
            top = jnp.max(s, axis=-1, keepdims=True)
            e = jnp.exp2((s - top) * factor)
            share = 1.0 / jnp.sum(e, axis=-1, keepdims=True)
            p = (e * share).reshape(384, 768)
            out = dot(p.astype(BF16), vw)
            delta = jnp.sum(out * dm.astype(F32), axis=-1, keepdims=True)
            ctx[rows, cols] = joined(out).astype(BF16)
            ds = (p * (dot_nt(dm, vw) - delta)).astype(BF16)
            dqkv[rows, cols] = (joined(dot(ds, kw)) * 0.125).astype(BF16)
            kept = stats[rows, :]
            for h in range(4):
                values = (top[h], share[h], delta[h * 96 : h * 96 + 96])
                for kind, value in enumerate(values):
                    kept = jnp.where(stat_lane == t * 16 + kind * 4 + h, value, kept)
            stats[rows, :] = kept

    def keys_of(t):
        cols, vcols = tile(t), tile(t, 1024)

        for j in range(3):
            rows = pl.ds(j * 96, 96)
            seen = pl.ds(j * 192, 768)
            km, vm = apart(own_kv[rows, cols]), apart(own_kv[rows, vcols])
            qw, dw = ext_q[seen, cols], kv[seen, cols]
            known = stat_rows[j, 16 * t : 16 * t + 16, :]
            top, share, delta = (known[4 * i : 4 * i + 4].reshape(4, 1, 768) for i in range(3))
            s = dot_nt(km, qw).reshape(4, 96, 768) + query_bias[...][None]
            p = jnp.exp2((s - top) * factor) * share
            ds = p * (dot_nt(vm, dw).reshape(4, 96, 768) - delta)
            dk = joined(dot(ds.reshape(384, 768).astype(BF16), qw)) * 0.125
            dv = joined(dot(p.reshape(384, 768).astype(BF16), dw))
            dqkv[rows, tile(t, 1024)] = dk.astype(BF16)
            dqkv[rows, tile(t, 2048)] = dv.astype(BF16)

    def add_to_total(t):
        dk, dv = dqkv[:, tile(t, 1024)], dqkv[:, tile(t, 2048)]
        for c in range(4):
            rows = slice(256 * c, 256 * c + 256)
            more = dot_nt(dk, w_qkv[rows, tile(t, 1024)]) + dot_nt(dv, w_qkv[rows, tile(t, 2048)])
            total[:, rows] += more

    @pl.loop(0, 4)
    def _(t):
        queries(t)

        @pl.when(t == 2)
        def _():
            finish(g_rows_moved)
            g_ext[288:864, :] = dot(to_middle[...], g_stacked[...]).astype(BF16)
            begin(g_sides_moved)

    stat_pieces[...] = reordered(to_piece[...], stats[...])
    stat_stacked[144:432, :] = stats[...]
    begin(stat_rows_moved)

    mades, gots = (made_a, made_b), (got_a, got_b)

    def columns(job):
        return pl.ds(JOBS[job][1], JOBS[job][2])

    def store_made(made, half, cols, value):
        made[half, :, :, :, :, :, cols] = value.astype(BF16).reshape(4, 2, 2, 4, 16, 256)

    def make_a(half):
        @pl.when(half == 0)
        def _():
            @pl.loop(0, 4)
            def _(t):
                store_made(made_a, half, tile(t), dot(xm_t[...], dqkv[:, tile(t)]))

        @pl.when(half == 1)
        def _():
            @pl.loop(0, 4)
            def _(t):
                store_made(made_a, half, tile(t), dot(ctx_t[...], g[:, tile(t)]))

    def make_b(n, half):
        cols = pl.ds(pl.multiple_of(half * 1024 + 1024 + 256 * n, 256), 256)
        store_made(made_b, half, pl.ds(256 * n, 256), dot(xm_t[...], dqkv[:, cols]))

    def exchange(job):
        where = (EVERY,) * 5 + (columns(job),)
        phase = JOBS[job][0]
        return copy_to(mades[phase].at[(1 - core, *where)], gots[phase].at[where], 12 + job, partner)

    def exchanged(job):
        exchange(job).wait()
        cols, made, got = columns(job), mades[JOBS[job][0]], gots[JOBS[job][0]]

        @pl.loop(0, 4)
        def _(a):
            for b in range(2):
                for c in range(2):
                    both = made[core, a, b, c, :, :, cols].astype(F32)
                    both = both + got[a, b, c, :, :, cols].astype(F32)
                    made[core, a, b, c, :, :, cols] = both.astype(BF16)

        start(job, 0)

    def held(job, stage, at):
        order = JOBS[job][3]
        here = index_of(without(order, stage), order[stage], at)
        if stage == 0:
            return mades[JOBS[job][0]], (core, *here, EVERY, columns(job))
        return scratch[job][2 * stage - 1], (*here, EVERY, EVERY)

    def stage_copies(job, stage):
        axis = JOBS[job][3][stage]
        copies = []
        for by in (2, 1, 3):
            ref, where = held(job, stage, lax.rem(mine[axis] + by, 4))
            target = scratch[job][2 * stage].at[by - 1]
            sem = 12 + len(JOBS) + job * 9 + stage * 3 + by - 1
            copies.append(copy_to(ref.at[where], target, sem, device(axis, by)))
        return copies

    def start(job, stage):
        for copy in stage_copies(job, stage):
            copy.start()

    def reduced(job, stage):
        for copy in stage_copies(job, stage):
            copy.wait()
        ref, where = held(job, stage, mine[JOBS[job][3][stage]])
        piece = ref[where].astype(F32)
        for slot in range(3):
            piece = piece + scratch[job][2 * stage][slot].astype(F32)
        if stage < 2:
            scratch[job][2 * stage + 1][...] = piece.astype(BF16)
            start(job, stage + 1)
        else:
            final = (final_a, final_b)[JOBS[job][0]]
            final[:, columns(job)] = piece * (1.0 / 192.0)

    def swap(phase):
        rows = pl.ds(pl.multiple_of((1 - core) * 8, 8), 8)
        source = (final_a, final_b)[phase].at[rows, pl.ds(0, 1024)]
        return copy_to(source, (cross_a, cross_b)[phase], 12 + 10 * len(JOBS) + phase, partner)

    def group(n):
        make_b(n, 1 - core)
        for job in OF_QUAD[n]:
            exchange(job).start()
        make_b(n, core)

    ctx_t[...] = ctx[...].T
    leaving = (
        pltpu.make_async_copy(block_out, block_out_hbm, load.at[6]),
        pltpu.make_async_copy(grad_tokens, grad_tokens_hbm, load.at[7]),
    )
    make_a(1 - core)
    for job in (0, 1, 2):
        exchange(job).start()

    project(4, ext_q, 0, False)
    finish(stat_rows_moved)
    stat_ext[288:864, :] = reordered(to_middle[...], stat_stacked[...])
    finish(g_sides_moved)
    begin(stat_sides_moved)
    make_a(core)
    for job in (0, 1, 2):
        exchanged(job)

    @pl.loop(0, 4)
    def _(t):
        kv[:, tile(t)] = dot_nt(g_ext[...], w_out[tile(t), :]).astype(BF16)

    finish(stat_sides_moved)
    for j in range(3):
        stat_rows[j] = stat_ext[192 * j : 192 * j + 768, :].T

    def advance(*steps):
        for job, stage in steps:
            reduced(job, stage)

    keys_of(0)
    group(0)
    add_to_total(0)
    exchanged(3)
    keys_of(1)
    advance((0, 0), (1, 0), (2, 0))
    group(1)
    add_to_total(1)
    exchanged(4)
    keys_of(2)
    advance((0, 1), (1, 1), (2, 1), (3, 0))
    group(2)

    @pl.loop(0, 4)
    def _(t):
        cols = tile(t)
        total[:, cols] += dot_nt(dqkv[:, 0:1024], w_qkv[cols, 0:1024])

    add_to_total(2)
    exchanged(5)
    keys_of(3)
    make_b(3, 1 - core)
    for job in OF_QUAD[3]:
        exchange(job).start()
    add_to_total(3)

    @pl.loop(0, 4)
    def _(t):
        cols = tile(t)
        hit = hits[...]
        value = total[:, cols]
        high = value.astype(BF16)
        low = (value - high.astype(F32)).astype(BF16)
        column = dot_tn(high, hit.astype(BF16)) + dot_tn(low, hit.astype(BF16))
        column = column.astype(BF16).reshape(2, 2, 4, 16, 128)
        made_b[0, t, :, :, :, :, 1024:1152] = column
        made_b[1, t, :, :, :, :, 1024:1152] = column

    exchange(8).start()
    make_b(3, core)
    exchanged(6)
    exchanged(7)
    exchanged(8)
    advance((3, 1), (4, 0), (5, 0), (0, 2), (1, 2), (2, 2))
    swap(0).start()

    @pl.loop(0, 4)
    def _(t):
        cols = tile(t)
        hit = hits[...]
        value = total[:, cols]
        kept = jnp.where(jnp.concatenate([hit, hit], axis=1) > 0.5, 0.0, value).astype(BF16)
        kept = dot(to_given[...], kept).astype(BF16)
        grad_tokens[:, :, :, cols] = kept.reshape(12, 12, 2, 256)

    leaving[1].start()
    advance((6, 0), (7, 0), (8, 0))

    @pl.loop(0, 4)
    def _(t):
        cols = tile(t)
        value = xm[:, cols].astype(F32) + dot(ctx[...], w_out[:, cols])
        value = dot(to_given[...], value.astype(BF16)).astype(BF16)
        block_out[:, :, :, cols] = value.reshape(12, 12, 2, 256)

    leaving[0].start()
    advance((4, 1), (5, 1), (3, 2), (6, 1), (7, 1), (8, 1))
    advance((4, 2), (5, 2), (6, 2), (7, 2), (8, 2))
    swap(1).start()
    finish(leaving)
    swap(0).wait()
    swap(1).wait()
    rows = pl.ds(pl.multiple_of(core * 8, 8), 8)
    gm[...] = final_b[rows, 1024:]

    @pl.when(core == 0)
    def _():
        gq[:, 0:1024] = final_a[rows, :]
        gq[:, 1024:2048] = final_b[rows, 0:1024]
        gq[:, 2048:] = cross_b[...]
        go[...] = cross_a[...]

    @pl.when(core == 1)
    def _():
        gq[:, 0:1024] = cross_a[...]
        gq[:, 1024:2048] = cross_b[...]
        gq[:, 2048:] = final_b[rows, 0:1024]
        go[...] = final_a[rows, :]


def hand_out_kernel(block_out, grad_tokens, gq, go, gm, *targets):
    for source, target in zip((block_out, grad_tokens, gq, go), targets):
        target[...] = source[...]
    row = lax.broadcasted_iota(jnp.int32, (8, 128), 0)
    lane = lax.broadcasted_iota(jnp.int32, (8, 128), 1)
    targets[4][...] = jnp.sum(jnp.where(row == lane, gm[...], 0.0), axis=0)[0:8]


def local(tokens, masked, mask_embed, w_qkv, w_out, cotangent):
    given = one_hot(given_order(), 288)
    piece, middle = one_hot(piece_order(), 288), one_hot(middle_order(), 576)
    orders = [given, given.T, piece, middle]
    vmem, hbm = pl.BlockSpec(memory_space=pltpu.VMEM), pl.BlockSpec(memory_space=pl.ANY)
    jobs = []
    for _, _, wide, order in JOBS:
        for stage in (1, 2):
            left = extent(without(order, stage))
            jobs.append(pltpu.VMEM((3, *left, 16, wide), BF16))
            jobs.append(pltpu.VMEM((*left, 16, wide), BF16))
        jobs.append(pltpu.VMEM((3, 16, wide), BF16))
    block_out, grad_tokens, gq, go, gm = pl.pallas_call(
        block_kernel,
        out_shape=(
            jax.ShapeDtypeStruct((12, 12, 2, 1024), BF16),
            jax.ShapeDtypeStruct((12, 12, 2, 1024), BF16),
            jax.ShapeDtypeStruct((8, 3072), F32),
            jax.ShapeDtypeStruct((8, 1024), F32),
            jax.ShapeDtypeStruct((8, 128), F32),
        ),
        in_specs=[vmem] * 3 + [hbm] * 5 + [vmem] * 3 + [hbm],
        out_specs=(hbm, hbm, vmem, vmem, vmem),
        scratch_shapes=[
            pltpu.VMEM((12, 12, 2, 1024), BF16),
            pltpu.VMEM((12, 12, 2, 1024), BF16),
            pltpu.VMEM((1024, 3072), BF16),
            pltpu.VMEM((1024, 1024), BF16),
            pltpu.VMEM((12, 12, 2, 1024), BF16),
            pltpu.VMEM((96, 768), F32),
            pltpu.VMEM((96, 768), F32),
            pltpu.VMEM((576, 576), BF16),
            pltpu.VMEM((288, 1024), BF16),
            pltpu.VMEM((288, 1024), BF16),
            pltpu.VMEM((288, 128), F32),
            pltpu.VMEM((288, 1024), BF16),
            pltpu.VMEM((288, 3072), BF16),
            pltpu.VMEM((288, 1024), BF16),
            pltpu.VMEM((576, 1024), BF16),
            pltpu.VMEM((1152, 1024), BF16),
            pltpu.VMEM((576, 1024), BF16),
            pltpu.VMEM((1152, 1024), BF16),
            pltpu.VMEM((288, 128), F32),
            pltpu.VMEM((288, 128), F32),
            pltpu.VMEM((576, 128), F32),
            pltpu.VMEM((1152, 128), F32),
            pltpu.VMEM((3, 128, 768), F32),
            pltpu.VMEM((288, 1024), BF16),
            pltpu.VMEM((288, 1024), BF16),
            pltpu.VMEM((1152, 2048), BF16),
            pltpu.VMEM((288, 2048), BF16),
            pltpu.VMEM((1152, 1024), BF16),
            pltpu.VMEM((288, 1024), F32),
            pltpu.VMEM((1024, 288), BF16),
            pltpu.VMEM((1024, 288), BF16),
            pltpu.VMEM((2, 4, 2, 2, 4, 16, 1024), BF16),
            pltpu.VMEM((2, 4, 2, 2, 4, 16, 1152), BF16),
            pltpu.VMEM((4, 2, 2, 4, 16, 1024), BF16),
            pltpu.VMEM((4, 2, 2, 4, 16, 1152), BF16),
            *jobs,
            pltpu.VMEM((16, 1024), F32),
            pltpu.VMEM((16, 1152), F32),
            pltpu.VMEM((8, 1024), F32),
            pltpu.VMEM((8, 1024), F32),
            pltpu.SemaphoreType.DMA((8,)),
            pltpu.SemaphoreType.DMA((14 + 10 * len(JOBS),)),
            pltpu.SemaphoreType.DMA((14 + 10 * len(JOBS),)),
        ],
        compiler_params=pltpu.CompilerParams(
            collective_id=1, has_side_effects=True, vmem_limit_bytes=63 * 1024 * 1024
        ),
        name="attention_block",
    )(
        tokens.transpose(1, 2, 0, 3), masked, mask_embed.reshape(8, 128), w_qkv, w_out,
        cotangent.transpose(1, 2, 0, 3), jnp.asarray(near(0)), jnp.asarray(near(1)),
        *[jnp.asarray(order, BF16) for order in orders],
    )
    block_out, grad_tokens, gq, go, gm = pl.pallas_call(
        hand_out_kernel,
        out_shape=(
            jax.ShapeDtypeStruct((12, 12, 2, 1024), BF16),
            jax.ShapeDtypeStruct((12, 12, 2, 1024), BF16),
            jax.ShapeDtypeStruct((8, 3072), F32),
            jax.ShapeDtypeStruct((8, 1024), F32),
            jax.ShapeDtypeStruct((8,), F32),
        ),
        in_specs=[vmem] * 5,
        out_specs=(vmem,) * 5,
        name="hand_out",
    )(block_out, grad_tokens, gq, go, gm)
    block_out, grad_tokens = block_out.transpose(2, 0, 1, 3), grad_tokens.transpose(2, 0, 1, 3)
    return (block_out, grad_tokens, gq, go, gm)


def solution(mesh):
    placed = (
        P(None, "lat", "lon", None),
        P("lat", "lon", None),
        P(),
        P(),
        P(),
        P(None, "lat", "lon", None),
    )
    return jax.shard_map(
        local,
        mesh=mesh,
        in_specs=placed,
        out_specs=(
            P(None, "lat", "lon", None),
            P(None, "lat", "lon", None),
            P(("lat", "lon"), None),
            P(("lat", "lon"), None),
            P(("lat", "lon")),
        ),
        check_vma=False,
    )
```

```python
import math

import jax
import jax.numpy as jnp
import numpy as np
from jax import lax
from jax.experimental import pallas as pl
from jax.experimental.pallas import tpu as pltpu
from jax.sharding import PartitionSpec as P

HEADS = 16
MESH = pl.DeviceIdType.MESH
BF16 = jnp.bfloat16
F32 = jnp.float32
EVERY = slice(None)


JOBS = (
    (0, 0, 384, "zyx"),
    (0, 384, 384, "yxz"),
    (0, 768, 256, "xzy"),
    (1, 0, 256, "xzy"),
    (1, 256, 256, "zyx"),
    (1, 512, 256, "yxz"),
    (1, 768, 128, "xzy"),
    (1, 896, 128, "zyx"),
    (1, 1024, 128, "yxz"),
)
OF_QUAD = ((3,), (4,), (5,), (6, 7))


def piece_order():
    column, row, lev = np.meshgrid(np.arange(12), np.arange(6), np.arange(2), indexing="ij")
    top = (column * 24 + row * 2 + lev).reshape(-1)
    return np.concatenate([top, top + 12])


def middle_order():
    column, row, lev = np.meshgrid(np.arange(12), np.arange(24), np.arange(2), indexing="ij")
    north = column * 12 + row * 2 + lev
    inside = 144 + column * 24 + (row - 6) * 2 + lev
    south = 432 + column * 12 + (row - 18) * 2 + lev
    return np.where(row < 6, north, np.where(row < 18, inside, south)).reshape(-1)


def given_order():
    column, row, lev = np.meshgrid(np.arange(12), np.arange(12), np.arange(2), indexing="ij")
    return (row * 24 + column * 2 + lev).reshape(-1)


def one_hot(order, size):
    return (order[:, None] == np.arange(size)[None, :]).astype(np.float32)


def near(shift):
    inner, outer = np.arange(96), np.arange(768)
    row = outer[None] % 48 // 2 - inner[:, None] % 24 // 2 - shift
    column = outer[None] // 48 - inner[:, None] // 24 - shift
    allowed = (row >= 0) & (row <= 11) & (column >= 0) & (column <= 11)
    return np.where(allowed, 0.0, -np.inf).astype(np.float32)


def dot(a, b):
    return jnp.dot(a, b, preferred_element_type=F32)


def dot_nt(a, b):
    return lax.dot_general(a, b, (((1,), (1,)), ((), ())), preferred_element_type=F32)


def dot_tn(a, b):
    return lax.dot_general(a, b, (((0,), (0,)), ((), ())), preferred_element_type=F32)


def without(axes, count):
    return [axis for axis in "zxy" if axis not in axes[:count]]


def extent(axes):
    return tuple(size for axis in axes for size in ((2, 2) if axis == "x" else (4,)))


def index_of(axes, chosen, at):
    out = []
    for axis in axes:
        if axis == "x":
            out += [lax.rem(at, 2), lax.div(at, 2)] if chosen == "x" else [EVERY, EVERY]
        else:
            out += [at] if axis == chosen else [EVERY]
    return tuple(out)


def block_kernel(
    tokens, masked, embed, w_qkv_hbm, w_out_hbm, cotangent_hbm, near_keys_hbm, near_queries_hbm,
    from_given, to_given, to_piece, to_middle_hbm,
    block_out_hbm, grad_tokens_hbm, gq, go, gm,
    block_out, grad_tokens, w_qkv, w_out, cotangent, key_bias, query_bias, to_middle, xm, g, hits, ctx, dqkv,
    pieces, stacked, ext, g_stacked, g_ext,
    stats, stat_pieces, stat_stacked, stat_ext, stat_rows, q, d, kv, own_kv, ext_q,
    total, xm_t, ctx_t, made_a, made_b, got_a, got_b, *rest,
):
    scratch = [rest[5 * i : 5 * i + 5] for i in range(len(JOBS))]
    final_a, final_b, cross_a, cross_b, load, send, recv = rest[5 * len(JOBS) :]
    lat, lon = lax.axis_index("lat"), lax.axis_index("lon")
    z, xl = lax.div(lat, 2), lax.rem(lat, 2)
    xh, y, core = lax.div(lon, 8), lax.rem(lax.div(lon, 2), 4), lax.rem(lon, 2)
    x = xh * 2 + xl
    mine = {"x": x, "y": y, "z": z}

    def device(axis, by):
        zz, yy, xx = z, y, x
        if axis == "z":
            zz = lax.rem(z + by, 4)
        elif axis == "y":
            yy = lax.rem(y + by, 4)
        else:
            xx = lax.rem(x + by, 4)
        return (zz * 2 + lax.rem(xx, 2), lax.div(xx, 2) * 8 + yy * 2 + core)

    partner = (lat, lon + 1 - 2 * core)
    north, south = (lax.rem(lat + 7, 8), lon), (lax.rem(lat + 1, 8), lon)
    west, east = (lat, lax.rem(lon + 15, 16)), (lat, lax.rem(lon + 1, 16))

    barrier = pltpu.get_barrier_semaphore()
    greeted = [north, south, west, east, partner]
    greeted += [device(axis, by) for axis in "xyz" for by in (1, 2, 3)]
    for other in greeted:
        pl.semaphore_signal(barrier, inc=1, device_id=other, device_id_type=MESH)

    loaded = (
        (cotangent_hbm, cotangent),
        (near_keys_hbm, key_bias),
        (near_queries_hbm, query_bias),
        (to_middle_hbm, to_middle),
        (w_qkv_hbm, w_qkv),
        (w_out_hbm, w_out),
    )
    loads = [pltpu.make_async_copy(*pair, load.at[i]) for i, pair in enumerate(loaded)]
    for copy in loads:
        copy.start()

    place = lax.broadcasted_iota(jnp.int32, (288, 1), 0)
    place = lax.rem(place, 2) * 144 + lax.div(lax.rem(place, 24), 2) * 12 + lax.div(place, 24)
    found = jnp.where(masked[0] == place, 1.0, 0.0)
    hit = jnp.max(found, axis=-1, keepdims=True) > 0.5
    hits[...] = jnp.where(hit, 1.0, 0.0) + jnp.zeros((288, 128), F32)
    own_tokens = dot(from_given[...], tokens[...].reshape(288, 1024))
    mask_rows = embed[...].astype(F32)
    mask_row = jnp.concatenate([mask_rows[i : i + 1] for i in range(8)], axis=1)
    xm[...] = jnp.where(hit, mask_row, own_tokens).astype(BF16)

    pieces[...] = dot(to_piece[...], xm[...]).astype(BF16)
    stacked[144:432, :] = xm[...]
    pl.semaphore_wait(barrier, len(greeted))

    def copy_to(source, target, sem, other):
        return pltpu.make_async_remote_copy(
            src_ref=source,
            dst_ref=target,
            send_sem=send.at[sem],
            recv_sem=recv.at[sem],
            device_id=other,
            device_id_type=MESH,
        )

    def part(start, rows):
        return pl.ds(start, rows)

    def tile(t, start=0):
        return pl.ds(pl.multiple_of(t * 256 + start, 256), 256)

    def to_neighbours(source, target, sem):
        return (
            copy_to(source.at[part(0, 144)], target.at[part(432, 144)], sem, north),
            copy_to(source.at[part(144, 144)], target.at[part(0, 144)], sem + 1, south),
        )

    def to_sides(whole, sem):
        return (
            copy_to(whole.at[part(288, 288)], whole.at[part(864, 288)], sem, west),
            copy_to(whole.at[part(576, 288)], whole.at[part(0, 288)], sem + 1, east),
        )

    def begin(copies):
        for copy in copies:
            copy.start()

    def finish(copies):
        for copy in copies:
            copy.wait()

    def reordered(matrix, value):
        high = value.astype(BF16)
        rest_of = value - high.astype(F32)
        middle = rest_of.astype(BF16)
        low = (rest_of - middle.astype(F32)).astype(BF16)
        return (dot(matrix, high) + dot(matrix, middle)) + dot(matrix, low)

    rows_moved = to_neighbours(pieces, stacked, 0)
    sides_moved = to_sides(ext, 2)
    g_rows_moved = to_neighbours(pieces, g_stacked, 4)
    g_sides_moved = to_sides(g_ext, 6)
    stat_rows_moved = to_neighbours(stat_pieces, stat_stacked, 8)
    stat_sides_moved = to_sides(stat_ext, 10)
    begin(rows_moved)

    finish(loads[:4])
    g[...] = dot(from_given[...], cotangent[...].reshape(288, 1024)).astype(BF16)
    g_stacked[144:432, :] = g[...]
    total[...] = g[...].astype(F32)
    xm_t[...] = xm[...].T
    stats[...] = jnp.zeros((288, 128), F32)
    ext_row = lax.broadcasted_iota(jnp.int32, (1, 768), 1)
    ext_row = lax.div(lax.rem(ext_row, 48), 2) + lat * 12 - 6
    on_grid = (ext_row >= 0) & (ext_row < 96)
    key_bias[...] = jnp.where(on_grid, key_bias[...], -jnp.inf)
    query_bias[...] = jnp.where(on_grid, query_bias[...], -jnp.inf)
    finish(loads[4:])

    @pl.loop(0, 4)
    def _(t):
        cols = tile(t)
        q[:, cols] = dot(xm[...], w_qkv[:, cols]).astype(BF16)
        d[:, cols] = dot_nt(g[...], w_out[cols, :]).astype(BF16)
        own_kv[:, cols] = dot(xm[...], w_qkv[:, tile(t, 1024)]).astype(BF16)
        own_kv[:, tile(t, 1024)] = dot(xm[...], w_qkv[:, tile(t, 2048)]).astype(BF16)

    finish(rows_moved)
    ext[288:864, :] = dot(to_middle[...], stacked[...]).astype(BF16)
    begin(sides_moved)
    pieces[...] = dot(to_piece[...], g[...]).astype(BF16)

    def project(tiles, target, first_tile, middle):
        @pl.loop(0, tiles)
        def _(t):
            weights = w_qkv[:, tile(t, first_tile * 256)]
            if middle:
                target[288:864, tile(t)] = dot(ext[288:864, :], weights).astype(BF16)
            else:
                sides = jnp.concatenate([ext[0:288, :], ext[864:1152, :]], axis=0)
                sides = dot(sides, weights).astype(BF16)
                target[0:288, tile(t)] = sides[0:288]
                target[864:1152, tile(t)] = sides[288:576]

    project(8, kv, 4, True)
    project(4, ext_q, 0, True)
    finish(sides_moved)
    begin(g_rows_moved)
    project(8, kv, 4, False)

    lane_head = lax.div(lax.broadcasted_iota(jnp.int32, (96, 256), 1), 64)
    picks = [lane_head == h for h in range(4)]
    nothing = jnp.zeros((96, 256), BF16)
    stat_lane = lax.broadcasted_iota(jnp.int32, (96, 128), 1)
    factor = math.log2(math.e) / 8.0

    def apart(block):
        return jnp.concatenate([jnp.where(pick, block, nothing) for pick in picks], axis=0)

    def joined(out):
        whole = jnp.where(picks[0], out[0:96], 0.0)
        for h in range(1, 4):
            whole = jnp.where(picks[h], out[h * 96 : h * 96 + 96], whole)
        return whole

    def queries(t):
        cols, vcols = tile(t), tile(t, 1024)

        for j in range(3):
            rows = pl.ds(j * 96, 96)
            keys = pl.ds(j * 192, 768)
            qm, dm = apart(q[rows, cols]), apart(d[rows, cols])
            kw, vw = kv[keys, cols], kv[keys, vcols]
            s = dot_nt(qm, kw).reshape(4, 96, 768) + key_bias[...][None]
            top = jnp.max(s, axis=-1, keepdims=True)
            e = jnp.exp2((s - top) * factor)
            share = 1.0 / jnp.sum(e, axis=-1, keepdims=True)
            p = (e * share).reshape(384, 768)
            out = dot(p.astype(BF16), vw)
            delta = jnp.sum(out * dm.astype(F32), axis=-1, keepdims=True)
            ctx[rows, cols] = joined(out).astype(BF16)
            ds = (p * (dot_nt(dm, vw) - delta)).astype(BF16)
            dqkv[rows, cols] = (joined(dot(ds, kw)) * 0.125).astype(BF16)
            kept = stats[rows, :]
            for h in range(4):
                values = (top[h], share[h], delta[h * 96 : h * 96 + 96])
                for kind, value in enumerate(values):
                    kept = jnp.where(stat_lane == t * 16 + kind * 4 + h, value, kept)
            stats[rows, :] = kept

    def keys_of(t):
        cols, vcols = tile(t), tile(t, 1024)

        for j in range(3):
            rows = pl.ds(j * 96, 96)
            seen = pl.ds(j * 192, 768)
            km, vm = apart(own_kv[rows, cols]), apart(own_kv[rows, vcols])
            qw, dw = ext_q[seen, cols], kv[seen, cols]
            known = stat_rows[j, 16 * t : 16 * t + 16, :]
            top, share, delta = (known[4 * i : 4 * i + 4].reshape(4, 1, 768) for i in range(3))
            s = dot_nt(km, qw).reshape(4, 96, 768) + query_bias[...][None]
            p = jnp.exp2((s - top) * factor) * share
            ds = p * (dot_nt(vm, dw).reshape(4, 96, 768) - delta)
            dk = joined(dot(ds.reshape(384, 768).astype(BF16), qw)) * 0.125
            dv = joined(dot(p.reshape(384, 768).astype(BF16), dw))
            dqkv[rows, tile(t, 1024)] = dk.astype(BF16)
            dqkv[rows, tile(t, 2048)] = dv.astype(BF16)

    def add_to_total(t):
        dk, dv = dqkv[:, tile(t, 1024)], dqkv[:, tile(t, 2048)]
        for c in range(4):
            rows = slice(256 * c, 256 * c + 256)
            more = dot_nt(dk, w_qkv[rows, tile(t, 1024)]) + dot_nt(dv, w_qkv[rows, tile(t, 2048)])
            total[:, rows] += more

    @pl.loop(0, 4)
    def _(t):
        queries(t)

        @pl.when(t == 2)
        def _():
            finish(g_rows_moved)
            g_ext[288:864, :] = dot(to_middle[...], g_stacked[...]).astype(BF16)
            begin(g_sides_moved)

    stat_pieces[...] = reordered(to_piece[...], stats[...])
    stat_stacked[144:432, :] = stats[...]
    begin(stat_rows_moved)

    mades, gots = (made_a, made_b), (got_a, got_b)

    def columns(job):
        return pl.ds(JOBS[job][1], JOBS[job][2])

    def store_made(made, half, cols, value):
        made[half, :, :, :, :, :, cols] = value.astype(BF16).reshape(4, 2, 2, 4, 16, 256)

    def make_a(half):
        @pl.when(half == 0)
        def _():
            @pl.loop(0, 4)
            def _(t):
                store_made(made_a, half, tile(t), dot(xm_t[...], dqkv[:, tile(t)]))

        @pl.when(half == 1)
        def _():
            @pl.loop(0, 4)
            def _(t):
                store_made(made_a, half, tile(t), dot(ctx_t[...], g[:, tile(t)]))

    def make_b(n, half):
        cols = pl.ds(pl.multiple_of(half * 1024 + 1024 + 256 * n, 256), 256)
        store_made(made_b, half, pl.ds(256 * n, 256), dot(xm_t[...], dqkv[:, cols]))

    def exchange(job):
        where = (EVERY,) * 5 + (columns(job),)
        phase = JOBS[job][0]
        return copy_to(mades[phase].at[(1 - core, *where)], gots[phase].at[where], 12 + job, partner)

    def exchanged(job):
        exchange(job).wait()
        cols, made, got = columns(job), mades[JOBS[job][0]], gots[JOBS[job][0]]

        @pl.loop(0, 4)
        def _(a):
            for b in range(2):
                for c in range(2):
                    both = made[core, a, b, c, :, :, cols].astype(F32)
                    both = both + got[a, b, c, :, :, cols].astype(F32)
                    made[core, a, b, c, :, :, cols] = both.astype(BF16)

        start(job, 0)

    def held(job, stage, at):
        order = JOBS[job][3]
        here = index_of(without(order, stage), order[stage], at)
        if stage == 0:
            return mades[JOBS[job][0]], (core, *here, EVERY, columns(job))
        return scratch[job][2 * stage - 1], (*here, EVERY, EVERY)

    def stage_copies(job, stage):
        axis = JOBS[job][3][stage]
        copies = []
        for by in (2, 1, 3):
            ref, where = held(job, stage, lax.rem(mine[axis] + by, 4))
            target = scratch[job][2 * stage].at[by - 1]
            sem = 12 + len(JOBS) + job * 9 + stage * 3 + by - 1
            copies.append(copy_to(ref.at[where], target, sem, device(axis, by)))
        return copies

    def start(job, stage):
        for copy in stage_copies(job, stage):
            copy.start()

    def reduced(job, stage):
        for copy in stage_copies(job, stage):
            copy.wait()
        ref, where = held(job, stage, mine[JOBS[job][3][stage]])
        piece = ref[where].astype(F32)
        for slot in range(3):
            piece = piece + scratch[job][2 * stage][slot].astype(F32)
        if stage < 2:
            scratch[job][2 * stage + 1][...] = piece.astype(BF16)
            start(job, stage + 1)
        else:
            final = (final_a, final_b)[JOBS[job][0]]
            final[:, columns(job)] = piece * (1.0 / 192.0)

    def swap(phase):
        rows = pl.ds(pl.multiple_of((1 - core) * 8, 8), 8)
        source = (final_a, final_b)[phase].at[rows, pl.ds(0, 1024)]
        return copy_to(source, (cross_a, cross_b)[phase], 12 + 10 * len(JOBS) + phase, partner)

    def group(n):
        make_b(n, 1 - core)
        for job in OF_QUAD[n]:
            exchange(job).start()
        make_b(n, core)

    ctx_t[...] = ctx[...].T
    leaving = (
        pltpu.make_async_copy(block_out, block_out_hbm, load.at[6]),
        pltpu.make_async_copy(grad_tokens, grad_tokens_hbm, load.at[7]),
    )
    make_a(1 - core)
    for job in (0, 1, 2):
        exchange(job).start()

    project(4, ext_q, 0, False)
    finish(stat_rows_moved)
    stat_ext[288:864, :] = reordered(to_middle[...], stat_stacked[...])
    finish(g_sides_moved)
    begin(stat_sides_moved)
    make_a(core)
    for job in (0, 1, 2):
        exchanged(job)

    @pl.loop(0, 4)
    def _(t):
        kv[:, tile(t)] = dot_nt(g_ext[...], w_out[tile(t), :]).astype(BF16)

    finish(stat_sides_moved)
    for j in range(3):
        stat_rows[j] = stat_ext[192 * j : 192 * j + 768, :].T

    def advance(*steps):
        for job, stage in steps:
            reduced(job, stage)

    keys_of(0)
    group(0)
    add_to_total(0)
    exchanged(3)
    keys_of(1)
    advance((0, 0), (1, 0), (2, 0))
    group(1)
    add_to_total(1)
    exchanged(4)
    keys_of(2)
    advance((0, 1), (1, 1), (2, 1), (3, 0))
    group(2)

    @pl.loop(0, 4)
    def _(t):
        cols = tile(t)
        total[:, cols] += dot_nt(dqkv[:, 0:1024], w_qkv[cols, 0:1024])

    add_to_total(2)
    exchanged(5)
    keys_of(3)
    make_b(3, 1 - core)
    for job in OF_QUAD[3]:
        exchange(job).start()
    add_to_total(3)

    @pl.loop(0, 4)
    def _(t):
        cols = tile(t)
        hit = hits[...]
        value = total[:, cols]
        high = value.astype(BF16)
        low = (value - high.astype(F32)).astype(BF16)
        column = dot_tn(high, hit.astype(BF16)) + dot_tn(low, hit.astype(BF16))
        column = column.astype(BF16).reshape(2, 2, 4, 16, 128)
        made_b[0, t, :, :, :, :, 1024:1152] = column
        made_b[1, t, :, :, :, :, 1024:1152] = column

    exchange(8).start()
    make_b(3, core)
    exchanged(6)
    exchanged(7)
    exchanged(8)
    advance((3, 1), (4, 0), (5, 0), (0, 2), (1, 2), (2, 2))
    swap(0).start()

    @pl.loop(0, 4)
    def _(t):
        cols = tile(t)
        hit = hits[...]
        value = total[:, cols]
        kept = jnp.where(jnp.concatenate([hit, hit], axis=1) > 0.5, 0.0, value).astype(BF16)
        kept = dot(to_given[...], kept).astype(BF16)
        grad_tokens[:, :, :, cols] = kept.reshape(12, 12, 2, 256)

    leaving[1].start()
    advance((6, 0), (7, 0), (8, 0))

    @pl.loop(0, 4)
    def _(t):
        cols = tile(t)
        value = xm[:, cols].astype(F32) + dot(ctx[...], w_out[:, cols])
        value = dot(to_given[...], value.astype(BF16)).astype(BF16)
        block_out[:, :, :, cols] = value.reshape(12, 12, 2, 256)

    leaving[0].start()
    advance((4, 1), (5, 1), (3, 2), (6, 1), (7, 1), (8, 1))
    advance((4, 2), (5, 2), (6, 2), (7, 2), (8, 2))
    swap(1).start()
    finish(leaving)
    swap(0).wait()
    swap(1).wait()
    rows = pl.ds(pl.multiple_of(core * 8, 8), 8)
    gm[...] = final_b[rows, 1024:]

    @pl.when(core == 0)
    def _():
        gq[:, 0:1024] = final_a[rows, :]
        gq[:, 1024:2048] = final_b[rows, 0:1024]
        gq[:, 2048:] = cross_b[...]
        go[...] = cross_a[...]

    @pl.when(core == 1)
    def _():
        gq[:, 0:1024] = cross_a[...]
        gq[:, 1024:2048] = cross_b[...]
        gq[:, 2048:] = final_b[rows, 0:1024]
        go[...] = final_a[rows, :]


def hand_out_kernel(block_out, grad_tokens, gq, go, gm, *targets):
    for source, target in zip((block_out, grad_tokens, gq, go), targets):
        target[...] = source[...]
    row = lax.broadcasted_iota(jnp.int32, (8, 128), 0)
    lane = lax.broadcasted_iota(jnp.int32, (8, 128), 1)
    targets[4][...] = jnp.sum(jnp.where(row == lane, gm[...], 0.0), axis=0)[0:8]


def local(tokens, masked, mask_embed, w_qkv, w_out, cotangent):
    given = one_hot(given_order(), 288)
    piece, middle = one_hot(piece_order(), 288), one_hot(middle_order(), 576)
    orders = [given, given.T, piece, middle]
    vmem, hbm = pl.BlockSpec(memory_space=pltpu.VMEM), pl.BlockSpec(memory_space=pl.ANY)
    jobs = []
    for _, _, wide, order in JOBS:
        for stage in (1, 2):
            left = extent(without(order, stage))
            jobs.append(pltpu.VMEM((3, *left, 16, wide), BF16))
            jobs.append(pltpu.VMEM((*left, 16, wide), BF16))
        jobs.append(pltpu.VMEM((3, 16, wide), BF16))
    block_out, grad_tokens, gq, go, gm = pl.pallas_call(
        block_kernel,
        out_shape=(
            jax.ShapeDtypeStruct((12, 12, 2, 1024), BF16),
            jax.ShapeDtypeStruct((12, 12, 2, 1024), BF16),
            jax.ShapeDtypeStruct((8, 3072), F32),
            jax.ShapeDtypeStruct((8, 1024), F32),
            jax.ShapeDtypeStruct((8, 128), F32),
        ),
        in_specs=[vmem] * 3 + [hbm] * 5 + [vmem] * 3 + [hbm],
        out_specs=(hbm, hbm, vmem, vmem, vmem),
        scratch_shapes=[
            pltpu.VMEM((12, 12, 2, 1024), BF16),
            pltpu.VMEM((12, 12, 2, 1024), BF16),
            pltpu.VMEM((1024, 3072), BF16),
            pltpu.VMEM((1024, 1024), BF16),
            pltpu.VMEM((12, 12, 2, 1024), BF16),
            pltpu.VMEM((96, 768), F32),
            pltpu.VMEM((96, 768), F32),
            pltpu.VMEM((576, 576), BF16),
            pltpu.VMEM((288, 1024), BF16),
            pltpu.VMEM((288, 1024), BF16),
            pltpu.VMEM((288, 128), F32),
            pltpu.VMEM((288, 1024), BF16),
            pltpu.VMEM((288, 3072), BF16),
            pltpu.VMEM((288, 1024), BF16),
            pltpu.VMEM((576, 1024), BF16),
            pltpu.VMEM((1152, 1024), BF16),
            pltpu.VMEM((576, 1024), BF16),
            pltpu.VMEM((1152, 1024), BF16),
            pltpu.VMEM((288, 128), F32),
            pltpu.VMEM((288, 128), F32),
            pltpu.VMEM((576, 128), F32),
            pltpu.VMEM((1152, 128), F32),
            pltpu.VMEM((3, 128, 768), F32),
            pltpu.VMEM((288, 1024), BF16),
            pltpu.VMEM((288, 1024), BF16),
            pltpu.VMEM((1152, 2048), BF16),
            pltpu.VMEM((288, 2048), BF16),
            pltpu.VMEM((1152, 1024), BF16),
            pltpu.VMEM((288, 1024), F32),
            pltpu.VMEM((1024, 288), BF16),
            pltpu.VMEM((1024, 288), BF16),
            pltpu.VMEM((2, 4, 2, 2, 4, 16, 1024), BF16),
            pltpu.VMEM((2, 4, 2, 2, 4, 16, 1152), BF16),
            pltpu.VMEM((4, 2, 2, 4, 16, 1024), BF16),
            pltpu.VMEM((4, 2, 2, 4, 16, 1152), BF16),
            *jobs,
            pltpu.VMEM((16, 1024), F32),
            pltpu.VMEM((16, 1152), F32),
            pltpu.VMEM((8, 1024), F32),
            pltpu.VMEM((8, 1024), F32),
            pltpu.SemaphoreType.DMA((8,)),
            pltpu.SemaphoreType.DMA((14 + 10 * len(JOBS),)),
            pltpu.SemaphoreType.DMA((14 + 10 * len(JOBS),)),
        ],
        compiler_params=pltpu.CompilerParams(
            collective_id=1, has_side_effects=True, vmem_limit_bytes=63 * 1024 * 1024
        ),
        name="attention_block",
    )(
        tokens.transpose(1, 2, 0, 3), masked, mask_embed.reshape(8, 128), w_qkv, w_out,
        cotangent.transpose(1, 2, 0, 3), jnp.asarray(near(0)), jnp.asarray(near(1)),
        *[jnp.asarray(order, BF16) for order in orders],
    )
    block_out, grad_tokens, gq, go, gm = pl.pallas_call(
        hand_out_kernel,
        out_shape=(
            jax.ShapeDtypeStruct((12, 12, 2, 1024), BF16),
            jax.ShapeDtypeStruct((12, 12, 2, 1024), BF16),
            jax.ShapeDtypeStruct((8, 3072), F32),
            jax.ShapeDtypeStruct((8, 1024), F32),
            jax.ShapeDtypeStruct((8,), F32),
        ),
        in_specs=[vmem] * 5,
        out_specs=(vmem,) * 5,
        name="hand_out",
    )(block_out, grad_tokens, gq, go, gm)
    block_out, grad_tokens = block_out.transpose(2, 0, 1, 3), grad_tokens.transpose(2, 0, 1, 3)
    return (block_out, grad_tokens, gq, go, gm)


def solution(mesh):
    placed = (
        P(None, "lat", "lon", None),
        P("lat", "lon", None),
        P(),
        P(),
        P(),
        P(None, "lat", "lon", None),
    )
    return jax.shard_map(
        local,
        mesh=mesh,
        in_specs=placed,
        out_specs=(
            P(None, "lat", "lon", None),
            P(None, "lat", "lon", None),
            P(("lat", "lon"), None),
            P(("lat", "lon"), None),
            P(("lat", "lon")),
        ),
        check_vma=False,
    )
```
